32 devices in a mesh: dp: 2 (over y), fsdp: 16 (over z, x, core).
Axes of the slice: x: 2, y: 2, z: 4, core: 2. Of those that a mesh axis runs over, the one named last changes fastest.
Arguments:
- content_in: bfloat16 [96, 512, 768], P(('dp', 'fsdp')), may hold values from -6 to 6
- query_in: bfloat16 [96, 77, 768], P(('dp', 'fsdp')), may hold values from -6 to 6
- permutation: int32 [96, 512], P(('dp', 'fsdp')), may hold values from 0 to 511, each once within a row
- query_weight: bfloat16 [768, 768], P('fsdp'), may hold values from -0.21875 to 0.21875
- key_weight: bfloat16 [768, 768], P('fsdp'), may hold values from -0.21875 to 0.21875
- value_weight: bfloat16 [768, 768], P('fsdp'), may hold values from -0.21875 to 0.21875
- output_weight: bfloat16 [768, 768], P('fsdp'), may hold values from -2 to 2
- inner_weight: bfloat16 [768, 3072], P('fsdp'), may hold values from -0.21875 to 0.21875
- outer_weight: bfloat16 [3072, 768], P('fsdp'), may hold values from -0.109375 to 0.109375
- query_bias: bfloat16 [768], P('fsdp'), may hold values from -3 to 3
- value_bias: bfloat16 [768], P('fsdp'), may hold values from -3 to 3
- output_bias: bfloat16 [768], P('fsdp'), may hold values from -3 to 3
- first_gain: bfloat16 [768], P('fsdp'), may hold values from 0.099609375 to 1.8984375
- first_shift: bfloat16 [768], P('fsdp'), may hold values from -3 to 3
- inner_bias: bfloat16 [3072], P('fsdp'), may hold values from -3 to 3
- outer_bias: bfloat16 [768], P('fsdp'), may hold values from -3 to 3
- second_gain: bfloat16 [768], P('fsdp'), may hold values from 0.099609375 to 1.8984375
- second_shift: bfloat16 [768], P('fsdp'), may hold values from -3 to 3
- bias_table: bfloat16 [384], P('fsdp'), may hold values from -4 to 4
- content_cotangent: bfloat16 [96, 512, 768], P(('dp', 'fsdp')), may hold values from -6 to 6
- query_cotangent: bfloat16 [96, 77, 768], P(('dp', 'fsdp')), may hold values from -6 to 6
Outputs:
- content_out: bfloat16 [96, 512, 768], P(('dp', 'fsdp'))
- query_out: bfloat16 [96, 77, 768], P(('dp', 'fsdp'))
- content_grad: float32 [96, 512, 768], P(('dp', 'fsdp'))
- query_grad: float32 [96, 77, 768], P(('dp', 'fsdp'))
- query_weight_grad: float32 [768, 768], P('fsdp')
- key_weight_grad: float32 [768, 768], P('fsdp')
- value_weight_grad: float32 [768, 768], P('fsdp')
- output_weight_grad: float32 [768, 768], P('fsdp')
- inner_weight_grad: float32 [768, 3072], P('fsdp')
- outer_weight_grad: float32 [3072, 768], P('fsdp')
- query_bias_grad: float32 [768], P('fsdp')
- value_bias_grad: float32 [768], P('fsdp')
- output_bias_grad: float32 [768], P('fsdp')
- first_gain_grad: float32 [768], P('fsdp')
- first_shift_grad: float32 [768], P('fsdp')
- inner_bias_grad: float32 [3072], P('fsdp')
- outer_bias_grad: float32 [768], P('fsdp')
- second_gain_grad: float32 [768], P('fsdp')
- second_shift_grad: float32 [768], P('fsdp')
- bias_table_grad: float32 [384], P('fsdp')
The draws below stay inside these ranges and needn't reach their ends.
All inputs are finite; a program needn't handle non-finite values.
Results may differ from the reference program's by a relative error of at most 0.015.
Values may be sent and summed in bfloat16 or wider, within the bound.
A program may use at most 256 MiB of HBM per device.

```python
import jax
import jax.numpy as jnp
from jax import lax

D = 768
HEADS = 12
HEAD = 64
FF = 3072
BUCKETS = 32
LEN = 512
PRED = 77
SEQS = 96


def strengthened(array, own_key, source, target, parts, factor):
    def block_of(position):
        return (jnp.arange(array.shape[position]) // (array.shape[position] // parts)).reshape((-1,) + (1,) * (array.ndim - 1 - position))

    one_side = jax.random.permutation(own_key, parts)[block_of(target)]
    other_side = (block_of(target) + parts // 2) % parts
    return jnp.where((block_of(source) == one_side) | (block_of(source) == other_side), factor * array, array)


def block_scale(stream_key, dims, split, least, largest):
    level = 1.0
    for dim, parts in split:
        draws = jax.random.uniform(jax.random.fold_in(jax.random.fold_in(stream_key, 6), dim), (parts,), jnp.float32, least / len(split), largest / len(split))
        level = level * jnp.repeat(jnp.exp(draws), dims[dim] // parts).reshape((-1,) + (1,) * (len(dims) - 1 - dim))
    return level


def bell_draw(own_key, shape, deviation, bound, cuts=(), held_as=jnp.bfloat16):
    entries = jax.random.normal(own_key, shape, jnp.float32) * deviation
    if len(cuts) > 0:
        entries = block_scale(own_key, shape, cuts, -0.22, 0.18) * entries
    return jnp.clip(entries, min=-bound, max=bound).astype(held_as)


def noise_with(rng, shape, deviation, bound, split, heavy, held_as=jnp.bfloat16):
    values = deviation * jax.random.normal(rng, shape, jnp.float32)
    if split:
        values = values * block_scale(rng, shape, split, -0.22, 0.18)
    return jnp.clip(strengthened(values, jax.random.fold_in(rng, 3), *heavy), -bound, bound).astype(held_as)


def setup_inputs(seed: int = 0) -> dict:
    key_list = jax.random.split(jax.random.key(seed), 22)
    content_in = bell_draw(key_list[0], (SEQS, LEN, D), 1.0, 6.0, ((0, 32),))
    query_in = bell_draw(key_list[1], (SEQS, PRED, D), 1.0, 6.0, ((0, 32),))
    permutation = jax.vmap(lambda own: jax.random.permutation(own, LEN))(jax.random.split(key_list[2], SEQS)).reshape((SEQS, LEN)).astype(jnp.int32)
    query_weight = bell_draw(key_list[3], (D, D), D ** -0.5, 0.21875, ((0, 16),))
    key_weight = bell_draw(key_list[4], (D, D), D ** -0.5, 0.21875, ((0, 16),))
    value_weight = bell_draw(key_list[5], (D, D), D ** -0.5, 0.21875, ((0, 16),))
    output_weight = bell_draw(key_list[6], (D, D), (D // 96) ** -0.5, 2.0, ((0, 16),))
    inner_weight = bell_draw(key_list[7], (D, FF), D ** -0.5, 0.21875, ((0, 16),))
    outer_weight = bell_draw(key_list[8], (FF, D), FF ** -0.5, 0.109375, ((0, 16),))
    query_bias = bell_draw(key_list[9], (D,), 0.5, 3.0, ((0, 16),))
    value_bias = bell_draw(key_list[10], (D,), 0.5, 3.0, ((0, 16),))
    output_bias = bell_draw(key_list[11], (D,), 0.5, 3.0, ((0, 16),))
    first_gain = jnp.clip(1.0 + 0.18 * jax.random.normal(key_list[12], (D,), jnp.float32), 0.099609375, 1.8984375).astype(jnp.bfloat16)
    first_shift = bell_draw(key_list[13], (D,), 0.5, 3.0, ((0, 16),))
    inner_bias = bell_draw(key_list[14], (FF,), 0.5, 3.0, ((0, 16),))
    outer_bias = bell_draw(key_list[15], (D,), 0.5, 3.0, ((0, 16),))
    second_gain = jnp.clip(1.0 + 0.18 * jax.random.normal(key_list[16], (D,), jnp.float32), 0.099609375, 1.8984375).astype(jnp.bfloat16)
    second_shift = bell_draw(key_list[17], (D,), 0.5, 3.0, ((0, 16),))
    bias_table = bell_draw(key_list[18], (BUCKETS * HEADS,), 1.0, 4.0, ((0, 16),))
    content_cotangent = noise_with(key_list[19], (SEQS, LEN, D), 1.0, 6.0, ((0, 32),), (0, 2, 32, 2.75))
    query_cotangent = noise_with(key_list[20], (SEQS, PRED, D), 1.0, 6.0, ((0, 32),), (0, 2, 32, 2.75))
    return {"content_in": content_in, "query_in": query_in, "permutation": permutation, "query_weight": query_weight, "key_weight": key_weight, "value_weight": value_weight, "output_weight": output_weight, "inner_weight": inner_weight, "outer_weight": outer_weight, "query_bias": query_bias, "value_bias": value_bias, "output_bias": output_bias, "first_gain": first_gain, "first_shift": first_shift, "inner_bias": inner_bias, "outer_bias": outer_bias, "second_gain": second_gain, "second_shift": second_shift, "bias_table": bias_table, "content_cotangent": content_cotangent, "query_cotangent": query_cotangent}


@jax.custom_vjp
def low(v):
    return lax.optimization_barrier(v.astype(jnp.bfloat16)).astype(jnp.float32)

@jax.custom_vjp
def low_back(v):
    return v

def low_keep(v):
    return (low(v), None)

def low_pass(kept, grad):
    return (grad,)

def back_keep(v):
    return (v, None)

def back_low(kept, grad):
    return (low(grad),)
low.defvjp(low_keep, low_pass)
low_back.defvjp(back_keep, back_low)
highest = lax.Precision.HIGHEST
eps_norm = 1e-05
inverse_root = 0.7071067811865476
bucket_edges = (12, 16, 23, 32, 46, 64, 91)

def bucket_index(relative):
    distance = jnp.abs(relative)
    coarse = 8 + sum(((distance >= boundary).astype(jnp.int32) for boundary in bucket_edges))
    within = jnp.where(distance < 8, distance, coarse)
    return within + 16 * (relative > 0).astype(jnp.int32)

def layout(order_row):
    length = order_row.shape[0]
    ranking = jnp.zeros((length,), jnp.int32).at[order_row].set(jnp.arange(length, dtype=jnp.int32))
    positions = jnp.concatenate([jnp.arange(length, dtype=jnp.int32), order_row[length - PRED:]])
    limits = jnp.concatenate([jnp.maximum(ranking, length - PRED - 1), jnp.arange(PRED, dtype=jnp.int32) + (length - PRED - 1)])
    visible = ranking[None, :] <= limits[:, None]
    buckets = bucket_index(jnp.arange(length, dtype=jnp.int32)[None, :] - positions[:, None])
    return (visible, buckets)

def norm_rows(values, gain_row, shift_row):
    centered = values - lax.optimization_barrier(jnp.mean(values, axis=-1, keepdims=True))
    variance = lax.optimization_barrier(jnp.mean(centered * centered, axis=-1, keepdims=True))
    return centered * lax.rsqrt(variance + eps_norm) * gain_row + shift_row

def matmul(left, right):
    return jnp.dot(left, right, precision=highest)

def forward(content, query, weight_set, visible, buckets):
    query_weight, key_weight, value_weight, output_weight, inner_weight, outer_weight, query_bias, value_bias, output_bias, first_gain, first_shift, inner_bias, outer_bias, second_gain, second_shift, bias_table = weight_set
    stacked = jnp.concatenate([content, query], axis=0)
    row_count = stacked.shape[0]
    queries = low_back(low(matmul(stacked, query_weight) + query_bias)).reshape(row_count, HEADS, HEAD)
    keys_all = low_back(low(matmul(content, key_weight))).reshape(LEN, HEADS, HEAD)
    values_all = low_back(low(matmul(content, value_weight) + value_bias)).reshape(LEN, HEADS, HEAD)
    bucket_table = bias_table.reshape(BUCKETS, HEADS)
    biases = jnp.transpose(bucket_table[buckets], (2, 0, 1))
    products = jnp.einsum('qhe,khe->hqk', queries, keys_all, precision=highest)
    scores = low_back(products * HEAD ** (-0.5) + biases)
    scores = jnp.where(visible[None], scores, -1000000000.0)
    row_peak = lax.optimization_barrier(jnp.max(scores, axis=-1, keepdims=True))
    exponent = jnp.exp(scores - row_peak)
    attention = low(exponent / lax.optimization_barrier(jnp.sum(exponent, axis=-1, keepdims=True)))
    mixture = jnp.einsum('hqk,khe->qhe', attention, values_all, precision=highest)
    mixture = low_back(low(mixture)).reshape(row_count, D)
    branch = low_back(matmul(mixture, output_weight) + output_bias)
    normed_one = norm_rows(stacked + branch, first_gain, first_shift)
    hidden_pre = low_back(matmul(low(normed_one), inner_weight) + inner_bias)
    activated = low(0.5 * hidden_pre * (1.0 + lax.erf(hidden_pre * inverse_root)))
    branch_two = low_back(matmul(activated, outer_weight) + outer_bias)
    result = norm_rows(normed_one + branch_two, second_gain, second_shift)
    return (result[:LEN], result[LEN:])

def reference(content_in, query_in, permutation, query_weight, key_weight, value_weight, output_weight, inner_weight, outer_weight, query_bias, value_bias, output_bias, first_gain, first_shift, inner_bias, outer_bias, second_gain, second_shift, bias_table, content_cotangent, query_cotangent):
    weight_set = tuple((weight_arg.astype(jnp.float32) for weight_arg in (query_weight, key_weight, value_weight, output_weight, inner_weight, outer_weight, query_bias, value_bias, output_bias, first_gain, first_shift, inner_bias, outer_bias, second_gain, second_shift, bias_table)))

    def per_sequence(totals, inputs):
        content, query, order_row, content_cot, query_cot = inputs
        visible, buckets = layout(order_row)

        def local_forward(content_value, query_value, weight_values):
            return forward(content_value, query_value, weight_values, visible, buckets)
        outputs, pullback = jax.vjp(local_forward, content.astype(jnp.float32), query.astype(jnp.float32), weight_set)
        content_back, query_back, weight_back = pullback((content_cot.astype(jnp.float32), query_cot.astype(jnp.float32)))
        totals = jax.tree.map(lambda total_part, new_part: total_part + new_part, totals, weight_back)
        return (totals, (outputs[0].astype(jnp.bfloat16), outputs[1].astype(jnp.bfloat16), content_back, query_back))
    zeros = jax.tree.map(jnp.zeros_like, weight_set)
    totals, (content_out, query_out, content_grad, query_grad) = lax.scan(per_sequence, zeros, (content_in, query_in, permutation, content_cotangent, query_cotangent))
    return (content_out, query_out, content_grad, query_grad) + tuple(totals)
```

```python
import functools

import jax
import jax.numpy as jnp
from jax import lax
from jax.experimental import pallas as pl
from jax.experimental.pallas import tpu as pltpu
from jax.sharding import PartitionSpec as P

D = 768
HEADS = 12
HEAD = 64
BUCKETS = 32
LEN = 512
PRED = 77
QP = 80
R = LEN + QP
f32 = jnp.float32
bf16 = jnp.bfloat16
NT = (((1,), (1,)), ((), ()))

eps_norm = 1e-05
inverse_root = 0.7071067811865476
density_scale = 0.3989422804014327
bucket_edges = (12, 16, 23, 32, 46, 64, 91)
VMEM_LIMIT = 60 * 1024 * 1024


def bucket_index(relative):
    distance = jnp.abs(relative)
    coarse = 8 + sum(((distance >= boundary).astype(jnp.int32) for boundary in bucket_edges))
    within = jnp.where(distance < 8, distance, coarse)
    return within + 16 * (relative > 0).astype(jnp.int32)


def iota(shape, dim):
    return lax.broadcasted_iota(jnp.int32, shape, dim)


def ranking_column(perm_row):
    hit = perm_row == iota((LEN, LEN), 0)
    return jnp.sum(jnp.where(hit, iota((LEN, LEN), 1), 0).astype(f32), axis=1, keepdims=True)


def build_bias(table, full, near, far):
    rel = iota((128, 1024), 1) - 512
    onehot = (bucket_index(rel) == iota((128, 1024), 0)).astype(bf16)
    by_rel = jnp.dot(table, onehot, preferred_element_type=f32)
    for h in range(HEADS):
        far[h, 0:8] = jnp.broadcast_to(by_rel[h : h + 1, 0:1], (8, 128))
        far[h, 8:16] = jnp.broadcast_to(by_rel[h : h + 1, 1023:1024], (8, 128))
        for d in range(-3, 4):
            if abs(d) >= 2:
                at = 512 + 128 * d
                block = jnp.broadcast_to(by_rel[h : h + 1, at : at + 1], (128, 128)).astype(bf16)
            else:
                base = 512 + 128 * d - 128
                row = jnp.broadcast_to(by_rel[h : h + 1, base : base + 256], (128, 256))
                tile = pltpu.roll(row, 0, 1, stride=1, stride_axis=0)[:, 128:]
                near[h, d + 1] = tile
                block = tile.astype(bf16)
            for bi in range(4):
                bj = bi + d
                if 0 <= bj < 4:
                    full[h, bi * 128 : (bi + 1) * 128, bj * 128 : (bj + 1) * 128] = block


def attn_fwd(
    perm_ref, x_ref, wq, wk, wv, bq, bv, tab_ref,
    q_ref, k_ref, v_ref, o_ref, ol_ref, r_ref, p_ref,
    full, near, far, scores, row_mark, key_mark, slot_hot,
):
    s = pl.program_id(0)
    hp = pl.program_id(1)

    @pl.when((s == 0) & (hp == 0))
    def _():
        build_bias(tab_ref[...], full, near, far)

    @pl.when(hp == 0)
    def _():
        x = x_ref[0]
        q = (jnp.dot(x, wq[...], preferred_element_type=f32) + bq[...]).astype(bf16)
        q_ref[0] = q * jnp.asarray(0.125, bf16)
        xc = x[:LEN]
        k_ref[0] = jnp.dot(xc, wk[...], preferred_element_type=f32).astype(bf16)
        v_ref[0] = (jnp.dot(xc, wv[...], preferred_element_type=f32) + bv[...]).astype(bf16)
        rank = ranking_column(perm_ref[0])
        rank_row = jnp.transpose(jnp.broadcast_to(rank, (LEN, 128)))[:1]
        slot = iota((LEN, 128), 1).astype(f32) + float(LEN - PRED)
        limit = jnp.maximum(rank, float(LEN - PRED - 1))
        row_mark[:LEN] = jnp.where(limit < slot, 1.0, 0.0).astype(bf16)
        row_mark[LEN:] = jnp.where(iota((QP, 128), 0) <= iota((QP, 128), 1), 1.0, 0.0).astype(bf16)
        key_mark[...] = jnp.where(rank == slot, -1e9, 0.0).astype(bf16)
        wanted = (iota((QP, LEN), 0) + (LEN - PRED)).astype(f32)
        slot_hot[...] = (rank_row == wanted).astype(bf16)

    cols = pl.ds(pl.multiple_of(hp * 128, 128), 128)
    q2 = q_ref[0, :, cols]
    k2 = k_ref[0, :, cols]
    v2 = v_ref[0, :, cols]
    half = iota((LEN, 128), 1) // 64
    left = jnp.concatenate([q2, row_mark[...]], axis=1)
    for h in range(2):
        right = jnp.concatenate([jnp.where(half == h, k2, jnp.zeros_like(k2)), key_mark[...]], axis=1)
        scores[h, :LEN] = lax.dot_general(left[:LEN], right, NT, preferred_element_type=f32)
        scores[h, LEN:] = lax.dot_general(left[LEN:], right, NT, preferred_element_type=f32) + jnp.dot(
            slot_hot[...], full[2 * hp + h], preferred_element_type=f32
        )
    for h in range(2):
        head = 2 * hp + h
        for bi in range(4):
            rows = slice(bi * 128, bi * 128 + 128)
            tiles = []
            for bj in range(4):
                d = bj - bi
                bias = near[head, d + 1] if abs(d) < 2 else far[head, 8:9] if d > 0 else far[head, 0:1]
                tiles.append(scores[h, rows, bj * 128 : (bj + 1) * 128] + bias)
            biased = jnp.concatenate(tiles, axis=1)
            peak = jnp.max(biased, axis=1, keepdims=True)
            p_ref[0, h, rows] = jnp.exp(biased - peak).astype(bf16)
        biased = scores[h, LEN:]
        peak = jnp.max(biased, axis=1, keepdims=True)
        p_ref[0, h, LEN:] = jnp.exp(biased - peak).astype(bf16)
    mixed = []
    for h in range(2):
        vm = jnp.where(half == h, v2, jnp.ones_like(v2))
        mixed.append(jnp.dot(p_ref[0, h], vm, preferred_element_type=f32))
    low = iota((R, 128), 1) < 64
    inverse = 1.0 / pltpu.roll(jnp.where(low, mixed[1], mixed[0]), 64, 1)
    out = jnp.where(low, mixed[0], mixed[1]) * inverse
    out_low = out.astype(bf16)
    o_ref[0, :, cols] = out_low
    ol_ref[0, :, cols] = (out - out_low.astype(f32)).astype(bf16)
    r_ref[0, :, cols] = inverse


def whole_rows(n):
    return pl.BlockSpec((1, n, D), lambda s, h: (s, 0, 0))


def fixed(shape):
    return pl.BlockSpec(shape, lambda s, h: (0,) * len(shape))


def attention_forward(perm, x, wq, wk, wv, bq, bv, table):
    n = x.shape[0]
    sds = jax.ShapeDtypeStruct
    return pl.pallas_call(
        attn_fwd,
        grid=(n, HEADS // 2),
        in_specs=[pl.BlockSpec((1, 1, LEN), lambda s, h: (s, 0, 0)), whole_rows(R)]
        + [fixed((D, D))] * 3
        + [fixed((1, D))] * 2
        + [fixed((16, 128))],
        out_specs=[
            whole_rows(R), whole_rows(LEN), whole_rows(LEN), whole_rows(R), whole_rows(R), whole_rows(R),
            pl.BlockSpec((1, 2, R, LEN), lambda s, h: (s, h, 0, 0)),
        ],
        out_shape=[
            sds((n, R, D), bf16), sds((n, LEN, D), bf16), sds((n, LEN, D), bf16), sds((n, R, D), bf16),
            sds((n, R, D), bf16), sds((n, R, D), f32), sds((n, HEADS, R, LEN), bf16),
        ],
        scratch_shapes=[
            pltpu.VMEM((HEADS, LEN, LEN), bf16),
            pltpu.VMEM((HEADS, 3, 128, 128), f32),
            pltpu.VMEM((HEADS, 16, 128), f32),
            pltpu.VMEM((2, R, LEN), f32),
            pltpu.VMEM((R, 128), bf16),
            pltpu.VMEM((LEN, 128), bf16),
            pltpu.VMEM((QP, LEN), bf16),
        ],
        compiler_params=pltpu.CompilerParams(vmem_limit_bytes=VMEM_LIMIT),
        name="attention_forward",
    )(perm[:, None], x, wq, wk, wv, bq, bv, table)


def reduce_table(n, slot_cols, kept, near_sum, far_sum):
    c = iota((896, 128), 0)
    rel = jnp.where(c < 768, 128 * (c // 256 - 1) + c % 256 - 128, jnp.where(c % 128 < 64, -200, 200))
    onehot = (bucket_index(rel) == iota((896, 128), 1)).astype(f32)
    slots = jnp.concatenate([slot_cols[i] for i in range(n)], axis=1)
    sub = iota((8, 256), 0)
    lane8 = iota((8, 128), 1)
    lane1 = iota((1, 128), 1)
    rows = []
    for head in range(HEADS):
        moved = jnp.dot(slots, kept[head], preferred_element_type=f32)
        near = [near_sum[head, d] for d in range(3)]
        far = [far_sum[head, 0:8], far_sum[head, 8:16]]
        for bi in range(4):
            for bj in range(4):
                d = bj - bi
                tile = moved[bi * 128 : (bi + 1) * 128, bj * 128 : (bj + 1) * 128]
                if abs(d) < 2:
                    near[d + 1] = near[d + 1] + tile
                else:
                    far[int(d > 0)] = far[int(d > 0)] + tile.reshape(16, 8, 128).sum(0)
        parts = []
        for d in range(3):
            high = low = None
            for a in range(16):
                x = near[d][8 * a : 8 * a + 8]
                if a:
                    x = pltpu.roll(x, 128 - 8 * a, 1)
                keep = lane8 < 128 - 8 * a
                u = jnp.where(keep, x, 0.0)
                w = jnp.where(keep, 0.0, x)
                high = u if high is None else high + u
                low = w if low is None else low + w
            y = jnp.concatenate([low, high], axis=1)
            for k in (1, 2, 4):
                y = jnp.where((sub & k) != 0, pltpu.roll(y, 256 - k, 1), y)
            parts.append(jnp.sum(y, axis=0, keepdims=True))
        parts.append(jnp.where(lane1 == 0, jnp.sum(far[0]), jnp.where(lane1 == 64, jnp.sum(far[1]), 0.0)))
        rows.append(jnp.concatenate(parts, axis=1))
    rows.append(jnp.zeros((4, 896), f32))
    return jnp.dot(
        jnp.concatenate(rows, axis=0), onehot, preferred_element_type=f32, precision=lax.Precision.HIGHEST
    )


def attn_bwd(
    perm_ref, q_ref, k_ref, v_ref, o_ref, ol_ref, r_ref, p_ref, do_ref,
    dq_ref, dk_ref, dv_ref, tab_ref,
    dp, ds, kept, slot_cols, near_sum, far_sum,
):
    n = slot_cols.shape[0]
    s = pl.program_id(0)
    hp = pl.program_id(1)

    @pl.when((s == 0) & (hp == 0))
    def _():
        near_sum[...] = jnp.zeros_like(near_sum)
        far_sum[...] = jnp.zeros_like(far_sum)

    @pl.when(hp == 0)
    def _():
        rank = ranking_column(perm_ref[0])
        slot_cols[s] = (rank == (iota((LEN, QP), 1) + (LEN - PRED)).astype(f32)).astype(bf16)

    cols = pl.ds(pl.multiple_of(hp * 128, 128), 128)
    q2 = q_ref[0, :, cols]
    k2 = k_ref[0, :, cols]
    v2 = v_ref[0, :, cols]
    delta = (do_ref[0, :, cols].astype(f32) * r_ref[0, :, cols]).astype(bf16)
    prod = delta.astype(f32) * (o_ref[0, :, cols].astype(f32) + ol_ref[0, :, cols].astype(f32))
    high = prod.astype(bf16)
    rest = pltpu.roll(prod - high.astype(f32), 64, 1).astype(bf16)
    low = iota((R, 128), 1) < 64
    half = iota((LEN, 128), 1) // 64
    extra = [jnp.where(low, high, rest), jnp.where(low, rest, high)]
    minus = jnp.full((LEN, 128), -1.0, bf16)
    for h in range(2):
        vm = jnp.where(half == h, v2, jnp.zeros_like(v2))
        dp[h] = lax.dot_general(
            jnp.concatenate([delta, extra[h]], axis=1),
            jnp.concatenate([vm, minus], axis=1),
            NT,
            preferred_element_type=f32,
        )
    for h in range(2):
        head = 2 * hp + h
        far = [None, None]
        for bi in range(4):
            rows = slice(bi * 128, bi * 128 + 128)
            d_rows = p_ref[0, h, rows].astype(f32) * dp[h, rows]
            ds[h, rows] = d_rows.astype(bf16)
            for bj in range(4):
                d = bj - bi
                tile = d_rows[:, bj * 128 : (bj + 1) * 128]
                if abs(d) < 2:
                    near_sum[head, d + 1] += tile
                else:
                    part = tile.reshape(16, 8, 128).sum(0)
                    far[int(d > 0)] = part if far[int(d > 0)] is None else far[int(d > 0)] + part
        far_sum[head, 0:8] += far[0]
        far_sum[head, 8:16] += far[1]
        d_slots = (p_ref[0, h, LEN:].astype(f32) * dp[h, LEN:]).astype(bf16)
        ds[h, LEN:] = d_slots
        kept[head, pl.ds(pl.multiple_of(s * QP, 16), QP)] = d_slots
    dq = None
    for h in range(2):
        km = jnp.where(half == h, k2, jnp.zeros_like(k2))
        part = jnp.dot(ds[h], km, preferred_element_type=f32)
        dq = part if dq is None else dq + part
    dq_ref[0, :, cols] = (dq * 0.125).astype(bf16)
    q_t = jnp.transpose(q2)
    delta_t = jnp.transpose(delta)
    dk_t = [jnp.dot(q_t[h * 64 : (h + 1) * 64], ds[h], preferred_element_type=f32) for h in range(2)]
    dv_t = [jnp.dot(delta_t[h * 64 : (h + 1) * 64], p_ref[0, h], preferred_element_type=f32) for h in range(2)]
    dk_ref[0, :, cols] = jnp.transpose(jnp.concatenate(dk_t, axis=0).astype(bf16))
    dv_ref[0, :, cols] = jnp.transpose(jnp.concatenate(dv_t, axis=0).astype(bf16))

    @pl.when((s == n - 1) & (hp == HEADS // 2 - 1))
    def _():
        tab_ref[...] = reduce_table(n, slot_cols, kept, near_sum, far_sum)


def attention_backward(perm, q, k, v, o, ol, r, p, do):
    n = q.shape[0]
    sds = jax.ShapeDtypeStruct
    return pl.pallas_call(
        attn_bwd,
        grid=(n, HEADS // 2),
        in_specs=[
            pl.BlockSpec((1, 1, LEN), lambda s, h: (s, 0, 0)),
            whole_rows(R), whole_rows(LEN), whole_rows(LEN), whole_rows(R), whole_rows(R), whole_rows(R),
            pl.BlockSpec((1, 2, R, LEN), lambda s, h: (s, h, 0, 0)),
            whole_rows(R),
        ],
        out_specs=[whole_rows(R), whole_rows(LEN), whole_rows(LEN), fixed((16, 128))],
        out_shape=[sds((n, R, D), bf16), sds((n, LEN, D), bf16), sds((n, LEN, D), bf16), sds((16, 128), f32)],
        scratch_shapes=[
            pltpu.VMEM((2, R, LEN), f32),
            pltpu.VMEM((2, R, LEN), bf16),
            pltpu.VMEM((HEADS, n * QP, LEN), bf16),
            pltpu.VMEM((n, LEN, QP), bf16),
            pltpu.VMEM((HEADS, 3, 128, 128), f32),
            pltpu.VMEM((HEADS, 16, 128), f32),
        ],
        compiler_params=pltpu.CompilerParams(vmem_limit_bytes=VMEM_LIMIT),
        name="attention_backward",
    )(perm[:, None], q, k, v, o, ol, r, p, do)


def norm_parts(values):
    centered = values - jnp.mean(values, axis=-1, keepdims=True)
    inv = lax.rsqrt(jnp.mean(centered * centered, axis=-1, keepdims=True) + eps_norm)
    return centered * inv, inv


def norm_back(grad, unit, inv, gain):
    scaled = grad * gain
    return inv * (
        scaled - jnp.mean(scaled, axis=-1, keepdims=True) - unit * jnp.mean(scaled * unit, axis=-1, keepdims=True)
    )


def gelu_slope(values):
    return 0.5 * (1.0 + lax.erf(values * inverse_root)) + values * jnp.exp(-0.5 * values * values) * density_scale


def project(left, right_matrix):
    return jnp.einsum("srd,de->sre", left, right_matrix, preferred_element_type=f32)


def project_back(left, right_matrix):
    return jnp.einsum("sre,de->srd", left, right_matrix, preferred_element_type=f32)


def outer_sum(left, right_rows):
    return jnp.einsum("srd,sre->de", left, right_rows, preferred_element_type=f32)


def row_sum(values):
    return jnp.sum(values.astype(f32), axis=(0, 1))


def per_device(
    content_in, query_in, permutation,
    query_weight, key_weight, value_weight, output_weight, inner_weight, outer_weight,
    query_bias, value_bias, output_bias, first_gain, first_shift, inner_bias, outer_bias,
    second_gain, second_shift, bias_table,
    content_cotangent, query_cotangent,
):
    own = query_weight.shape[0]
    n_f = lax.axis_size("fsdp")
    vectors = (
        query_bias, value_bias, output_bias, first_gain, first_shift, outer_bias, second_gain, second_shift,
        inner_bias, bias_table,
    )
    sizes = [a.shape[0] for a in vectors]

    def gather(a):
        return lax.all_gather(a, "fsdp", axis=0, tiled=True)

    packed = lax.all_gather(jnp.concatenate(vectors), "fsdp", axis=0)
    full_vectors = []
    at = 0
    for size in sizes:
        full_vectors.append(packed[:, at : at + size].reshape(-1).astype(f32))
        at += size
    bq, bv, bo, g1, s1, b2, g2, s2, b1, table_flat = full_vectors
    table = jnp.zeros((16, 128), bf16).at[:HEADS, :BUCKETS].set(
        table_flat.reshape(BUCKETS, HEADS).T.astype(bf16)
    )
    qkvo = gather(jnp.concatenate([query_weight, key_weight, value_weight, output_weight], axis=1))
    wq, wk, wv, wo = (qkvo[:, i * D : (i + 1) * D] for i in range(4))
    w1 = gather(inner_weight)
    w2 = gather(outer_weight)

    pad = ((0, 0), (0, QP - PRED), (0, 0))
    x = jnp.concatenate([content_in, jnp.pad(query_in, pad)], axis=1)
    cot = jnp.concatenate([content_cotangent, jnp.pad(query_cotangent, pad)], axis=1).astype(f32)

    q, k, v, o, ol, r, p = attention_forward(permutation, x, wq, wk, wv, bq[None], bv[None], table)

    y1 = x.astype(f32) + project(o, wo) + bo
    unit1, inv1 = norm_parts(y1)
    normed = unit1 * g1 + s1
    low1 = normed.astype(bf16)
    hidden = project(low1, w1) + b1
    act = (0.5 * hidden * (1.0 + lax.erf(hidden * inverse_root))).astype(bf16)
    y2 = normed + project(act, w2) + b2
    unit2, inv2 = norm_parts(y2)
    out = (unit2 * g2 + s2).astype(bf16)

    s2_grad = row_sum(cot)
    g2_grad = row_sum(cot * unit2)
    back2 = norm_back(cot, unit2, inv2, g2)
    d2 = back2.astype(bf16)
    b2_grad = row_sum(d2)
    w2_grad = outer_sum(act, d2)
    dh = (project_back(d2, w2) * gelu_slope(hidden)).astype(bf16)
    b1_grad = row_sum(dh)
    w1_grad = outer_sum(low1, dh)
    da = back2 + project_back(dh, w1)
    s1_grad = row_sum(da)
    g1_grad = row_sum(da * unit1)
    back1 = norm_back(da, unit1, inv1, g1)
    d1 = back1.astype(bf16)
    bo_grad = row_sum(d1)
    wo_grad = outer_sum(o, d1)
    do = project_back(d1, wo).astype(bf16)

    dq, dk, dv, table_grad = attention_backward(permutation, q, k, v, o, ol, r, p, do)

    wq_grad = outer_sum(x, dq)
    wk_grad = outer_sum(x[:, :LEN], dk)
    wv_grad = outer_sum(x[:, :LEN], dv)
    bq_grad = row_sum(dq)
    bv_grad = row_sum(dv)
    dx = back1 + project_back(dq, wq)
    content_grad = dx[:, :LEN] + project_back(dk, wk) + project_back(dv, wv)
    query_grad = dx[:, LEN : LEN + PRED]

    def scatter(a):
        return lax.psum_scatter(a.astype(bf16), "fsdp", scatter_dimension=0, tiled=True)

    qkvo_grad = scatter(jnp.concatenate([wq_grad, wk_grad, wv_grad, wo_grad], axis=1))
    w1_share = scatter(w1_grad)
    w2_share = scatter(w2_grad)
    table_grad_flat = table_grad[:HEADS, :BUCKETS].T.reshape(-1)
    vector_grads = (bq_grad, bv_grad, bo_grad, g1_grad, s1_grad, b2_grad, g2_grad, s2_grad, b1_grad, table_grad_flat)
    packed_grads = jnp.concatenate([a.reshape(n_f, -1) for a in vector_grads], axis=1)
    packed_share = lax.psum_scatter(packed_grads, "fsdp", scatter_dimension=0, tiled=True).astype(bf16)
    qkvo_grad, w1_share, w2_share, packed_share = jax.tree.map(
        lambda a: a.astype(f32), lax.psum((qkvo_grad, w1_share, w2_share, packed_share), "dp")
    )
    parts = []
    at = 0
    for size in sizes:
        parts.append(packed_share[0, at : at + size])
        at += size
    bq_s, bv_s, bo_s, g1_s, s1_s, b2_s, g2_s, s2_s, b1_s, tab_s = parts
    wq_s, wk_s, wv_s, wo_s = (qkvo_grad[:, i * D : (i + 1) * D] for i in range(4))
    return (
        out[:, :LEN], out[:, LEN : LEN + PRED], content_grad, query_grad,
        wq_s, wk_s, wv_s, wo_s, w1_share, w2_share,
        bq_s, bv_s, bo_s, g1_s, s1_s, b1_s, b2_s, g2_s, s2_s, tab_s,
    )


def solution(mesh):
    rows3 = P(("dp", "fsdp"), None, None)
    matrix = P("fsdp", None)
    vector = P("fsdp")
    return jax.shard_map(
        per_device,
        mesh=mesh,
        in_specs=(rows3, rows3, P(("dp", "fsdp"), None)) + (matrix,) * 6 + (vector,) * 10 + (rows3, rows3),
        out_specs=(rows3,) * 4 + (matrix,) * 6 + (vector,) * 10,
        check_vma=False,
    )
```

```python
import functools

import jax
import jax.numpy as jnp
from jax import lax
from jax.experimental import pallas as pl
from jax.experimental.pallas import tpu as pltpu
from jax.sharding import PartitionSpec as P

D = 768
HEADS = 12
HEAD = 64
FF = 3072
GROUP = 256
BUCKETS = 32
LEN = 512
PRED = 77
QP = 80
R = LEN + QP
f32 = jnp.float32
bf16 = jnp.bfloat16
MESH = pl.DeviceIdType.MESH
NT = (((1,), (1,)), ((), ()))
TN = (((0,), (0,)), ((), ()))

eps_norm = 1e-05
inverse_root = 0.7071067811865476
density_scale = 0.3989422804014327
bucket_edges = (12, 16, 23, 32, 46, 64, 91)
VMEM_LIMIT = 60 * 1024 * 1024


def bucket_index(relative):
    distance = jnp.abs(relative)
    coarse = 8 + sum(((distance >= boundary).astype(jnp.int32) for boundary in bucket_edges))
    within = jnp.where(distance < 8, distance, coarse)
    return within + 16 * (relative > 0).astype(jnp.int32)


def iota(shape, dim):
    return lax.broadcasted_iota(jnp.int32, shape, dim)


def ranking_column(perm_row):
    hit = perm_row == iota((LEN, LEN), 0)
    return jnp.sum(jnp.where(hit, iota((LEN, LEN), 1), 0).astype(f32), axis=1, keepdims=True)


def place():
    f = lax.axis_index("fsdp")
    return f // 4, (f // 2) % 2, f % 2, lax.axis_index("dp")


def device(z, x, c, y):
    return (y, z * 4 + x * 2 + c)


def partners():
    z, x, c, y = place()
    return [device((z + k) % 4, x, c, y) for k in (1, 2, 3)] + [
        device(z, 1 - x, c, y), device(z, x, c, 1 - y), device(z, x, 1 - c, y),
    ]


def greet():
    barrier = pltpu.get_barrier_semaphore()
    for other in partners():
        pl.semaphore_signal(barrier, inc=1, device_id=other, device_id_type=MESH)
    pl.semaphore_wait(barrier, 6)


def half_of(y, cols):
    at, size = cols
    return pl.ds(pl.multiple_of(at + y * (size // 2), 128), size // 2)


class Gather:
    def __init__(self, ref, rows, cols, send, recv, item):
        self.ref, self.rows, self.cols = ref, rows, cols
        self.send, self.recv, self.item = send, recv, item

    def copies(self, stage):
        z, x, c, y = place()
        rows = pl.ds(*self.rows)
        every = pl.ds(*self.cols)
        half = half_of(y, self.cols)

        def copy(index, part, other):
            return pltpu.make_async_remote_copy(
                src_ref=part, dst_ref=part,
                send_sem=self.send.at[self.item, index], recv_sem=self.recv.at[self.item, index],
                device_id=other, device_id_type=MESH,
            )

        ref = self.ref
        if stage == 0:
            part = ref.at[z, x, c, rows, half]
            return [copy(k - 1, part, device((z + k) % 4, x, c, y)) for k in (1, 2, 3)]
        if stage == 1:
            return [
                copy(3, ref.at[0:2, x, c, rows, half], device(z, 1 - x, c, y)),
                copy(4, ref.at[2:4, x, c, rows, half], device(z, x, c, 1 - y)),
            ]
        if stage == 2:
            return [
                copy(5, ref.at[0:2, :, c, rows, half], device(z, x, c, 1 - y)),
                copy(6, ref.at[2:4, x, c, rows, every], device(z, 1 - x, c, y)),
            ]
        return [copy(7, ref.at[:, :, c, rows, every], device(z, x, 1 - c, y))]

    def start(self, stage):
        for copy in self.copies(stage):
            copy.start()

    def arrive(self, stage):
        for copy in self.copies(stage):
            copy.wait_recv()

    def step(self, stage):
        if stage > 0:
            self.arrive(stage - 1)
        if stage < 4:
            self.start(stage)

    def drain(self):
        for stage in range(4):
            for copy in self.copies(stage):
                copy.wait_send()


def spread_vectors(raw, f):
    i = iota((256, D), 0)
    lane = iota((256, D), 1)

    def put(size, at):
        hot = jnp.where((i < size) & (lane == i + at), 1.0, 0.0).astype(bf16)
        return jnp.dot(raw, hot, preferred_element_type=f32)

    row = iota((16, D), 0)
    plain = put(D // 16, f * (D // 16))
    wide = put(192, (f % 4) * 192)
    table = put(24, f * 24)
    wide_row = jnp.sum(jnp.where(row == 8, wide, 0.0), axis=0, keepdims=True)
    return jnp.where(
        row < 8, plain, jnp.where(row == 12, table, jnp.where(row == 8 + f // 4, jnp.broadcast_to(wide_row, (16, D)), 0.0))
    )
GATHER_STEPS = {
    "g0": (-1, -1, -1, -1, -1),
    "g1": (-1, -1, -1, 3, 5),
    "g2": (-1, -1, 1, 4, 7),
    "o": (-1, 1, 3, 6, 8),
    "1a": (-1, 2, 5, 9, 12),
    "1b": (1, 4, 7, 12, 14),
    "2a": (3, 7, 11, 15, 18),
    "2b": (5, 9, 14, 18, 18),
}


def build_bias(vectors, full, near, far):
    lane = iota((16, 384), 1)
    own_head = jnp.where(lane % HEADS == iota((16, 384), 0), vectors[12:13, :384], 0.0).astype(bf16)
    rel = iota((384, 1024), 1) - 512
    onehot = (bucket_index(rel) == iota((384, 1024), 0) // HEADS).astype(bf16)
    by_rel = jnp.dot(own_head, onehot, preferred_element_type=f32)
    for h in range(HEADS):
        far[h, 0:8] = jnp.broadcast_to(by_rel[h : h + 1, 0:1], (8, 128))
        far[h, 8:16] = jnp.broadcast_to(by_rel[h : h + 1, 1023:1024], (8, 128))
        for d in range(-3, 4):
            if abs(d) >= 2:
                at = 512 + 128 * d
                block = jnp.broadcast_to(by_rel[h : h + 1, at : at + 1], (128, 128)).astype(bf16)
            else:
                base = 512 + 128 * d - 128
                row = jnp.broadcast_to(by_rel[h : h + 1, base : base + 256], (128, 256))
                tile = pltpu.roll(row, 0, 1, stride=1, stride_axis=0)[:, 128:]
                near[h, d + 1] = tile
                block = tile.astype(bf16)
            for bi in range(4):
                bj = bi + d
                if 0 <= bj < 4:
                    full[h, bi * 128 : (bi + 1) * 128, bj * 128 : (bj + 1) * 128] = block


def build_marks(s, perm_row, row_mark, key_mark, slot_hot):
    rank = ranking_column(perm_row)
    rank_row = jnp.transpose(jnp.broadcast_to(rank, (LEN, 128)))[:1]
    slot = iota((LEN, 128), 1).astype(f32) + float(LEN - PRED)
    limit = jnp.maximum(rank, float(LEN - PRED - 1))
    row_mark[s, :LEN] = jnp.where(limit < slot, 1.0, 0.0).astype(bf16)
    row_mark[s, LEN:] = jnp.where(iota((QP, 128), 0) <= iota((QP, 128), 1), 1.0, 0.0).astype(bf16)
    key_mark[s] = jnp.where(rank == slot, -1e9, 0.0).astype(bf16)
    wanted = (iota((QP, LEN), 0) + (LEN - PRED)).astype(f32)
    slot_hot[s] = (rank_row == wanted).astype(bf16)


def project_group(x, weights, vectors, g, qkv_ref):
    cols = pl.ds(pl.multiple_of(g * GROUP, 128), GROUP)
    bias_q = vectors[0:1, cols]
    bias_v = vectors[1:2, cols]
    eighth = jnp.asarray(0.125, bf16)
    rows = jnp.dot(x[:LEN], weights, preferred_element_type=f32)
    qkv_ref[0, 0, :LEN, :GROUP] = (rows[:, :GROUP] + bias_q).astype(bf16) * eighth
    qkv_ref[0, 0, :LEN, GROUP : 2 * GROUP] = rows[:, GROUP : 2 * GROUP].astype(bf16)
    qkv_ref[0, 0, :LEN, 2 * GROUP :] = (rows[:, 2 * GROUP :] + bias_v).astype(bf16)
    rows = jnp.dot(x[LEN:], weights[:, :GROUP], preferred_element_type=f32)
    qkv_ref[0, 0, LEN:, :GROUP] = (rows + bias_q).astype(bf16) * eighth


def attend_pair(s, hp, j, qkv_ref, o_ref, ol_ref, r_ref, p_ref, full, near, far, scores, row_mark, key_mark, slot_hot):
    q2 = qkv_ref[0, 0, :, pl.ds(pl.multiple_of(j * 128, 128), 128)]
    k2 = qkv_ref[0, 0, :LEN, pl.ds(pl.multiple_of(GROUP + j * 128, 128), 128)]
    v2 = qkv_ref[0, 0, :LEN, pl.ds(pl.multiple_of(2 * GROUP + j * 128, 128), 128)]
    half = iota((LEN, 128), 1) // 64
    left = jnp.concatenate([q2, row_mark[s]], axis=1)
    for h in range(2):
        right = jnp.concatenate([jnp.where(half == h, k2, jnp.zeros_like(k2)), key_mark[s]], axis=1)
        scores[h, :LEN] = lax.dot_general(left[:LEN], right, NT, preferred_element_type=f32)
        scores[h, LEN:] = lax.dot_general(left[LEN:], right, NT, preferred_element_type=f32) + jnp.dot(
            slot_hot[s], full[2 * hp + h], preferred_element_type=f32
        )
    for h in range(2):
        head = 2 * hp + h
        for bi in range(4):
            rows = slice(bi * 128, bi * 128 + 128)
            tiles = []
            for bj in range(4):
                d = bj - bi
                bias = near[head, d + 1] if abs(d) < 2 else far[head, 8:9] if d > 0 else far[head, 0:1]
                tiles.append(scores[h, rows, bj * 128 : (bj + 1) * 128] + bias)
            biased = jnp.concatenate(tiles, axis=1)
            peak = jnp.max(biased, axis=1, keepdims=True)
            p_ref[0, h, rows] = jnp.exp(biased - peak).astype(bf16)
        biased = scores[h, LEN:]
        peak = jnp.max(biased, axis=1, keepdims=True)
        p_ref[0, h, LEN:] = jnp.exp(biased - peak).astype(bf16)
    mixed = []
    for h in range(2):
        vm = jnp.where(half == h, v2, jnp.ones_like(v2))
        mixed.append(jnp.dot(p_ref[0, h], vm, preferred_element_type=f32))
    low = iota((R, 128), 1) < 64
    inverse = 1.0 / pltpu.roll(jnp.where(low, mixed[1], mixed[0]), 64, 1)
    out = jnp.where(low, mixed[0], mixed[1]) * inverse
    out_low = out.astype(bf16)
    o_ref[0] = out_low
    ol_ref[0] = (out - out_low.astype(f32)).astype(bf16)
    r_ref[0] = inverse


def forward_kernel(remote, n, *refs):
    if remote:
        (
            perm_ref, x_ref, raw_ref, wq, wk, wv, wo, w1, w2,
            qkv_ref, o_ref, ol_ref, r_ref, p_ref, vec_ref, wqkv_out, wo_out, w1_out, w2_out,
            full, near, far, scores, row_mark, key_mark, slot_hot,
            wqkv, own_qkv, vec_send, vec_recv, local_sem, send, recv, vec_send_sem, vec_recv_sem,
        ) = refs
    else:
        (
            perm_ref, x_ref, vec_in, wqkv,
            qkv_ref, o_ref, ol_ref, r_ref, p_ref,
            full, near, far, scores, row_mark, key_mark, slot_hot,
        ) = refs
    g = pl.program_id(0)
    s = pl.program_id(1)
    j = pl.program_id(2)
    step = (g * n + s) * 2 + j
    last = 3 * n * 2 - 1

    if remote:
        z, x_at, c, y = place()
        shard = D // 16
        items = {}
        for i in range(3):
            items[f"g{i}"] = Gather(wqkv.at[i], (0, shard), (0, D), send, recv, i)
        items["o"] = Gather(wo_out, (0, shard), (0, D), send, recv, 3)
        items["1a"] = Gather(w1_out, (0, shard), (0, FF // 2), send, recv, 4)
        items["1b"] = Gather(w1_out, (0, shard), (FF // 2, FF // 2), send, recv, 5)
        items["2a"] = Gather(w2_out, (0, 96), (0, D), send, recv, 6)
        items["2b"] = Gather(w2_out, (96, 96), (0, D), send, recv, 7)
        own = []
        for part, whole, cols in (
            (wo, wo_out, (0, D)), (w1, w1_out, (0, FF // 2)), (w1, w1_out, (FF // 2, FF // 2)), (w2, w2_out, (0, D)),
        ):
            half = half_of(y, cols)
            own.append(
                pltpu.make_async_copy(part.at[:, half], whole.at[z, x_at, c, :, half], local_sem.at[len(own)])
            )

        def vec_copy(k):
            other = (
                device(z, x_at, 1 - c, y), device(z, 1 - x_at, c, y),
                *(device((z + t) % 4, x_at, c, y) for t in (1, 2, 3)),
            )[k]
            return pltpu.make_async_remote_copy(
                src_ref=vec_send.at[min(k, 2)], dst_ref=vec_recv.at[k],
                send_sem=vec_send_sem.at[k], recv_sem=vec_recv_sem.at[k], device_id=other, device_id_type=MESH,
            )

        @pl.when(step == 0)
        def _():
            greet()
            half = half_of(y, (0, D))
            for i in range(3):
                for m, part in enumerate((wq, wk, wv)):
                    own_qkv[i, :, m * GROUP : (m + 1) * GROUP] = part[:, i * GROUP : (i + 1) * GROUP]
                wqkv[i, z, x_at, c, :, half] = own_qkv[i, :, half]
            items["g0"].step(0)
            for copy in own:
                copy.start()
            vec_send[0] = spread_vectors(raw_ref[...], z * 4 + x_at * 2 + c)
            vec_copy(0).start()
            build_marks(0, perm_ref[0], row_mark, key_mark, slot_hot)
            items["g0"].step(1)
            items["g1"].step(0)
            items["g2"].step(0)
            vec_copy(0).wait_recv()
            vec_send[1] = vec_send[0] + vec_recv[0]
            vec_copy(1).start()
            items["g0"].step(2)
            for i in range(1, n):
                build_marks(i, perm_ref[i], row_mark, key_mark, slot_hot)
            vec_copy(1).wait_recv()
            vec_send[2] = vec_send[1] + vec_recv[1]
            for k in (2, 3, 4):
                vec_copy(k).start()
            items["g1"].step(1)
            for copy in own:
                copy.wait()
            items["o"].step(0)
            for k in (2, 3, 4):
                vec_copy(k).wait_recv()
            vec_ref[...] = vec_send[2] + vec_recv[2] + vec_recv[3] + vec_recv[4]
            build_bias(vec_ref[...], full, near, far)
            items["g2"].step(1)
            items["1a"].step(0)
            items["g0"].step(3)
            items["g1"].step(2)
            items["g0"].step(4)

        for at in sorted({a for steps in GATHER_STEPS.values() for a in steps if 0 <= a <= last}):

            @pl.when(step == at)
            def _(at=at):
                for stage in range(5):
                    for name, steps in GATHER_STEPS.items():
                        if steps[stage] == at:
                            items[name].step(stage)
        vectors = vec_ref
    else:
        vectors = vec_in

        @pl.when(step == 0)
        def _():
            for i in range(n):
                build_marks(i, perm_ref[i], row_mark, key_mark, slot_hot)
            build_bias(vec_in[...], full, near, far)

    @pl.when(j == 0)
    def _():
        weights = wqkv[g].reshape(D, D) if remote else wqkv[g]
        project_group(x_ref[s], weights, vectors, g, qkv_ref)

    attend_pair(
        s, 2 * g + j, j, qkv_ref, o_ref, ol_ref, r_ref, p_ref,
        full, near, far, scores, row_mark, key_mark, slot_hot,
    )

    if remote:

        @pl.when(step == last)
        def _():
            back = pltpu.make_async_copy(wqkv, wqkv_out, local_sem.at[0])
            back.start()
            for stage in range(5):
                for name, steps in GATHER_STEPS.items():
                    if steps[stage] > last:
                        items[name].step(stage)
            for k in range(5):
                vec_copy(k).wait_send()
            for item in items.values():
                item.drain()
            back.wait()


VMEM_WHOLE = pl.BlockSpec(memory_space=pltpu.VMEM)
ANYWHERE = pl.BlockSpec(memory_space=pl.ANY)


def forward_call(n, remote, *operands):
    sds = jax.ShapeDtypeStruct
    pair = pl.BlockSpec((1, R, 128), lambda g, s, j: (s, 0, 2 * g + j))
    out_specs = [
        pl.BlockSpec((1, 1, R, D), lambda g, s, j: (g, s, 0, 0)), pair, pair, pair,
        pl.BlockSpec((1, 2, R, LEN), lambda g, s, j: (s, 2 * g + j, 0, 0)),
    ]
    out_shape = [
        sds((3, n, R, D), bf16), sds((n, R, D), bf16), sds((n, R, D), bf16), sds((n, R, D), f32),
        sds((n, HEADS, R, LEN), bf16),
    ]
    scratch = [
        pltpu.VMEM((HEADS, LEN, LEN), bf16),
        pltpu.VMEM((HEADS, 3, 128, 128), f32),
        pltpu.VMEM((HEADS, 16, 128), f32),
        pltpu.VMEM((2, R, LEN), f32),
        pltpu.VMEM((n, R, 128), bf16),
        pltpu.VMEM((n, LEN, 128), bf16),
        pltpu.VMEM((n, QP, LEN), bf16),
    ]
    if remote:
        in_specs = [VMEM_WHOLE] * 9
        out_specs += [pl.BlockSpec((16, D), lambda g, s, j: (0, 0))] + [ANYWHERE] * 4
        block = (4, 2, 2, D // 16)
        out_shape += [
            sds((16, D), f32), sds((3, *block, D), bf16), sds((*block, D), bf16), sds((*block, FF), bf16),
            sds((4, 2, 2, FF // 16, D), bf16),
        ]
        scratch += [
            pltpu.VMEM((3, *block, D), bf16),
            pltpu.VMEM((3, D // 16, D), bf16),
            pltpu.VMEM((3, 16, D), f32),
            pltpu.VMEM((5, 16, D), f32),
            pltpu.SemaphoreType.DMA((4,)),
            pltpu.SemaphoreType.DMA((8, 8)),
            pltpu.SemaphoreType.DMA((8, 8)),
            pltpu.SemaphoreType.DMA((5,)),
            pltpu.SemaphoreType.DMA((5,)),
        ]
        params = pltpu.CompilerParams(vmem_limit_bytes=VMEM_LIMIT, collective_id=1, has_side_effects=True)
    else:
        in_specs = [VMEM_WHOLE] * 4
        params = pltpu.CompilerParams(vmem_limit_bytes=VMEM_LIMIT)
    return pl.pallas_call(
        functools.partial(forward_kernel, remote, n),
        grid=(3, n, 2),
        in_specs=in_specs,
        out_specs=out_specs,
        out_shape=out_shape,
        scratch_shapes=scratch,
        compiler_params=params,
        name="attention_forward",
    )(*operands)

REDUCE_STEPS = {
    "2a": (0, 1, 4, 6, 8, 10),
    "2b": (0, 3, 8, 10, 12, 14),
    "1a": (2, 6, 11, 13, 15, 17),
    "1b": (5, 9, 14, 16, 18, 18),
    "o": (9, 12, 16, 18, 18, 18),
    "g0": (7, 14, 18, 18, 18, 18),
    "g1": (13, 16, 18, 18, 18, 18),
    "g2": (18, 18, 18, 18, 18, 18),
}


def add(a, b):
    return (a.astype(f32) + b.astype(f32)).astype(bf16)


class Reduce:
    @staticmethod
    def scratch(rows, cols, loads):
        half = cols // 2
        shapes = [
            (4, 2, rows, cols), (2, 2, rows, half), (2, rows, cols), (2, rows, half), (2, rows, half),
            (4, rows, half), (3, rows, half),
        ]
        if loads:
            shapes.append((4, 2, rows, cols))
        return [pltpu.VMEM(shape, bf16) for shape in shapes]

    def __init__(self, source, at, rows, cols, bufs, out, send, recv, load, item):
        self.source, self.at, self.rows, self.cols = source, at, rows, cols
        self.rc, self.ry, self.rx, self.sx, self.sy, self.a3, self.rz = bufs[:7]
        self.own = bufs[7] if len(bufs) > 7 else None
        self.out, self.send, self.recv, self.load, self.item = out, send, recv, load, item

    def part(self, core):
        rows = pl.ds(self.at[0], self.rows)
        cols = pl.ds(self.at[1], self.cols)
        return self.source.at[:, :, core, rows, cols]

    def load_copy(self):
        z, x, c, y = place()
        return pltpu.make_async_copy(self.part(c), self.own, self.load)

    def copies(self, stage):
        z, x, c, y = place()
        half = self.cols // 2
        other_half = pl.ds(pl.multiple_of((1 - y) * half, 128), half)

        def copy(index, src, dst, other):
            return pltpu.make_async_remote_copy(
                src_ref=src, dst_ref=dst,
                send_sem=self.send.at[self.item, index], recv_sem=self.recv.at[self.item, index],
                device_id=other, device_id_type=MESH,
            )

        if stage == 0:
            return [copy(0, self.part(1 - c), self.rc, device(z, x, 1 - c, y))]
        if stage == 1:
            return [
                copy(1, self.rc.at[0:2, :, :, other_half], self.ry, device(z, x, c, 1 - y)),
                copy(2, self.rc.at[2:4, 1 - x], self.rx, device(z, 1 - x, c, y)),
            ]
        if stage == 2:
            return [
                copy(3, self.ry.at[:, 1 - x], self.sx, device(z, 1 - x, c, y)),
                copy(4, self.rx.at[:, :, other_half], self.sy, device(z, x, c, 1 - y)),
            ]
        if stage == 3:
            return [
                copy(4 + k, self.a3.at[(z + k) % 4], self.rz.at[k - 1], device((z + k) % 4, x, c, y))
                for k in (1, 2, 3)
            ]
        return [copy(8, self.out.at[y], self.out.at[y], device(z, x, c, 1 - y))]

    def combine(self, stage):
        z, x, c, y = place()
        half = self.cols // 2
        own_half = pl.ds(pl.multiple_of(y * half, 128), half)
        if stage == 0:
            if self.own is not None:
                self.load_copy().wait()
            for i in range(4):
                for k in range(2):
                    mine = self.own[i, k] if self.own is not None else self.source[i, k, c]
                    self.rc[i, k] = add(self.rc[i, k], mine)
        elif stage == 1:
            for i in range(2):
                for k in range(2):
                    self.ry[i, k] = add(self.ry[i, k], self.rc[i, k, :, own_half])
                self.rx[i] = add(self.rx[i], self.rc[2 + i, x])
        elif stage == 2:
            for i in range(2):
                self.a3[i] = add(self.sx[i], self.ry[i, x])
                self.a3[2 + i] = add(self.sy[i], self.rx[i, :, own_half])
        elif stage == 3:
            total = self.a3[z].astype(f32)
            for k in range(3):
                total = total + self.rz[k].astype(f32)
            self.out[y] = total.astype(bf16)

    def step(self, stage):
        if stage == 0 and self.own is not None:
            self.load_copy().start()
        if stage > 0:
            for copy in self.copies(stage - 1):
                copy.wait_recv()
            if stage < 5:
                self.combine(stage - 1)
        if stage < 5:
            for copy in self.copies(stage):
                copy.start()

    def drain(self):
        for stage in range(5):
            for copy in self.copies(stage):
                copy.wait_send()


def reduce_table(group, n, slot_cols, kept, near_sum, far_sum):
    c = iota((896, 128), 0)
    rel = jnp.where(c < 768, 128 * (c // 256 - 1) + c % 256 - 128, jnp.where(c % 128 < 64, -200, 200))
    onehot = (bucket_index(rel) == iota((896, 128), 1)).astype(f32)
    slots = jnp.concatenate([slot_cols[i] for i in range(n)], axis=1)
    sub = iota((8, 256), 0)
    lane8 = iota((8, 128), 1)
    lane1 = iota((1, 128), 1)
    rows = []
    for head in range(4):
        moved = jnp.dot(slots, kept[head], preferred_element_type=f32)
        near = [near_sum[head, d] for d in range(3)]
        far = [far_sum[head, 0:8], far_sum[head, 8:16]]
        for bi in range(4):
            for bj in range(4):
                d = bj - bi
                tile = moved[bi * 128 : (bi + 1) * 128, bj * 128 : (bj + 1) * 128]
                if abs(d) < 2:
                    near[d + 1] = near[d + 1] + tile
                else:
                    far[int(d > 0)] = far[int(d > 0)] + tile.reshape(16, 8, 128).sum(0)
        parts = []
        for d in range(3):
            high = low = None
            for a in range(16):
                x = near[d][8 * a : 8 * a + 8]
                if a:
                    x = pltpu.roll(x, 128 - 8 * a, 1)
                keep = lane8 < 128 - 8 * a
                u = jnp.where(keep, x, 0.0)
                w = jnp.where(keep, 0.0, x)
                high = u if high is None else high + u
                low = w if low is None else low + w
            y = jnp.concatenate([low, high], axis=1)
            for k in (1, 2, 4):
                y = jnp.where((sub & k) != 0, pltpu.roll(y, 256 - k, 1), y)
            parts.append(jnp.sum(y, axis=0, keepdims=True))
        parts.append(jnp.where(lane1 == 0, jnp.sum(far[0]), jnp.where(lane1 == 64, jnp.sum(far[1]), 0.0)))
        rows.append(jnp.concatenate(parts, axis=1))
    rows.append(jnp.zeros((4, 896), f32))
    return jnp.dot(
        jnp.concatenate(rows, axis=0), onehot, preferred_element_type=f32, precision=lax.Precision.HIGHEST
    )


def table_row(by_head):
    spread = (iota((128, D), 0) == iota((128, D), 1) // HEADS).astype(f32)
    wide = jnp.dot(by_head, spread, preferred_element_type=f32, precision=lax.Precision.HIGHEST)
    lane = iota((16, D), 1)
    mine = (lane % HEADS == iota((16, D), 0)) & (lane < BUCKETS * HEADS)
    return jnp.sum(jnp.where(mine, wide, 0.0), axis=0, keepdims=True)


def attend_pair_back(
    s, hp, j, qkv_ref, o_ref, ol_ref, r_ref, p_ref, do_ref, dqkv, dp, ds, kept, near_sum, far_sum
):
    q2 = qkv_ref[0, 0, :, pl.ds(pl.multiple_of(j * 128, 128), 128)]
    k2 = qkv_ref[0, 0, :LEN, pl.ds(pl.multiple_of(GROUP + j * 128, 128), 128)]
    v2 = qkv_ref[0, 0, :LEN, pl.ds(pl.multiple_of(2 * GROUP + j * 128, 128), 128)]
    delta = (do_ref[0].astype(f32) * r_ref[0]).astype(bf16)
    prod = delta.astype(f32) * (o_ref[0].astype(f32) + ol_ref[0].astype(f32))
    high = prod.astype(bf16)
    rest = pltpu.roll(prod - high.astype(f32), 64, 1).astype(bf16)
    low = iota((R, 128), 1) < 64
    half = iota((LEN, 128), 1) // 64
    extra = [jnp.where(low, high, rest), jnp.where(low, rest, high)]
    minus = jnp.full((LEN, 128), -1.0, bf16)
    for h in range(2):
        vm = jnp.where(half == h, v2, jnp.zeros_like(v2))
        dp[h] = lax.dot_general(
            jnp.concatenate([delta, extra[h]], axis=1),
            jnp.concatenate([vm, minus], axis=1),
            NT,
            preferred_element_type=f32,
        )
    for h in range(2):
        head = 2 * j + h
        far = [None, None]
        for bi in range(4):
            rows = slice(bi * 128, bi * 128 + 128)
            d_rows = p_ref[0, h, rows].astype(f32) * dp[h, rows]
            ds[h, rows] = d_rows.astype(bf16)
            for bj in range(4):
                d = bj - bi
                tile = d_rows[:, bj * 128 : (bj + 1) * 128]
                if abs(d) < 2:
                    near_sum[head, d + 1] += tile
                else:
                    part = tile.reshape(16, 8, 128).sum(0)
                    far[int(d > 0)] = part if far[int(d > 0)] is None else far[int(d > 0)] + part
        far_sum[head, 0:8] += far[0]
        far_sum[head, 8:16] += far[1]
        d_slots = (p_ref[0, h, LEN:].astype(f32) * dp[h, LEN:]).astype(bf16)
        ds[h, LEN:] = d_slots
        kept[head, pl.ds(pl.multiple_of(s * QP, 16), QP)] = d_slots
    dq = None
    for h in range(2):
        km = jnp.where(half == h, k2, jnp.zeros_like(k2))
        part = jnp.dot(ds[h], km, preferred_element_type=f32)
        dq = part if dq is None else dq + part
    dqkv[s, :, pl.ds(pl.multiple_of(j * 128, 128), 128)] = (dq * 0.125).astype(bf16)
    q_t = jnp.transpose(q2)
    delta_t = jnp.transpose(delta)
    dk_t = [jnp.dot(q_t[h * 64 : (h + 1) * 64], ds[h], preferred_element_type=f32) for h in range(2)]
    dv_t = [jnp.dot(delta_t[h * 64 : (h + 1) * 64], p_ref[0, h], preferred_element_type=f32) for h in range(2)]
    dqkv[s, :LEN, pl.ds(pl.multiple_of(GROUP + j * 128, 128), 128)] = jnp.transpose(
        jnp.concatenate(dk_t, axis=0).astype(bf16)
    )
    dqkv[s, :LEN, pl.ds(pl.multiple_of(2 * GROUP + j * 128, 128), 128)] = jnp.transpose(
        jnp.concatenate(dv_t, axis=0).astype(bf16)
    )


def backward_kernel(remote, n, *refs):
    (
        perm_ref, x_ref, wqkv, vec_in, qkv_ref, o_ref, ol_ref, r_ref, p_ref, do_ref, dy_ref,
        *refs,
    ) = refs
    if remote:
        (
            wo_grad, w1_grad, w2_grad,
            dx_ref, vec_ref, g_out, o_out, w1_out, w2_out,
            dx, dqkv, dp, ds, kept, slot_cols, near_sum, far_sum, tab, dy_sem,
            wqkv_grad, g_sum, o_sum, w1_sum, w2_sum, vec_send, vec_recv, load_sem, send, recv, vec_send_sem, vec_recv_sem,
            *bufs,
        ) = refs
    else:
        (
            dx_ref, vec_ref, wqkv_grad,
            dx, dqkv, dp, ds, kept, slot_cols, near_sum, far_sum, tab, dy_sem,
        ) = refs
    g = pl.program_id(0)
    s = pl.program_id(1)
    j = pl.program_id(2)
    step = (g * n + s) * 2 + j
    last = 3 * n * 2 - 1
    dy_copy = pltpu.make_async_copy(dy_ref, dx, dy_sem)

    if remote:
        z, x_at, c, y = place()
        shard = D // 16
        wide = 2 * FF // 4

        def item(name, index, source, at, rows, cols, out):
            first = index * 8 if index < 5 else 40 + (index - 5) * 7
            take = 8 if index < 5 else 7
            return Reduce(
                source, at, rows, cols, bufs[first : first + take], out, send, recv,
                load_sem.at[index] if index < 5 else None, index,
            )

        items = {
            "2a": item("2a", 0, w2_grad, (0, 0), 96, D, w2_sum.at[0]),
            "2b": item("2b", 1, w2_grad, (96, 0), 96, D, w2_sum.at[1]),
            "1a": item("1a", 2, w1_grad, (0, 0), shard, wide, w1_sum.at[0]),
            "1b": item("1b", 3, w1_grad, (0, wide), shard, wide, w1_sum.at[1]),
            "o": item("o", 4, wo_grad, (0, 0), shard, D, o_sum),
        }
        for i in range(3):
            items[f"g{i}"] = item(f"g{i}", 5 + i, wqkv_grad.at[i], (0, 0), shard, D, g_sum.at[i])

        def vec_copy(k):
            other = (
                device(z, x_at, 1 - c, y), device(z, x_at, c, 1 - y), device(z, 1 - x_at, c, y),
                *(device((z + t) % 4, x_at, c, y) for t in (1, 2, 3)),
            )[k]
            return pltpu.make_async_remote_copy(
                src_ref=vec_send.at[min(k, 3)], dst_ref=vec_recv.at[k],
                send_sem=vec_send_sem.at[k], recv_sem=vec_recv_sem.at[k], device_id=other, device_id_type=MESH,
            )

    @pl.when(step == 0)
    def _():
        dy_copy.start()
        if remote:
            greet()
        vec_ref[...] = vec_in[...]
        for i in range(n):
            rank = ranking_column(perm_ref[i])
            slot_cols[i] = (rank == (iota((LEN, QP), 1) + (LEN - PRED)).astype(f32)).astype(bf16)
        dqkv[:, LEN:, GROUP:] = jnp.zeros((n, QP, 2 * GROUP), bf16)

    if remote:
        for at in sorted({a for steps in REDUCE_STEPS.values() for a in steps if a <= last}):

            @pl.when(step == at)
            def _(at=at):
                for stage in range(6):
                    for name, steps in REDUCE_STEPS.items():
                        if steps[stage] == at:
                            items[name].step(stage)

    @pl.when((s == 0) & (j == 0))
    def _():
        near_sum[...] = jnp.zeros_like(near_sum)
        far_sum[...] = jnp.zeros_like(far_sum)

    attend_pair_back(
        s, 2 * g + j, j, qkv_ref, o_ref, ol_ref, r_ref, p_ref, do_ref, dqkv, dp, ds, kept, near_sum, far_sum
    )

    @pl.when(step == 1)
    def _():
        dy_copy.wait()

    @pl.when((s == n - 1) & (j == 1))
    def _():
        total = None
        for i in range(n):
            part = lax.dot_general(x_ref[i], dqkv[i], TN, preferred_element_type=f32)
            total = part if total is None else total + part
        total = total.astype(bf16)
        wqkv_grad[g] = total.reshape(4, 2, 2, D // 16, D) if remote else total

    if remote:

        @pl.when(step == last)
        def _():
            items["g2"].step(0)

    @pl.when(j == 1)
    def _():
        weights = wqkv[g]
        dx[s] += lax.dot_general(dqkv[s], weights, NT, preferred_element_type=f32)

    @pl.when((s == n - 1) & (j == 1))
    def _():
        tab[g] = reduce_table(g, n, slot_cols, kept, near_sum, far_sum)
        sums = jnp.sum(dqkv[0].astype(f32), axis=0, keepdims=True)
        for i in range(1, n):
            sums = sums + jnp.sum(dqkv[i].astype(f32), axis=0, keepdims=True)
        cols = pl.ds(pl.multiple_of(g * GROUP, 128), GROUP)
        vec_ref[0:1, cols] = sums[:, :GROUP]
        vec_ref[1:2, cols] = sums[:, 2 * GROUP :]

    @pl.when(step == last)
    def _():
        by_head = jnp.concatenate([tab[0, :4], tab[1, :4], tab[2, :4], jnp.zeros((4, 128), f32)], axis=0)
        vec_ref[12:13] = table_row(by_head)
        out_copy = pltpu.make_async_copy(dx, dx_ref, dy_sem)
        out_copy.start()
        if remote:
            vec_send[0] = vec_ref[...]
            vec_copy(0).start()
            tail = [(stage, name) for stage in range(6) for name in REDUCE_STEPS if REDUCE_STEPS[name][stage] > last]
            tail.remove((0, "g2"))
            order = sorted(tail, key=lambda t: t[0] - LATE[t[1]])
            done = 0
            for count, (stage, name) in enumerate(order):
                items[name].step(stage)
                if done < 3 and count >= 2 * (done + 1):
                    vec_copy(done).wait_recv()
                    vec_send[done + 1] = vec_send[done] + vec_recv[done]
                    done += 1
                    for k in (done,) if done < 3 else (3, 4, 5):
                        vec_copy(k).start()
            for k in (3, 4, 5):
                vec_copy(k).wait_recv()
            vec_ref[...] = vec_send[3] + vec_recv[3] + vec_recv[4] + vec_recv[5]
            for k in range(6):
                vec_copy(k).wait_send()
            for entry in items.values():
                entry.drain()
            g_out[...] = g_sum[...]
            o_out[...] = o_sum[...]
            w1_out[...] = w1_sum[...]
            w2_out[...] = w2_sum[...]
        out_copy.wait()


LATE = {"2a": 0, "2b": 0, "1a": 0, "1b": 0, "o": 1, "g0": 2, "g1": 3, "g2": 4}


def backward_call(n, remote, *operands):
    sds = jax.ShapeDtypeStruct
    pair = pl.BlockSpec((1, R, 128), lambda g, s, j: (s, 0, 2 * g + j))
    block = (4, 2, 2, D // 16)
    in_specs = [VMEM_WHOLE] * 4 + [
        pl.BlockSpec((1, 1, R, D), lambda g, s, j: (g, s, 0, 0)), pair, pair, pair,
        pl.BlockSpec((1, 2, R, LEN), lambda g, s, j: (s, 2 * g + j, 0, 0)),
        pair, ANYWHERE,
    ]
    small = pl.BlockSpec((16, D), lambda g, s, j: (0, 0))
    out_specs = [ANYWHERE, small]
    out_shape = [sds((n, R, D), f32), sds((16, D), f32)]
    scratch = [
        pltpu.VMEM((n, R, D), f32),
        pltpu.VMEM((n, R, D), bf16),
        pltpu.VMEM((2, R, LEN), f32),
        pltpu.VMEM((2, R, LEN), bf16),
        pltpu.VMEM((4, n * QP, LEN), bf16),
        pltpu.VMEM((n, LEN, QP), bf16),
        pltpu.VMEM((4, 3, 128, 128), f32),
        pltpu.VMEM((4, 16, 128), f32),
        pltpu.VMEM((3, 8, 128), f32),
        pltpu.SemaphoreType.DMA,
    ]
    if remote:
        in_specs += [ANYWHERE] * 3
        out_specs += [VMEM_WHOLE] * 4
        shard = D // 16
        out_shape += [
            sds((3, 2, shard, D // 2), bf16), sds((2, shard, D // 2), bf16), sds((2, 2, shard, FF // 4), bf16),
            sds((2, 2, 96, D // 2), bf16),
        ]
        scratch += [
            pltpu.VMEM((3, *block, D), bf16),
            *(pltpu.VMEM(a.shape, bf16) for a in out_shape[2:]),
            pltpu.VMEM((4, 16, D), f32),
            pltpu.VMEM((6, 16, D), f32),
            pltpu.SemaphoreType.DMA((5,)),
            pltpu.SemaphoreType.DMA((8, 9)),
            pltpu.SemaphoreType.DMA((8, 9)),
            pltpu.SemaphoreType.DMA((6,)),
            pltpu.SemaphoreType.DMA((6,)),
        ]
        for rows, cols in ((96, D), (96, D), (shard, FF // 2), (shard, FF // 2), (shard, D)):
            scratch += Reduce.scratch(rows, cols, True)
        for _ in range(3):
            scratch += Reduce.scratch(shard, D, False)
        params = pltpu.CompilerParams(vmem_limit_bytes=VMEM_LIMIT, collective_id=2, has_side_effects=True)
    else:
        out_specs += [pl.BlockSpec(memory_space=pltpu.VMEM)]
        out_shape += [sds((3, D, D), bf16)]
        params = pltpu.CompilerParams(vmem_limit_bytes=VMEM_LIMIT)
    return pl.pallas_call(
        functools.partial(backward_kernel, remote, n),
        grid=(3, n, 2),
        in_specs=in_specs,
        out_specs=out_specs,
        out_shape=out_shape,
        scratch_shapes=scratch,
        compiler_params=params,
        name="attention_backward",
    )(*operands)
def norm_parts(values):
    centered = values - jnp.mean(values, axis=-1, keepdims=True)
    inv = lax.rsqrt(jnp.mean(centered * centered, axis=-1, keepdims=True) + eps_norm)
    return centered * inv, inv


def norm_back(grad, unit, inv, gain):
    scaled = grad * gain
    return inv * (
        scaled - jnp.mean(scaled, axis=-1, keepdims=True) - unit * jnp.mean(scaled * unit, axis=-1, keepdims=True)
    )


def gelu_slope(values):
    return 0.5 * (1.0 + lax.erf(values * inverse_root)) + values * jnp.exp(-0.5 * values * values) * density_scale


def project(left, right_matrix):
    return jnp.einsum("srd,de->sre", left, right_matrix, preferred_element_type=f32)


def project_back(left, right_matrix):
    return jnp.einsum("sre,de->srd", left, right_matrix, preferred_element_type=f32)


def outer_sum(left, right_rows):
    return jnp.einsum("srd,sre->de", left, right_rows, preferred_element_type=f32)


def row_sum(values):
    return jnp.sum(values.astype(f32), axis=(0, 1))


def middle(x, o, cot, vec, wo, w1, w2):
    bo, g1, s1, b2, g2, s2 = (vec[i] for i in range(2, 8))
    b1 = vec[8:12].reshape(-1)
    y1 = x.astype(f32) + project(o, wo) + bo
    unit1, inv1 = norm_parts(y1)
    normed = unit1 * g1 + s1
    low1 = normed.astype(bf16)
    hidden = project(low1, w1) + b1
    act = (0.5 * hidden * (1.0 + lax.erf(hidden * inverse_root))).astype(bf16)
    y2 = normed + project(act, w2) + b2
    unit2, inv2 = norm_parts(y2)
    out = (unit2 * g2 + s2).astype(bf16)
    s2_grad = row_sum(cot)
    g2_grad = row_sum(cot * unit2)
    back2 = norm_back(cot, unit2, inv2, g2)
    d2 = back2.astype(bf16)
    b2_grad = row_sum(d2)
    w2_grad = outer_sum(act, d2).astype(bf16)
    dh = (project_back(d2, w2) * gelu_slope(hidden)).astype(bf16)
    b1_grad = row_sum(dh)
    w1_grad = outer_sum(low1, dh).astype(bf16)
    da = back2 + project_back(dh, w1)
    s1_grad = row_sum(da)
    g1_grad = row_sum(da * unit1)
    back1 = norm_back(da, unit1, inv1, g1)
    d1 = back1.astype(bf16)
    bo_grad = row_sum(d1)
    wo_grad = outer_sum(o, d1).astype(bf16)
    do = project_back(d1, wo).astype(bf16)
    zero = jnp.zeros((D,), f32)
    rows = [zero, zero, bo_grad, g1_grad, s1_grad, b2_grad, g2_grad, s2_grad, *b1_grad.reshape(4, D), zero, zero, zero, zero]
    return out, do, back1, jnp.stack(rows), wo_grad, w1_grad, w2_grad


def pieces(own_vectors, places):
    return sum(jnp.pad(v[None], ((at, 15 - at), (0, 256 - v.shape[0]))) for at, v in zip(places, own_vectors))


ROWS = (0, 1, 2, 3, 4, 5, 6, 7, 8, 12)


def per_device(
    content_in, query_in, permutation,
    query_weight, key_weight, value_weight, output_weight, inner_weight, outer_weight,
    query_bias, value_bias, output_bias, first_gain, first_shift, inner_bias, outer_bias,
    second_gain, second_shift, bias_table,
    content_cotangent, query_cotangent,
):
    n = content_in.shape[0]
    n_f = lax.axis_size("fsdp")
    remote = n_f == 16 and lax.axis_size("dp") == 2 and n >= 2
    f = lax.axis_index("fsdp")
    vectors = (
        query_bias, value_bias, output_bias, first_gain, first_shift, outer_bias, second_gain, second_shift,
        inner_bias, bias_table,
    )
    sizes = [a.shape[0] for a in vectors]
    pad = ((0, 0), (0, QP - PRED), (0, 0))
    x = jnp.concatenate([content_in, jnp.pad(query_in, pad)], axis=1)
    perm = permutation[:, None]
    if remote:
        qkv, o, ol, r, p, vec, wqkv, wo, w1, w2 = forward_call(
            n, True, perm, x, pieces(vectors, ROWS),
            query_weight, key_weight, value_weight, output_weight, inner_weight, outer_weight,
        )
        wqkv = wqkv.reshape(3, D, D)
        wo, w1, w2 = wo.reshape(D, D), w1.reshape(D, FF), w2.reshape(FF, D)
    else:
        packed = lax.all_gather(jnp.concatenate(vectors), "fsdp", axis=0)
        rows = []
        at = 0
        for size in sizes:
            whole = packed[:, at : at + size].reshape(-1).astype(f32)
            rows.append(jnp.pad(whole, (0, -whole.shape[0] % D)).reshape(-1, D))
            at += size
        vec = jnp.concatenate(rows + [jnp.zeros((3, D), f32)], axis=0)
        whole = lax.all_gather(
            jnp.concatenate([query_weight, key_weight, value_weight, output_weight, inner_weight], axis=1),
            "fsdp", axis=0, tiled=True,
        )
        wqkv = jnp.stack(
            [
                jnp.concatenate([whole[:, m * D + g * GROUP : m * D + (g + 1) * GROUP] for m in range(3)], axis=1)
                for g in range(3)
            ]
        )
        wo, w1 = whole[:, 3 * D : 4 * D], whole[:, 4 * D :]
        w2 = lax.all_gather(outer_weight, "fsdp", axis=0, tiled=True)
        qkv, o, ol, r, p = forward_call(n, False, perm, x, vec, wqkv)

    cot = jnp.concatenate([content_cotangent, jnp.pad(query_cotangent, pad)], axis=1).astype(f32)
    out, do, dy, vec_grad, wo_grad, w1_grad, w2_grad = middle(x, o, cot, vec, wo, w1, w2)

    if remote:
        block = (4, 2, 2)
        dx, vec_grad, g_sum, o_sum, w1_sum, w2_sum = backward_call(
            n, True, perm, x, wqkv, vec_grad, qkv, o, ol, r, p, do, dy,
            wo_grad.reshape(*block, D // 16, D), w1_grad.reshape(*block, D // 16, FF),
            w2_grad.reshape(*block, FF // 16, D),
        )
        g_sum = jnp.concatenate([g_sum[:, 0], g_sum[:, 1]], axis=-1).astype(f32)
        wq_s, wk_s, wv_s = (
            jnp.concatenate([g_sum[g, :, m * GROUP : (m + 1) * GROUP] for g in range(3)], axis=1) for m in range(3)
        )
        wo_s = jnp.concatenate([o_sum[0], o_sum[1]], axis=1).astype(f32)
        w1_s = jnp.concatenate([w1_sum[i, k] for i in range(2) for k in range(2)], axis=1).astype(f32)
        w2_s = jnp.concatenate(
            [jnp.concatenate([w2_sum[i, 0], w2_sum[i, 1]], axis=1) for i in range(2)], axis=0
        ).astype(f32)
        whole_rows = [vec_grad[i] for i in range(8)] + [vec_grad[8:12].reshape(-1), vec_grad[12, : BUCKETS * HEADS]]
        shares = [lax.dynamic_slice_in_dim(v, f * size, size, 0) for v, size in zip(whole_rows, sizes)]
    else:
        dx, vec_grad, wqkv_grad = backward_call(n, False, perm, x, wqkv, vec_grad, qkv, o, ol, r, p, do, dy)

        def scatter(a):
            return lax.psum_scatter(a, "fsdp", scatter_dimension=0, tiled=True)

        flat = jnp.concatenate(
            [wqkv_grad[g, :, m * GROUP : (m + 1) * GROUP] for m in range(3) for g in range(3)] + [wo_grad, w1_grad],
            axis=1,
        )
        whole_rows = [vec_grad[i] for i in range(8)] + [vec_grad[8:12].reshape(-1), vec_grad[12, : BUCKETS * HEADS]]
        packed = jnp.concatenate([v.reshape(n_f, -1) for v in whole_rows], axis=1)
        sums = lax.psum((scatter(flat), scatter(w2_grad), scatter(packed).astype(bf16)), "dp")
        flat, w2_s, packed = (a.astype(f32) for a in sums)
        wq_s, wk_s, wv_s, wo_s = (flat[:, m * D : (m + 1) * D] for m in range(4))
        w1_s = flat[:, 4 * D :]
        shares = []
        at = 0
        for size in sizes:
            shares.append(packed[0, at : at + size])
            at += size
    bq_s, bv_s, bo_s, g1_s, s1_s, b2_s, g2_s, s2_s, b1_s, tab_s = shares
    return (
        out[:, :LEN], out[:, LEN : LEN + PRED], dx[:, :LEN], dx[:, LEN : LEN + PRED],
        wq_s, wk_s, wv_s, wo_s, w1_s, w2_s,
        bq_s, bv_s, bo_s, g1_s, s1_s, b1_s, b2_s, g2_s, s2_s, tab_s,
    )


def solution(mesh):
    rows3 = P(("dp", "fsdp"), None, None)
    matrix = P("fsdp", None)
    vector = P("fsdp")
    return jax.shard_map(
        per_device,
        mesh=mesh,
        in_specs=(rows3, rows3, P(("dp", "fsdp"), None)) + (matrix,) * 6 + (vector,) * 10 + (rows3, rows3),
        out_specs=(rows3,) * 4 + (matrix,) * 6 + (vector,) * 10,
        check_vma=False,
    )
```

```python
import functools

import jax
import jax.numpy as jnp
from jax import lax
from jax.experimental import pallas as pl
from jax.experimental.pallas import tpu as pltpu
from jax.sharding import PartitionSpec as P

D = 768
HEADS = 12
HEAD = 64
FF = 3072
GROUP = 256
BUCKETS = 32
LEN = 512
PRED = 77
QP = 80
R = LEN + QP
f32 = jnp.float32
bf16 = jnp.bfloat16
MESH = pl.DeviceIdType.MESH
NT = (((1,), (1,)), ((), ()))
TN = (((0,), (0,)), ((), ()))

eps_norm = 1e-05
inverse_root = 0.7071067811865476
density_scale = 0.3989422804014327
bucket_edges = (12, 16, 23, 32, 46, 64, 91)
VMEM_LIMIT = 60 * 1024 * 1024
VMEM_WHOLE = pl.BlockSpec(memory_space=pltpu.VMEM)
ANYWHERE = pl.BlockSpec(memory_space=pl.ANY)


def bucket_index(relative):
    distance = jnp.abs(relative)
    coarse = 8 + sum(((distance >= boundary).astype(jnp.int32) for boundary in bucket_edges))
    within = jnp.where(distance < 8, distance, coarse)
    return within + 16 * (relative > 0).astype(jnp.int32)


def iota(shape, dim):
    return lax.broadcasted_iota(jnp.int32, shape, dim)


def ranking_column(perm_row):
    hit = perm_row == iota((LEN, LEN), 0)
    return jnp.sum(jnp.where(hit, iota((LEN, LEN), 1), 0).astype(f32), axis=1, keepdims=True)


def place():
    f = lax.axis_index("fsdp")
    return f // 4, (f // 2) % 2, f % 2, lax.axis_index("dp")


def device(z, x, c, y):
    return (y, z * 4 + x * 2 + c)


def partners():
    z, x, c, y = place()
    return [device((z + k) % 4, x, c, y) for k in (1, 2, 3)] + [
        device(z, 1 - x, c, y), device(z, x, c, 1 - y), device(z, x, 1 - c, y),
    ]


def greet():
    barrier = pltpu.get_barrier_semaphore()
    for other in partners():
        pl.semaphore_signal(barrier, inc=1, device_id=other, device_id_type=MESH)
    pl.semaphore_wait(barrier, 6)


def half_of(y, cols):
    at, size = cols
    return pl.ds(pl.multiple_of(at + y * (size // 2), 128), size // 2)


class Gather:
    def __init__(self, ref, rows, cols, send, recv, item):
        self.ref, self.rows, self.cols = ref, rows, cols
        self.send, self.recv, self.item = send, recv, item

    def copies(self, stage):
        z, x, c, y = place()
        rows = pl.ds(*self.rows)
        every = pl.ds(*self.cols)
        half = half_of(y, self.cols)

        def copy(index, part, other):
            return pltpu.make_async_remote_copy(
                src_ref=part, dst_ref=part,
                send_sem=self.send.at[self.item, index], recv_sem=self.recv.at[self.item, index],
                device_id=other, device_id_type=MESH,
            )

        ref = self.ref
        if stage == 0:
            part = ref.at[z, x, c, rows, half]
            return [copy(k - 1, part, device((z + k) % 4, x, c, y)) for k in (1, 2, 3)]
        if stage == 1:
            return [
                copy(3, ref.at[0:2, x, c, rows, half], device(z, 1 - x, c, y)),
                copy(4, ref.at[2:4, x, c, rows, half], device(z, x, c, 1 - y)),
            ]
        if stage == 2:
            return [
                copy(5, ref.at[0:2, :, c, rows, half], device(z, x, c, 1 - y)),
                copy(6, ref.at[2:4, x, c, rows, every], device(z, 1 - x, c, y)),
            ]
        return [copy(7, ref.at[:, :, c, rows, every], device(z, x, 1 - c, y))]

    def start(self, stage):
        for copy in self.copies(stage):
            copy.start()

    def arrive(self, stage):
        for copy in self.copies(stage):
            copy.wait_recv()

    def step(self, stage):
        if stage > 0:
            self.arrive(stage - 1)
        if stage < 4:
            self.start(stage)

    def drain(self):
        for stage in range(4):
            for copy in self.copies(stage):
                copy.wait_send()


def spread_vectors(raw, f):
    i = iota((256, D), 0)
    lane = iota((256, D), 1)

    def put(size, at):
        hot = jnp.where((i < size) & (lane == i + at), 1.0, 0.0).astype(bf16)
        return jnp.dot(raw, hot, preferred_element_type=f32)

    row = iota((16, D), 0)
    plain = put(D // 16, f * (D // 16))
    wide = put(192, (f % 4) * 192)
    table = put(24, f * 24)
    wide_row = jnp.sum(jnp.where(row == 8, wide, 0.0), axis=0, keepdims=True)
    return jnp.where(
        row < 8, plain, jnp.where(row == 12, table, jnp.where(row == 8 + f // 4, jnp.broadcast_to(wide_row, (16, D)), 0.0))
    )
GATHER_STEPS = {
    "g0": (-1, -1, -1, -1, -1),
    "g1": (-1, -1, -1, 3, 5),
    "g2": (-1, -1, 1, 4, 7),
    "o": (-1, 1, 3, 6, 8),
    "1a": (-1, 2, 5, 9, 12),
    "1b": (1, 4, 7, 12, 14),
    "2a": (3, 7, 11, 15, 18),
    "2b": (5, 9, 14, 20, 99),
}


def build_bias(vectors, full, near, far):
    lane = iota((16, 384), 1)
    own_head = jnp.where(lane % HEADS == iota((16, 384), 0), vectors[12:13, :384], 0.0).astype(bf16)
    rel = iota((384, 1024), 1) - 512
    onehot = (bucket_index(rel) == iota((384, 1024), 0) // HEADS).astype(bf16)
    by_rel = jnp.dot(own_head, onehot, preferred_element_type=f32)
    for h in range(HEADS):
        far[h, 0:8] = jnp.broadcast_to(by_rel[h : h + 1, 0:1], (8, 128))
        far[h, 8:16] = jnp.broadcast_to(by_rel[h : h + 1, 1023:1024], (8, 128))
        for d in range(-3, 4):
            if abs(d) >= 2:
                at = 512 + 128 * d
                block = jnp.broadcast_to(by_rel[h : h + 1, at : at + 1], (128, 128)).astype(bf16)
            else:
                base = 512 + 128 * d - 128
                row = jnp.broadcast_to(by_rel[h : h + 1, base : base + 256], (128, 256))
                tile = pltpu.roll(row, 0, 1, stride=1, stride_axis=0)[:, 128:]
                near[h, d + 1] = tile
                block = tile.astype(bf16)
            for bi in range(4):
                bj = bi + d
                if 0 <= bj < 4:
                    full[h, bi * 128 : (bi + 1) * 128, bj * 128 : (bj + 1) * 128] = block


def build_marks(s, perm_row, row_mark, key_mark, slot_hot):
    rank = ranking_column(perm_row)
    rank_row = jnp.transpose(jnp.broadcast_to(rank, (LEN, 128)))[:1]
    slot = iota((LEN, 128), 1).astype(f32) + float(LEN - PRED)
    limit = jnp.maximum(rank, float(LEN - PRED - 1))
    row_mark[s, :LEN] = jnp.where(limit < slot, 1.0, 0.0).astype(bf16)
    row_mark[s, LEN:] = jnp.where(iota((QP, 128), 0) <= iota((QP, 128), 1), 1.0, 0.0).astype(bf16)
    key_mark[s] = jnp.where(rank == slot, -1e9, 0.0).astype(bf16)
    wanted = (iota((QP, LEN), 0) + (LEN - PRED)).astype(f32)
    slot_hot[s] = (rank_row == wanted).astype(bf16)


def project_group(x, weights, vectors, g, qkv_ref):
    cols = pl.ds(pl.multiple_of(g * GROUP, 128), GROUP)
    bias_q = vectors[0:1, cols]
    bias_v = vectors[1:2, cols]
    eighth = jnp.asarray(0.125, bf16)
    rows = jnp.dot(x[:LEN], weights, preferred_element_type=f32)
    qkv_ref[0, 0, :LEN, :GROUP] = (rows[:, :GROUP] + bias_q).astype(bf16) * eighth
    qkv_ref[0, 0, :LEN, GROUP : 2 * GROUP] = rows[:, GROUP : 2 * GROUP].astype(bf16)
    qkv_ref[0, 0, :LEN, 2 * GROUP :] = (rows[:, 2 * GROUP :] + bias_v).astype(bf16)
    rows = jnp.dot(x[LEN:], weights[:, :GROUP], preferred_element_type=f32)
    qkv_ref[0, 0, LEN:, :GROUP] = (rows + bias_q).astype(bf16) * eighth


def attend_pair(s, hp, j, qkv_ref, o_ref, ol_ref, r_ref, p_ref, full, near, far, scores, row_mark, key_mark, slot_hot):
    q2 = qkv_ref[0, 0, :, pl.ds(pl.multiple_of(j * 128, 128), 128)]
    k2 = qkv_ref[0, 0, :LEN, pl.ds(pl.multiple_of(GROUP + j * 128, 128), 128)]
    v2 = qkv_ref[0, 0, :LEN, pl.ds(pl.multiple_of(2 * GROUP + j * 128, 128), 128)]
    half = iota((LEN, 128), 1) // 64
    left = jnp.concatenate([q2, row_mark[s]], axis=1)
    for h in range(2):
        right = jnp.concatenate([jnp.where(half == h, k2, jnp.zeros_like(k2)), key_mark[s]], axis=1)
        scores[h, :LEN] = lax.dot_general(left[:LEN], right, NT, preferred_element_type=f32)
        scores[h, LEN:] = lax.dot_general(left[LEN:], right, NT, preferred_element_type=f32) + jnp.dot(
            slot_hot[s], full[2 * hp + h], preferred_element_type=f32
        )
    for h in range(2):
        head = 2 * hp + h
        for bi in range(4):
            rows = slice(bi * 128, bi * 128 + 128)
            tiles = []
            for bj in range(4):
                d = bj - bi
                bias = near[head, d + 1] if abs(d) < 2 else far[head, 8:9] if d > 0 else far[head, 0:1]
                tiles.append(scores[h, rows, bj * 128 : (bj + 1) * 128] + bias)
            biased = jnp.concatenate(tiles, axis=1)
            peak = jnp.max(biased, axis=1, keepdims=True)
            p_ref[0, h, rows] = jnp.exp(biased - peak).astype(bf16)
        biased = scores[h, LEN:]
        peak = jnp.max(biased, axis=1, keepdims=True)
        p_ref[0, h, LEN:] = jnp.exp(biased - peak).astype(bf16)
    mixed = []
    for h in range(2):
        vm = jnp.where(half == h, v2, jnp.ones_like(v2))
        mixed.append(jnp.dot(p_ref[0, h], vm, preferred_element_type=f32))
    low = iota((R, 128), 1) < 64
    inverse = 1.0 / pltpu.roll(jnp.where(low, mixed[1], mixed[0]), 64, 1)
    out = jnp.where(low, mixed[0], mixed[1]) * inverse
    out_low = out.astype(bf16)
    o_ref[0] = out_low
    ol_ref[0] = (out - out_low.astype(f32)).astype(bf16)
    r_ref[0] = inverse


def forward_kernel(remote, n, *refs):
    if remote:
        (
            perm_ref, content_ref, query_ref, raw_ref, wq, wk, wv, wo, w1, w2,
            qkv_ref, o_ref, ol_ref, r_ref, p_ref, g_ref, slope_ref, unit_ref, inv_ref, a_ref,
            vec_ref, wqkv_out, wo_out, w1_out, w2_out,
            full, near, far, scores, row_mark, key_mark, slot_hot, x_all, o_all, x_sem,
            wo_all, w1_all, wqkv, own_qkv, vec_send, vec_recv, local_sem, send, recv, vec_send_sem, vec_recv_sem,
        ) = refs
    else:
        (
            perm_ref, content_ref, query_ref, vec_in, wqkv, wo_all, w1_all,
            qkv_ref, o_ref, ol_ref, r_ref, p_ref, g_ref, slope_ref, unit_ref, inv_ref, a_ref,
            full, near, far, scores, row_mark, key_mark, slot_hot, x_all, o_all, x_sem,
        ) = refs
    step = pl.program_id(0)
    g, s, j = attention_step(step, n)
    attention_steps = 6 * n
    last = attention_steps + 2 * n - 1

    def load_x():
        return [
            pltpu.make_async_copy(content_ref, x_all.at[:, :LEN], x_sem.at[0]),
            pltpu.make_async_copy(query_ref, x_all.at[:, LEN:], x_sem.at[1]),
        ]

    @pl.when(step == 0)
    def _():
        for copy in load_x():
            copy.start()

    if remote:
        z, x_at, c, y = place()
        shard = D // 16
        items = {}
        for i in range(3):
            items[f"g{i}"] = Gather(wqkv.at[i], (0, shard), (0, D), send, recv, i)
        items["o"] = Gather(wo_all, (0, shard), (0, D), send, recv, 3)
        items["1a"] = Gather(w1_all, (0, shard), (0, FF // 2), send, recv, 4)
        items["1b"] = Gather(w1_all, (0, shard), (FF // 2, FF // 2), send, recv, 5)
        items["2a"] = Gather(w2_out, (0, 96), (0, D), send, recv, 6)
        items["2b"] = Gather(w2_out, (96, 96), (0, D), send, recv, 7)
        own = []
        for part, whole, cols in (
            (wo, wo_all, (0, D)), (w1, w1_all, (0, FF // 2)), (w1, w1_all, (FF // 2, FF // 2)), (w2, w2_out, (0, D)),
        ):
            half = half_of(y, cols)
            own.append(
                pltpu.make_async_copy(part.at[:, half], whole.at[z, x_at, c, :, half], local_sem.at[len(own)])
            )

        def vec_copy(k):
            other = (
                device(z, x_at, 1 - c, y), device(z, 1 - x_at, c, y),
                *(device((z + t) % 4, x_at, c, y) for t in (1, 2, 3)),
            )[k]
            return pltpu.make_async_remote_copy(
                src_ref=vec_send.at[min(k, 2)], dst_ref=vec_recv.at[k],
                send_sem=vec_send_sem.at[k], recv_sem=vec_recv_sem.at[k], device_id=other, device_id_type=MESH,
            )

        @pl.when(step == 0)
        def _():
            greet()
            half = half_of(y, (0, D))
            for i in range(3):
                for m, part in enumerate((wq, wk, wv)):
                    own_qkv[i, :, m * GROUP : (m + 1) * GROUP] = part[:, i * GROUP : (i + 1) * GROUP]
                wqkv[i, z, x_at, c, :, half] = own_qkv[i, :, half]
            items["g0"].step(0)
            for copy in own:
                copy.start()
            vec_send[0] = spread_vectors(raw_ref[...], z * 4 + x_at * 2 + c)
            vec_copy(0).start()
            build_marks(0, perm_ref[0], row_mark, key_mark, slot_hot)
            items["g0"].step(1)
            items["g1"].step(0)
            items["g2"].step(0)
            vec_copy(0).wait_recv()
            vec_send[1] = vec_send[0] + vec_recv[0]
            vec_copy(1).start()
            items["g0"].step(2)
            for i in range(1, n):
                build_marks(i, perm_ref[i], row_mark, key_mark, slot_hot)
            vec_copy(1).wait_recv()
            vec_send[2] = vec_send[1] + vec_recv[1]
            for k in (2, 3, 4):
                vec_copy(k).start()
            items["g1"].step(1)
            for copy in own:
                copy.wait()
            items["o"].step(0)
            for k in (2, 3, 4):
                vec_copy(k).wait_recv()
            vec_ref[...] = vec_send[2] + vec_recv[2] + vec_recv[3] + vec_recv[4]
            build_bias(vec_ref[...], full, near, far)
            items["g2"].step(1)
            items["1a"].step(0)
            items["g0"].step(3)
            items["g1"].step(2)
            items["g0"].step(4)

        for at in sorted({a for steps in GATHER_STEPS.values() for a in steps if 0 <= a <= last}):

            @pl.when(step == at)
            def _(at=at):
                for stage in range(5):
                    for name, steps in GATHER_STEPS.items():
                        if steps[stage] == at:
                            items[name].step(stage)
        vectors = vec_ref
    else:
        vectors = vec_in

        @pl.when(step == 0)
        def _():
            for i in range(n):
                build_marks(i, perm_ref[i], row_mark, key_mark, slot_hot)
            build_bias(vec_in[...], full, near, far)

    @pl.when(step == 0)
    def _():
        for copy in load_x():
            copy.wait()

    @pl.when((step < attention_steps) & (j == 0))
    def _():
        weights = wqkv[g].reshape(D, D) if remote else wqkv[g]
        project_group(x_all[s], weights, vectors, g, qkv_ref)

    @pl.when(step < attention_steps)
    def _():
        attend_pair(
            s, 2 * g + j, j, qkv_ref, o_ref, ol_ref, r_ref, p_ref,
            full, near, far, scores, row_mark, key_mark, slot_hot,
        )
        o_all[s, :, pl.ds(pl.multiple_of((2 * g + j) * 128, 128), 128)] = o_ref[0]

    @pl.when(step >= attention_steps)
    def _():
        s, part = after_step(step, n)

        @pl.when(part == 0)
        def _():
            y1 = x_all[s].astype(f32) + vectors[2:3] + jnp.dot(
                o_all[s], wo_all[...].reshape(D, D), preferred_element_type=f32
            )
            unit, inv = norm_parts(y1)
            unit_ref[0] = unit
            inv_ref[0] = jnp.broadcast_to(inv, (R, 128))
            a_ref[0] = (unit * vectors[3:4] + vectors[4:5]).astype(bf16)

        weights = w1_all[:, :, :, :, pl.ds(pl.multiple_of(part * (FF // 2), 128), FF // 2)] if remote else (
            w1_all[:, pl.ds(pl.multiple_of(part * (FF // 2), 128), FF // 2)]
        )
        weights = weights.reshape(D, FF // 2)
        for i in range(2):
            cols = slice(i * D, (i + 1) * D)
            hidden = jnp.dot(a_ref[0], weights[:, cols], preferred_element_type=f32) + vectors[pl.ds(8 + 2 * part + i, 1)]
            g_ref[0, :, cols], slope_ref[0, :, cols] = gelu_parts(hidden)

    if remote:

        @pl.when(step == last)
        def _():
            back = [
                pltpu.make_async_copy(here, there, local_sem.at[i])
                for i, (here, there) in enumerate(((wqkv, wqkv_out), (wo_all, wo_out), (w1_all, w1_out)))
            ]
            for copy in back:
                copy.start()
            for stage in range(5):
                for name, steps in GATHER_STEPS.items():
                    if steps[stage] > last:
                        items[name].step(stage)
            for k in range(5):
                vec_copy(k).wait_send()
            for item in items.values():
                item.drain()
            for copy in back:
                copy.wait()


def attention_step(step, n):
    t = jnp.minimum(step, 6 * n - 1)
    return t // (2 * n), (t // 2) % n, t % 2


def after_step(step, n):
    t = jnp.maximum(step - 6 * n, 0)
    return t // 2, t % 2


def norm_parts(values):
    centered = values - jnp.mean(values, axis=-1, keepdims=True)
    inv = lax.rsqrt(jnp.mean(centered * centered, axis=-1, keepdims=True) + eps_norm)
    return centered * inv, inv


def gelu_parts(hidden):
    phi = 0.5 + 0.5 * lax.erf(hidden * inverse_root)
    bell = jnp.exp(-0.5 * hidden * hidden) * density_scale
    return (hidden * phi).astype(bf16), (phi + hidden * bell).astype(bf16)


def forward_call(n, remote, *operands):
    sds = jax.ShapeDtypeStruct

    def pair(step):
        g, s, j = attention_step(step, n)
        return (s, 0, 2 * g + j)

    def group(step):
        g, s, j = attention_step(step, n)
        return (g, s, 0, 0)

    def pair_scores(step):
        g, s, j = attention_step(step, n)
        return (s, 2 * g + j, 0, 0)

    def after(step):
        s, part = after_step(step, n)
        return (s, 0, part)

    def after_whole(step):
        return (after_step(step, n)[0], 0, 0)

    out_specs = [
        pl.BlockSpec((1, 1, R, D), group), *[pl.BlockSpec((1, R, 128), pair)] * 3,
        pl.BlockSpec((1, 2, R, LEN), pair_scores),
        *[pl.BlockSpec((1, R, FF // 2), after)] * 2,
        pl.BlockSpec((1, R, D), after_whole), pl.BlockSpec((1, R, 128), after_whole), pl.BlockSpec((1, R, D), after_whole),
    ]
    out_shape = [
        sds((3, n, R, D), bf16), sds((n, R, D), bf16), sds((n, R, D), bf16), sds((n, R, D), f32),
        sds((n, HEADS, R, LEN), bf16), sds((n, R, FF), bf16), sds((n, R, FF), bf16), sds((n, R, D), f32),
        sds((n, R, 128), f32), sds((n, R, D), bf16),
    ]
    scratch = [
        pltpu.VMEM((HEADS, LEN, LEN), bf16),
        pltpu.VMEM((HEADS, 3, 128, 128), f32),
        pltpu.VMEM((HEADS, 16, 128), f32),
        pltpu.VMEM((2, R, LEN), f32),
        pltpu.VMEM((n, R, 128), bf16),
        pltpu.VMEM((n, LEN, 128), bf16),
        pltpu.VMEM((n, QP, LEN), bf16),
        pltpu.VMEM((n, R, D), bf16),
        pltpu.VMEM((n, R, D), bf16),
        pltpu.SemaphoreType.DMA((2,)),
    ]
    if remote:
        in_specs = [VMEM_WHOLE, ANYWHERE, ANYWHERE] + [VMEM_WHOLE] * 7
        out_specs += [pl.BlockSpec((16, D), lambda step: (0, 0))] + [ANYWHERE] * 4
        block = (4, 2, 2, D // 16)
        out_shape += [
            sds((16, D), f32), sds((3, *block, D), bf16), sds((*block, D), bf16), sds((*block, FF), bf16),
            sds((4, 2, 2, FF // 16, D), bf16),
        ]
        scratch += [
            pltpu.VMEM((*block, D), bf16),
            pltpu.VMEM((*block, FF), bf16),
            pltpu.VMEM((3, *block, D), bf16),
            pltpu.VMEM((3, D // 16, D), bf16),
            pltpu.VMEM((3, 16, D), f32),
            pltpu.VMEM((5, 16, D), f32),
            pltpu.SemaphoreType.DMA((4,)),
            pltpu.SemaphoreType.DMA((8, 8)),
            pltpu.SemaphoreType.DMA((8, 8)),
            pltpu.SemaphoreType.DMA((5,)),
            pltpu.SemaphoreType.DMA((5,)),
        ]
        params = pltpu.CompilerParams(vmem_limit_bytes=VMEM_LIMIT, collective_id=1, has_side_effects=True)
    else:
        in_specs = [VMEM_WHOLE, ANYWHERE, ANYWHERE] + [VMEM_WHOLE] * 4
        params = pltpu.CompilerParams(vmem_limit_bytes=VMEM_LIMIT)
    return pl.pallas_call(
        functools.partial(forward_kernel, remote, n),
        grid=(8 * n,),
        in_specs=in_specs,
        out_specs=out_specs,
        out_shape=out_shape,
        scratch_shapes=scratch,
        compiler_params=params,
        name="attention_forward",
    )(*operands)


def norm_back(grad, unit, inv, gain):
    scaled = grad * gain
    return inv * (
        scaled - jnp.mean(scaled, axis=-1, keepdims=True) - unit * jnp.mean(scaled * unit, axis=-1, keepdims=True)
    )


def column_sum(values):
    return jnp.sum(values.astype(f32), axis=0, keepdims=True)


def middle_kernel(
    n, unit_ref, inv_ref, g_ref, slope_ref, content_cot, query_cot, vec, wo_hbm, w1_hbm, w2_hbm,
    content_out, query_out, d2_ref, dh_ref, d1_ref, do_ref, dy_ref, sums,
    wo, w1, w2, sem,
):
    s = pl.program_id(0)
    loads = [
        pltpu.make_async_copy(there, here, sem.at[i])
        for i, (there, here) in enumerate(((w2_hbm, w2), (w1_hbm, w1), (wo_hbm, wo)))
    ]

    @pl.when(s == 0)
    def _():
        for copy in loads:
            copy.start()
        sums[...] = jnp.zeros_like(sums)
        loads[0].wait()

    unit1 = unit_ref[0]
    normed = unit1 * vec[3:4] + vec[4:5]
    y2 = normed + vec[5:6] + jnp.dot(g_ref[0], w2[...], preferred_element_type=f32)
    unit2, inv2 = norm_parts(y2)
    out = (unit2 * vec[6:7] + vec[7:8]).astype(bf16)
    content_out[0] = out[:LEN]
    query_out[0] = out[LEN : LEN + PRED]
    cot = jnp.concatenate([content_cot[0], query_cot[0]], axis=0).astype(f32)
    sums[7:8] += column_sum(cot)
    sums[6:7] += column_sum(cot * unit2)
    back2 = norm_back(cot, unit2, inv2, vec[6:7])
    d2 = back2.astype(bf16)
    d2_ref[0] = d2
    sums[5:6] += column_sum(d2)

    @pl.when(s == 0)
    def _():
        loads[1].wait()
        loads[2].wait()

    da = back2
    for i in range(FF // D):
        cols = slice(i * D, (i + 1) * D)
        dg = lax.dot_general(d2, w2[cols], NT, preferred_element_type=f32)
        dh = (dg * slope_ref[0, :, cols].astype(f32)).astype(bf16)
        dh_ref[0, :, cols] = dh
        sums[8 + i : 9 + i] += column_sum(dh)
        da = da + lax.dot_general(dh, w1[:, cols], NT, preferred_element_type=f32)
    sums[4:5] += column_sum(da)
    sums[3:4] += column_sum(da * unit1)
    back1 = norm_back(da, unit1, inv_ref[0, :, :1], vec[3:4])
    dy_ref[0] = back1
    d1 = back1.astype(bf16)
    d1_ref[0] = d1
    sums[2:3] += column_sum(d1)
    do_ref[0] = lax.dot_general(d1, wo[...], NT, preferred_element_type=f32).astype(bf16)


def middle_call(n, unit1, inv1, act, slope, content_cot, query_cot, vec, wo, w1, w2):
    sds = jax.ShapeDtypeStruct

    def rows(count, width):
        return pl.BlockSpec((1, count, width), lambda s: (s, 0, 0))

    small = pl.BlockSpec((16, D), lambda s: (0, 0))
    return pl.pallas_call(
        functools.partial(middle_kernel, n),
        grid=(n,),
        in_specs=[rows(R, D), rows(R, 128), rows(R, FF), rows(R, FF), rows(LEN, D), rows(QP, D), small]
        + [ANYWHERE] * 3,
        out_specs=[rows(LEN, D), rows(PRED, D), rows(R, D), rows(R, FF), rows(R, D), rows(R, D), rows(R, D), small],
        out_shape=[
            sds((n, LEN, D), bf16), sds((n, PRED, D), bf16), sds((n, R, D), bf16), sds((n, R, FF), bf16),
            sds((n, R, D), bf16), sds((n, R, D), bf16), sds((n, R, D), f32), sds((16, D), f32),
        ],
        scratch_shapes=[
            pltpu.VMEM((D, D), bf16), pltpu.VMEM((D, FF), bf16), pltpu.VMEM((FF, D), bf16), pltpu.SemaphoreType.DMA((3,)),
        ],
        compiler_params=pltpu.CompilerParams(vmem_limit_bytes=VMEM_LIMIT),
        name="middle",
    )(unit1, inv1, act, slope, content_cot, query_cot, vec, wo, w1, w2)


def weight_kernel(n, act, dh, d2, low1, o, d1, w1_grad, w2_grad, wo_grad):
    step = pl.program_id(0)
    chunks = FF // D

    def outer(left, right):
        return lax.dot_general(
            left[...].reshape(n * R, D), right[...].reshape(n * R, D), TN, preferred_element_type=f32
        ).astype(bf16)

    @pl.when(step < chunks)
    def _():
        w2_grad[...] = outer(act, d2)

    @pl.when((step >= chunks) & (step < 2 * chunks))
    def _():
        w1_grad[...] = outer(low1, dh)

    @pl.when(step == 2 * chunks)
    def _():
        wo_grad[...] = outer(o, d1)


def weight_call(n, act, dh, d2, low1, o, d1):
    sds = jax.ShapeDtypeStruct
    chunks = FF // D

    def first(step):
        return jnp.minimum(step, chunks - 1)

    def second(step):
        return jnp.clip(step - chunks, 0, chunks - 1)

    whole = pl.BlockSpec((n, R, D), lambda step: (0, 0, 0))
    return pl.pallas_call(
        functools.partial(weight_kernel, n),
        grid=(2 * chunks + 1,),
        in_specs=[
            pl.BlockSpec((n, R, D), lambda step: (0, 0, first(step))),
            pl.BlockSpec((n, R, D), lambda step: (0, 0, second(step))),
            whole, whole, whole, whole,
        ],
        out_specs=[
            pl.BlockSpec((D, D), lambda step: (0, second(step))),
            pl.BlockSpec((D, D), lambda step: (first(step), 0)),
            pl.BlockSpec((D, D), lambda step: (0, 0)),
        ],
        out_shape=[sds((D, FF), bf16), sds((FF, D), bf16), sds((D, D), bf16)],
        compiler_params=pltpu.CompilerParams(vmem_limit_bytes=VMEM_LIMIT),
        name="weight_gradients",
    )(act, dh, d2, low1, o, d1)

REDUCE_STEPS = {
    "2a": (0, 1, 4, 6, 8, 10),
    "2b": (0, 3, 8, 10, 12, 14),
    "1a": (2, 6, 11, 13, 15, 17),
    "1b": (5, 9, 14, 16, 18, 18),
    "o": (9, 12, 16, 18, 18, 18),
    "g0": (7, 14, 18, 18, 18, 18),
    "g1": (13, 16, 18, 18, 18, 18),
    "g2": (18, 18, 18, 18, 18, 18),
}


def add(a, b):
    return (a.astype(f32) + b.astype(f32)).astype(bf16)


class Reduce:
    @staticmethod
    def scratch(rows, cols, loads):
        half = cols // 2
        shapes = [
            (4, 2, rows, cols), (2, 2, rows, half), (2, rows, cols), (2, rows, half), (2, rows, half),
            (4, rows, half), (3, rows, half),
        ]
        if loads:
            shapes.append((4, 2, rows, cols))
        return [pltpu.VMEM(shape, bf16) for shape in shapes]

    def __init__(self, source, at, rows, cols, bufs, out, send, recv, load, item):
        self.source, self.at, self.rows, self.cols = source, at, rows, cols
        self.rc, self.ry, self.rx, self.sx, self.sy, self.a3, self.rz = bufs[:7]
        self.own = bufs[7] if len(bufs) > 7 else None
        self.out, self.send, self.recv, self.load, self.item = out, send, recv, load, item

    def part(self, core):
        rows = pl.ds(self.at[0], self.rows)
        cols = pl.ds(self.at[1], self.cols)
        return self.source.at[:, :, core, rows, cols]

    def load_copy(self):
        z, x, c, y = place()
        return pltpu.make_async_copy(self.part(c), self.own, self.load)

    def copies(self, stage):
        z, x, c, y = place()
        half = self.cols // 2
        other_half = pl.ds(pl.multiple_of((1 - y) * half, 128), half)

        def copy(index, src, dst, other):
            return pltpu.make_async_remote_copy(
                src_ref=src, dst_ref=dst,
                send_sem=self.send.at[self.item, index], recv_sem=self.recv.at[self.item, index],
                device_id=other, device_id_type=MESH,
            )

        if stage == 0:
            return [copy(0, self.part(1 - c), self.rc, device(z, x, 1 - c, y))]
        if stage == 1:
            return [
                copy(1, self.rc.at[0:2, :, :, other_half], self.ry, device(z, x, c, 1 - y)),
                copy(2, self.rc.at[2:4, 1 - x], self.rx, device(z, 1 - x, c, y)),
            ]
        if stage == 2:
            return [
                copy(3, self.ry.at[:, 1 - x], self.sx, device(z, 1 - x, c, y)),
                copy(4, self.rx.at[:, :, other_half], self.sy, device(z, x, c, 1 - y)),
            ]
        if stage == 3:
            return [
                copy(4 + k, self.a3.at[(z + k) % 4], self.rz.at[k - 1], device((z + k) % 4, x, c, y))
                for k in (1, 2, 3)
            ]
        return [copy(8, self.out.at[y], self.out.at[y], device(z, x, c, 1 - y))]

    def combine(self, stage):
        z, x, c, y = place()
        half = self.cols // 2
        own_half = pl.ds(pl.multiple_of(y * half, 128), half)
        if stage == 0:
            if self.own is not None:
                self.load_copy().wait()
            for i in range(4):
                for k in range(2):
                    mine = self.own[i, k] if self.own is not None else self.source[i, k, c]
                    self.rc[i, k] = add(self.rc[i, k], mine)
        elif stage == 1:
            for i in range(2):
                for k in range(2):
                    self.ry[i, k] = add(self.ry[i, k], self.rc[i, k, :, own_half])
                self.rx[i] = add(self.rx[i], self.rc[2 + i, x])
        elif stage == 2:
            for i in range(2):
                self.a3[i] = add(self.sx[i], self.ry[i, x])
                self.a3[2 + i] = add(self.sy[i], self.rx[i, :, own_half])
        elif stage == 3:
            total = self.a3[z].astype(f32)
            for k in range(3):
                total = total + self.rz[k].astype(f32)
            self.out[y] = total.astype(bf16)

    def step(self, stage):
        if stage == 0 and self.own is not None:
            self.load_copy().start()
        if stage > 0:
            for copy in self.copies(stage - 1):
                copy.wait_recv()
            if stage < 5:
                self.combine(stage - 1)
        if stage < 5:
            for copy in self.copies(stage):
                copy.start()

    def drain(self):
        for stage in range(5):
            for copy in self.copies(stage):
                copy.wait_send()


def reduce_table(group, n, slot_cols, kept, near_sum, far_sum):
    c = iota((896, 128), 0)
    rel = jnp.where(c < 768, 128 * (c // 256 - 1) + c % 256 - 128, jnp.where(c % 128 < 64, -200, 200))
    onehot = (bucket_index(rel) == iota((896, 128), 1)).astype(f32)
    slots = jnp.concatenate([slot_cols[i] for i in range(n)], axis=1)
    sub = iota((8, 256), 0)
    lane8 = iota((8, 128), 1)
    lane1 = iota((1, 128), 1)
    rows = []
    for head in range(4):
        moved = jnp.dot(slots, kept[head], preferred_element_type=f32)
        near = [near_sum[head, d] for d in range(3)]
        far = [far_sum[head, 0:8], far_sum[head, 8:16]]
        for bi in range(4):
            for bj in range(4):
                d = bj - bi
                tile = moved[bi * 128 : (bi + 1) * 128, bj * 128 : (bj + 1) * 128]
                if abs(d) < 2:
                    near[d + 1] = near[d + 1] + tile
                else:
                    far[int(d > 0)] = far[int(d > 0)] + tile.reshape(16, 8, 128).sum(0)
        parts = []
        for d in range(3):
            high = low = None
            for a in range(16):
                x = near[d][8 * a : 8 * a + 8]
                if a:
                    x = pltpu.roll(x, 128 - 8 * a, 1)
                keep = lane8 < 128 - 8 * a
                u = jnp.where(keep, x, 0.0)
                w = jnp.where(keep, 0.0, x)
                high = u if high is None else high + u
                low = w if low is None else low + w
            y = jnp.concatenate([low, high], axis=1)
            for k in (1, 2, 4):
                y = jnp.where((sub & k) != 0, pltpu.roll(y, 256 - k, 1), y)
            parts.append(jnp.sum(y, axis=0, keepdims=True))
        parts.append(jnp.where(lane1 == 0, jnp.sum(far[0]), jnp.where(lane1 == 64, jnp.sum(far[1]), 0.0)))
        rows.append(jnp.concatenate(parts, axis=1))
    rows.append(jnp.zeros((4, 896), f32))
    return jnp.dot(
        jnp.concatenate(rows, axis=0), onehot, preferred_element_type=f32, precision=lax.Precision.HIGHEST
    )


def table_row(by_head):
    spread = (iota((128, D), 0) == iota((128, D), 1) // HEADS).astype(f32)
    wide = jnp.dot(by_head, spread, preferred_element_type=f32, precision=lax.Precision.HIGHEST)
    lane = iota((16, D), 1)
    mine = (lane % HEADS == iota((16, D), 0)) & (lane < BUCKETS * HEADS)
    return jnp.sum(jnp.where(mine, wide, 0.0), axis=0, keepdims=True)


def attend_pair_back(
    s, hp, j, qkv_ref, o_ref, ol_ref, r_ref, p_ref, do_ref, dqkv, dp, ds, kept, near_sum, far_sum
):
    q2 = qkv_ref[0, 0, :, pl.ds(pl.multiple_of(j * 128, 128), 128)]
    k2 = qkv_ref[0, 0, :LEN, pl.ds(pl.multiple_of(GROUP + j * 128, 128), 128)]
    v2 = qkv_ref[0, 0, :LEN, pl.ds(pl.multiple_of(2 * GROUP + j * 128, 128), 128)]
    delta = (do_ref[0].astype(f32) * r_ref[0]).astype(bf16)
    prod = delta.astype(f32) * (o_ref[0].astype(f32) + ol_ref[0].astype(f32))
    high = prod.astype(bf16)
    rest = pltpu.roll(prod - high.astype(f32), 64, 1).astype(bf16)
    low = iota((R, 128), 1) < 64
    half = iota((LEN, 128), 1) // 64
    extra = [jnp.where(low, high, rest), jnp.where(low, rest, high)]
    minus = jnp.full((LEN, 128), -1.0, bf16)
    for h in range(2):
        vm = jnp.where(half == h, v2, jnp.zeros_like(v2))
        dp[h] = lax.dot_general(
            jnp.concatenate([delta, extra[h]], axis=1),
            jnp.concatenate([vm, minus], axis=1),
            NT,
            preferred_element_type=f32,
        )
    for h in range(2):
        head = 2 * j + h
        far = [None, None]
        for bi in range(4):
            rows = slice(bi * 128, bi * 128 + 128)
            d_rows = p_ref[0, h, rows].astype(f32) * dp[h, rows]
            ds[h, rows] = d_rows.astype(bf16)
            for bj in range(4):
                d = bj - bi
                tile = d_rows[:, bj * 128 : (bj + 1) * 128]
                if abs(d) < 2:
                    near_sum[head, d + 1] += tile
                else:
                    part = tile.reshape(16, 8, 128).sum(0)
                    far[int(d > 0)] = part if far[int(d > 0)] is None else far[int(d > 0)] + part
        far_sum[head, 0:8] += far[0]
        far_sum[head, 8:16] += far[1]
        d_slots = (p_ref[0, h, LEN:].astype(f32) * dp[h, LEN:]).astype(bf16)
        ds[h, LEN:] = d_slots
        kept[head, pl.ds(pl.multiple_of(s * QP, 16), QP)] = d_slots
    dq = None
    for h in range(2):
        km = jnp.where(half == h, k2, jnp.zeros_like(k2))
        part = jnp.dot(ds[h], km, preferred_element_type=f32)
        dq = part if dq is None else dq + part
    dqkv[s, :, pl.ds(pl.multiple_of(j * 128, 128), 128)] = (dq * 0.125).astype(bf16)
    q_t = jnp.transpose(q2)
    delta_t = jnp.transpose(delta)
    dk_t = [jnp.dot(q_t[h * 64 : (h + 1) * 64], ds[h], preferred_element_type=f32) for h in range(2)]
    dv_t = [jnp.dot(delta_t[h * 64 : (h + 1) * 64], p_ref[0, h], preferred_element_type=f32) for h in range(2)]
    dqkv[s, :LEN, pl.ds(pl.multiple_of(GROUP + j * 128, 128), 128)] = jnp.transpose(
        jnp.concatenate(dk_t, axis=0).astype(bf16)
    )
    dqkv[s, :LEN, pl.ds(pl.multiple_of(2 * GROUP + j * 128, 128), 128)] = jnp.transpose(
        jnp.concatenate(dv_t, axis=0).astype(bf16)
    )


def backward_kernel(remote, n, *refs):
    (
        perm_ref, content_ref, query_ref, wqkv, vec_in, qkv_ref, o_ref, ol_ref, r_ref, p_ref, do_ref, dy_ref,
        *refs,
    ) = refs
    if remote:
        (
            wo_grad, w1_grad, w2_grad,
            dx_ref, vec_ref, g_out, o_out, w1_out, w2_out,
            dx, dqkv, dp, ds, kept, slot_cols, near_sum, far_sum, tab, x_all, dy_sem, x_sem,
            wqkv_grad, g_sum, o_sum, w1_sum, w2_sum, vec_send, vec_recv, load_sem, send, recv, vec_send_sem, vec_recv_sem,
            *bufs,
        ) = refs
    else:
        (
            dx_ref, vec_ref, wqkv_grad,
            dx, dqkv, dp, ds, kept, slot_cols, near_sum, far_sum, tab, x_all, dy_sem, x_sem,
        ) = refs
    g = pl.program_id(0)
    s = pl.program_id(1)
    j = pl.program_id(2)
    step = (g * n + s) * 2 + j
    last = 3 * n * 2 - 1
    loads = [
        pltpu.make_async_copy(dy_ref, dx, dy_sem),
        pltpu.make_async_copy(content_ref, x_all.at[:, :LEN], x_sem.at[0]),
        pltpu.make_async_copy(query_ref, x_all.at[:, LEN:], x_sem.at[1]),
    ]

    if remote:
        z, x_at, c, y = place()
        shard = D // 16
        wide = 2 * FF // 4

        def item(name, index, source, at, rows, cols, out):
            first = index * 8 if index < 5 else 40 + (index - 5) * 7
            take = 8 if index < 5 else 7
            return Reduce(
                source, at, rows, cols, bufs[first : first + take], out, send, recv,
                load_sem.at[index] if index < 5 else None, index,
            )

        items = {
            "2a": item("2a", 0, w2_grad, (0, 0), 96, D, w2_sum.at[0]),
            "2b": item("2b", 1, w2_grad, (96, 0), 96, D, w2_sum.at[1]),
            "1a": item("1a", 2, w1_grad, (0, 0), shard, wide, w1_sum.at[0]),
            "1b": item("1b", 3, w1_grad, (0, wide), shard, wide, w1_sum.at[1]),
            "o": item("o", 4, wo_grad, (0, 0), shard, D, o_sum),
        }
        for i in range(3):
            items[f"g{i}"] = item(f"g{i}", 5 + i, wqkv_grad.at[i], (0, 0), shard, D, g_sum.at[i])

        def vec_copy(k):
            other = (
                device(z, x_at, 1 - c, y), device(z, x_at, c, 1 - y), device(z, 1 - x_at, c, y),
                *(device((z + t) % 4, x_at, c, y) for t in (1, 2, 3)),
            )[k]
            return pltpu.make_async_remote_copy(
                src_ref=vec_send.at[min(k, 3)], dst_ref=vec_recv.at[k],
                send_sem=vec_send_sem.at[k], recv_sem=vec_recv_sem.at[k], device_id=other, device_id_type=MESH,
            )

    @pl.when(step == 0)
    def _():
        for copy in loads:
            copy.start()
        if remote:
            greet()
        vec_ref[...] = vec_in[...]
        for i in range(n):
            rank = ranking_column(perm_ref[i])
            slot_cols[i] = (rank == (iota((LEN, QP), 1) + (LEN - PRED)).astype(f32)).astype(bf16)
        dqkv[:, LEN:, GROUP:] = jnp.zeros((n, QP, 2 * GROUP), bf16)

    if remote:
        for at in sorted({a for steps in REDUCE_STEPS.values() for a in steps if a <= last}):

            @pl.when(step == at)
            def _(at=at):
                for stage in range(6):
                    for name, steps in REDUCE_STEPS.items():
                        if steps[stage] == at:
                            items[name].step(stage)

    @pl.when((s == 0) & (j == 0))
    def _():
        near_sum[...] = jnp.zeros_like(near_sum)
        far_sum[...] = jnp.zeros_like(far_sum)

    attend_pair_back(
        s, 2 * g + j, j, qkv_ref, o_ref, ol_ref, r_ref, p_ref, do_ref, dqkv, dp, ds, kept, near_sum, far_sum
    )

    @pl.when(step == 1)
    def _():
        for copy in loads:
            copy.wait()

    @pl.when((s == n - 1) & (j == 1))
    def _():
        total = lax.dot_general(
            x_all[...].reshape(n * R, D), dqkv[...].reshape(n * R, D), TN, preferred_element_type=f32
        ).astype(bf16)
        wqkv_grad[g] = total.reshape(4, 2, 2, D // 16, D) if remote else total

    if remote:

        @pl.when(step == last)
        def _():
            items["g2"].step(0)

    @pl.when(j == 1)
    def _():
        weights = wqkv[g]
        dx[s] += lax.dot_general(dqkv[s], weights, NT, preferred_element_type=f32)

    @pl.when((s == n - 1) & (j == 1))
    def _():
        tab[g] = reduce_table(g, n, slot_cols, kept, near_sum, far_sum)
        sums = jnp.sum(dqkv[0].astype(f32), axis=0, keepdims=True)
        for i in range(1, n):
            sums = sums + jnp.sum(dqkv[i].astype(f32), axis=0, keepdims=True)
        cols = pl.ds(pl.multiple_of(g * GROUP, 128), GROUP)
        vec_ref[0:1, cols] = sums[:, :GROUP]
        vec_ref[1:2, cols] = sums[:, 2 * GROUP :]

    @pl.when(step == last)
    def _():
        by_head = jnp.concatenate([tab[0, :4], tab[1, :4], tab[2, :4], jnp.zeros((4, 128), f32)], axis=0)
        vec_ref[12:13] = table_row(by_head)
        out_copy = pltpu.make_async_copy(dx, dx_ref, dy_sem)
        out_copy.start()
        if remote:
            vec_send[0] = vec_ref[...]
            vec_copy(0).start()
            tail = [(stage, name) for stage in range(6) for name in REDUCE_STEPS if REDUCE_STEPS[name][stage] > last]
            tail.remove((0, "g2"))
            order = sorted(tail, key=lambda t: t[0] - LATE[t[1]])
            done = 0
            for count, (stage, name) in enumerate(order):
                items[name].step(stage)
                if done < 3 and count >= 2 * (done + 1):
                    vec_copy(done).wait_recv()
                    vec_send[done + 1] = vec_send[done] + vec_recv[done]
                    done += 1
                    for k in (done,) if done < 3 else (3, 4, 5):
                        vec_copy(k).start()
            for k in (3, 4, 5):
                vec_copy(k).wait_recv()
            vec_ref[...] = vec_send[3] + vec_recv[3] + vec_recv[4] + vec_recv[5]
            for k in range(6):
                vec_copy(k).wait_send()
            for entry in items.values():
                entry.drain()
            g_out[...] = g_sum[...]
            o_out[...] = o_sum[...]
            w1_out[...] = w1_sum[...]
            w2_out[...] = w2_sum[...]
        out_copy.wait()


LATE = {"2a": 0, "2b": 0, "1a": 0, "1b": 0, "o": 1, "g0": 2, "g1": 3, "g2": 4}


def backward_call(n, remote, *operands):
    sds = jax.ShapeDtypeStruct
    pair = pl.BlockSpec((1, R, 128), lambda g, s, j: (s, 0, 2 * g + j))
    block = (4, 2, 2, D // 16)
    in_specs = [VMEM_WHOLE, ANYWHERE, ANYWHERE, VMEM_WHOLE, VMEM_WHOLE] + [
        pl.BlockSpec((1, 1, R, D), lambda g, s, j: (g, s, 0, 0)), pair, pair, pair,
        pl.BlockSpec((1, 2, R, LEN), lambda g, s, j: (s, 2 * g + j, 0, 0)),
        pair, ANYWHERE,
    ]
    small = pl.BlockSpec((16, D), lambda g, s, j: (0, 0))
    out_specs = [ANYWHERE, small]
    out_shape = [sds((n, R, D), f32), sds((16, D), f32)]
    scratch = [
        pltpu.VMEM((n, R, D), f32),
        pltpu.VMEM((n, R, D), bf16),
        pltpu.VMEM((2, R, LEN), f32),
        pltpu.VMEM((2, R, LEN), bf16),
        pltpu.VMEM((4, n * QP, LEN), bf16),
        pltpu.VMEM((n, LEN, QP), bf16),
        pltpu.VMEM((4, 3, 128, 128), f32),
        pltpu.VMEM((4, 16, 128), f32),
        pltpu.VMEM((3, 8, 128), f32),
        pltpu.VMEM((n, R, D), bf16),
        pltpu.SemaphoreType.DMA,
        pltpu.SemaphoreType.DMA((2,)),
    ]
    if remote:
        in_specs += [ANYWHERE] * 3
        out_specs += [VMEM_WHOLE] * 4
        shard = D // 16
        out_shape += [
            sds((3, 2, shard, D // 2), bf16), sds((2, shard, D // 2), bf16), sds((2, 2, shard, FF // 4), bf16),
            sds((2, 2, 96, D // 2), bf16),
        ]
        scratch += [
            pltpu.VMEM((3, *block, D), bf16),
            *(pltpu.VMEM(a.shape, bf16) for a in out_shape[2:]),
            pltpu.VMEM((4, 16, D), f32),
            pltpu.VMEM((6, 16, D), f32),
            pltpu.SemaphoreType.DMA((5,)),
            pltpu.SemaphoreType.DMA((8, 9)),
            pltpu.SemaphoreType.DMA((8, 9)),
            pltpu.SemaphoreType.DMA((6,)),
            pltpu.SemaphoreType.DMA((6,)),
        ]
        for rows, cols in ((96, D), (96, D), (shard, FF // 2), (shard, FF // 2), (shard, D)):
            scratch += Reduce.scratch(rows, cols, True)
        for _ in range(3):
            scratch += Reduce.scratch(shard, D, False)
        params = pltpu.CompilerParams(vmem_limit_bytes=VMEM_LIMIT, collective_id=2, has_side_effects=True)
    else:
        out_specs += [pl.BlockSpec(memory_space=pltpu.VMEM)]
        out_shape += [sds((3, D, D), bf16)]
        params = pltpu.CompilerParams(vmem_limit_bytes=VMEM_LIMIT)
    return pl.pallas_call(
        functools.partial(backward_kernel, remote, n),
        grid=(3, n, 2),
        in_specs=in_specs,
        out_specs=out_specs,
        out_shape=out_shape,
        scratch_shapes=scratch,
        compiler_params=params,
        name="attention_backward",
    )(*operands)


def output_kernel(dx_ref, vec, g_sum, o_sum, w1_sum, w2_sum, content, query, wq, wk, wv, wo, w1, w2, *vectors):
    content[0] = dx_ref[0, :LEN]
    query[0] = dx_ref[0, LEN : LEN + PRED]

    @pl.when(pl.program_id(0) == 0)
    def _():
        for m, out in enumerate((wq, wk, wv)):
            for g in range(3):
                for k in range(2):
                    at = m * 2 + k
                    out[:, g * GROUP + k * 128 : g * GROUP + (k + 1) * 128] = g_sum[
                        g, at // 3, :, (at % 3) * 128 : (at % 3 + 1) * 128
                    ].astype(f32)
        for k in range(2):
            wo[:, k * D // 2 : (k + 1) * D // 2] = o_sum[k].astype(f32)
            for i in range(2):
                at = i * (FF // 2) + k * (FF // 4)
                w1[:, at : at + FF // 4] = w1_sum[i, k].astype(f32)
                w2[i * 96 : (i + 1) * 96, k * D // 2 : (k + 1) * D // 2] = w2_sum[i, k].astype(f32)
        f = lax.axis_index("fsdp")
        lane = iota((D, 256), 0)
        i = iota((D, 256), 1)

        def take(rows, size, at):
            hot = jnp.where((i < size) & (lane == i + at), 1.0, 0.0)
            return jnp.dot(rows, hot, preferred_element_type=f32, precision=lax.Precision.HIGHEST)

        plain = take(vec[0:8], D // 16, f * (D // 16))
        wide = jnp.sum(jnp.where(iota((16, D), 0) == 8 + f // 4, vec[...], 0.0), axis=0, keepdims=True)
        wide = take(jnp.broadcast_to(wide, (8, D)), 192, (f % 4) * 192)
        table = take(jnp.broadcast_to(vec[12:13], (8, D)), 24, f * 24)
        rows = [plain[r : r + 1] for r in range(8)] + [wide[:1], table[:1]]
        for out, row in zip(vectors, rows):
            out[...] = row[0, : out.shape[0]]


def output_call(n, dx, vec, g_sum, o_sum, w1_sum, w2_sum, sizes):
    sds = jax.ShapeDtypeStruct

    def rows(count):
        return pl.BlockSpec((1, count, D), lambda s: (s, 0, 0))

    shard = D // 16
    return pl.pallas_call(
        output_kernel,
        grid=(n,),
        in_specs=[rows(R)] + [VMEM_WHOLE] * 5,
        out_specs=[rows(LEN), rows(PRED)] + [VMEM_WHOLE] * (6 + len(sizes)),
        out_shape=[sds((n, LEN, D), f32), sds((n, PRED, D), f32)]
        + [sds((shard, D), f32)] * 4
        + [sds((shard, FF), f32), sds((FF // 16, D), f32)]
        + [sds((size,), f32) for size in sizes],
        compiler_params=pltpu.CompilerParams(vmem_limit_bytes=VMEM_LIMIT),
        name="outputs",
    )(dx, vec, g_sum, o_sum, w1_sum, w2_sum)
def pieces(own_vectors, places):
    return sum(jnp.pad(v[None], ((at, 15 - at), (0, 256 - v.shape[0]))) for at, v in zip(places, own_vectors))


ROWS = (0, 1, 2, 3, 4, 5, 6, 7, 8, 12)


def per_device(
    content_in, query_in, permutation,
    query_weight, key_weight, value_weight, output_weight, inner_weight, outer_weight,
    query_bias, value_bias, output_bias, first_gain, first_shift, inner_bias, outer_bias,
    second_gain, second_shift, bias_table,
    content_cotangent, query_cotangent,
):
    n = content_in.shape[0]
    n_f = lax.axis_size("fsdp")
    remote = n_f == 16 and lax.axis_size("dp") == 2 and n == 3
    vectors = (
        query_bias, value_bias, output_bias, first_gain, first_shift, outer_bias, second_gain, second_shift,
        inner_bias, bias_table,
    )
    sizes = [a.shape[0] for a in vectors]
    pad = ((0, 0), (0, QP - PRED), (0, 0))
    perm = permutation[:, None]
    queries = jnp.pad(query_in, pad)
    query_cot = jnp.pad(query_cotangent, pad)
    if remote:
        qkv, o, ol, r, p, act, slope, unit1, inv1, low1, vec, wqkv, wo, w1, w2 = forward_call(
            n, True, perm, content_in, queries, pieces(vectors, ROWS),
            query_weight, key_weight, value_weight, output_weight, inner_weight, outer_weight,
        )
        wqkv = wqkv.reshape(3, D, D)
        wo, w1, w2 = wo.reshape(D, D), w1.reshape(D, FF), w2.reshape(FF, D)
    else:
        packed = lax.all_gather(jnp.concatenate(vectors), "fsdp", axis=0)
        rows = []
        at = 0
        for size in sizes:
            whole = packed[:, at : at + size].reshape(-1).astype(f32)
            rows.append(jnp.pad(whole, (0, -whole.shape[0] % D)).reshape(-1, D))
            at += size
        vec = jnp.concatenate(rows + [jnp.zeros((3, D), f32)], axis=0)
        whole = lax.all_gather(
            jnp.concatenate([query_weight, key_weight, value_weight, output_weight, inner_weight], axis=1),
            "fsdp", axis=0, tiled=True,
        )
        wqkv = jnp.stack(
            [
                jnp.concatenate([whole[:, m * D + g * GROUP : m * D + (g + 1) * GROUP] for m in range(3)], axis=1)
                for g in range(3)
            ]
        )
        wo, w1 = whole[:, 3 * D : 4 * D], whole[:, 4 * D :]
        w2 = lax.all_gather(outer_weight, "fsdp", axis=0, tiled=True)
        qkv, o, ol, r, p, act, slope, unit1, inv1, low1 = forward_call(
            n, False, perm, content_in, queries, vec, wqkv, wo, w1
        )

    content_out, query_out, d2, dh, d1, do, dy, sums = middle_call(
        n, unit1, inv1, act, slope, content_cotangent, query_cot, vec, wo, w1, w2
    )
    w1_grad, w2_grad, wo_grad = weight_call(n, act, dh, d2, low1, o, d1)

    if remote:
        block = (4, 2, 2)
        dx, sums, g_sum, o_sum, w1_sum, w2_sum = backward_call(
            n, True, perm, content_in, queries, wqkv, sums, qkv, o, ol, r, p, do, dy,
            wo_grad.reshape(*block, D // 16, D), w1_grad.reshape(*block, D // 16, FF),
            w2_grad.reshape(*block, FF // 16, D),
        )
        content_grad, query_grad, wq_s, wk_s, wv_s, wo_s, w1_s, w2_s, *shares = output_call(
            n, dx, sums, g_sum, o_sum, w1_sum, w2_sum, sizes
        )
    else:
        dx, sums, wqkv_grad = backward_call(
            n, False, perm, content_in, queries, wqkv, sums, qkv, o, ol, r, p, do, dy
        )
        content_grad, query_grad = dx[:, :LEN], dx[:, LEN : LEN + PRED]

        def scatter(a):
            return lax.psum_scatter(a, "fsdp", scatter_dimension=0, tiled=True)

        flat = jnp.concatenate(
            [wqkv_grad[g, :, m * GROUP : (m + 1) * GROUP] for m in range(3) for g in range(3)] + [wo_grad, w1_grad],
            axis=1,
        )
        whole_rows = [sums[i] for i in range(8)] + [sums[8:12].reshape(-1), sums[12, : BUCKETS * HEADS]]
        packed = jnp.concatenate([v.reshape(n_f, -1) for v in whole_rows], axis=1)
        totals = lax.psum((scatter(flat), scatter(w2_grad), scatter(packed).astype(bf16)), "dp")
        flat, w2_s, packed = (a.astype(f32) for a in totals)
        wq_s, wk_s, wv_s, wo_s = (flat[:, m * D : (m + 1) * D] for m in range(4))
        w1_s = flat[:, 4 * D :]
        shares = []
        at = 0
        for size in sizes:
            shares.append(packed[0, at : at + size])
            at += size
    bq_s, bv_s, bo_s, g1_s, s1_s, b2_s, g2_s, s2_s, b1_s, tab_s = shares
    return (
        content_out, query_out, content_grad, query_grad,
        wq_s, wk_s, wv_s, wo_s, w1_s, w2_s,
        bq_s, bv_s, bo_s, g1_s, s1_s, b1_s, b2_s, g2_s, s2_s, tab_s,
    )


def solution(mesh):
    rows3 = P(("dp", "fsdp"), None, None)
    matrix = P("fsdp", None)
    vector = P("fsdp")
    return jax.shard_map(
        per_device,
        mesh=mesh,
        in_specs=(rows3, rows3, P(("dp", "fsdp"), None)) + (matrix,) * 6 + (vector,) * 10 + (rows3, rows3),
        out_specs=(rows3,) * 4 + (matrix,) * 6 + (vector,) * 10,
        check_vma=False,
    )
```

```python
import functools

import jax
import jax.numpy as jnp
from jax import lax
from jax.experimental import pallas as pl
from jax.experimental.pallas import tpu as pltpu
from jax.sharding import PartitionSpec as P

D = 768
HEADS = 12
HEAD = 64
FF = 3072
GROUP = 256
BUCKETS = 32
LEN = 512
PRED = 77
QP = 80
R = LEN + QP
f32 = jnp.float32
bf16 = jnp.bfloat16
MESH = pl.DeviceIdType.MESH
NT = (((1,), (1,)), ((), ()))
TN = (((0,), (0,)), ((), ()))

eps_norm = 1e-05
inverse_root = 0.7071067811865476
density_scale = 0.3989422804014327
bucket_edges = (12, 16, 23, 32, 46, 64, 91)
VMEM_LIMIT = 60 * 1024 * 1024
VMEM_WHOLE = pl.BlockSpec(memory_space=pltpu.VMEM)
ANYWHERE = pl.BlockSpec(memory_space=pl.ANY)


def bucket_index(relative):
    distance = jnp.abs(relative)
    coarse = 8 + sum(((distance >= boundary).astype(jnp.int32) for boundary in bucket_edges))
    within = jnp.where(distance < 8, distance, coarse)
    return within + 16 * (relative > 0).astype(jnp.int32)


def iota(shape, dim):
    return lax.broadcasted_iota(jnp.int32, shape, dim)


def ranking_column(perm_row):
    hit = perm_row == iota((LEN, LEN), 0)
    return jnp.sum(jnp.where(hit, iota((LEN, LEN), 1), 0).astype(f32), axis=1, keepdims=True)


def place():
    f = lax.axis_index("fsdp")
    return f // 4, (f // 2) % 2, f % 2, lax.axis_index("dp")


def device(z, x, c, y):
    return (y, z * 4 + x * 2 + c)


def partners():
    z, x, c, y = place()
    return [device((z + k) % 4, x, c, y) for k in (1, 2, 3)] + [
        device(z, 1 - x, c, y), device(z, x, c, 1 - y), device(z, x, 1 - c, y),
        device(z, 1 - x, c, 1 - y), device(z, 1 - x, 1 - c, y),
    ]


def greet():
    barrier = pltpu.get_barrier_semaphore()
    for other in partners():
        pl.semaphore_signal(barrier, inc=1, device_id=other, device_id_type=MESH)
    pl.semaphore_wait(barrier, 8)


def half_of(y, cols):
    at, size = cols
    return pl.ds(pl.multiple_of(at + y * (size // 2), 128), size // 2)


class Gather:
    def __init__(self, ref, rows, cols, send, recv, item):
        self.ref, self.rows, self.cols = ref, rows, cols
        self.send, self.recv, self.item = send, recv, item

    def copies(self, stage):
        z, x, c, y = place()
        rows = pl.ds(*self.rows)
        every = pl.ds(*self.cols)
        half = half_of(y, self.cols)

        def copy(index, part, other):
            return pltpu.make_async_remote_copy(
                src_ref=part, dst_ref=part,
                send_sem=self.send.at[self.item, index], recv_sem=self.recv.at[self.item, index],
                device_id=other, device_id_type=MESH,
            )

        ref = self.ref
        if stage == 0:
            part = ref.at[z, x, c, rows, half]
            return [copy(k - 1, part, device((z + k) % 4, x, c, y)) for k in (1, 2, 3)]
        if stage == 1:
            return [
                copy(3, ref.at[0:2, x, c, rows, half], device(z, 1 - x, c, y)),
                copy(4, ref.at[2:4, x, c, rows, half], device(z, x, c, 1 - y)),
            ]
        if stage == 2:
            return [
                copy(5, ref.at[0:2, :, c, rows, half], device(z, x, c, 1 - y)),
                copy(6, ref.at[2:4, x, c, rows, every], device(z, 1 - x, c, y)),
            ]
        return [copy(7, ref.at[:, :, c, rows, every], device(z, x, 1 - c, y))]

    def start(self, stage):
        for copy in self.copies(stage):
            copy.start()

    def arrive(self, stage):
        for copy in self.copies(stage):
            copy.wait_recv()

    def step(self, stage):
        if stage > 0:
            self.arrive(stage - 1)
        if stage < 4:
            self.start(stage)

    def drain(self):
        for stage in range(4):
            for copy in self.copies(stage):
                copy.wait_send()


def spread_vectors(raw, f):
    i = iota((256, D), 0)
    lane = iota((256, D), 1)

    def put(size, at):
        hot = jnp.where((i < size) & (lane == i + at), 1.0, 0.0).astype(bf16)
        return jnp.dot(raw, hot, preferred_element_type=f32)

    row = iota((16, D), 0)
    plain = put(D // 16, f * (D // 16))
    wide = put(192, (f % 4) * 192)
    table = put(24, f * 24)
    wide_row = jnp.sum(jnp.where(row == 8, wide, 0.0), axis=0, keepdims=True)
    return jnp.where(
        row < 8, plain, jnp.where(row == 12, table, jnp.where(row == 8 + f // 4, jnp.broadcast_to(wide_row, (16, D)), 0.0))
    )
GATHER_STEPS = {
    "g0": (-1, -1, -1, -1, -1),
    "g1": (-1, -1, -1, 3, 6),
    "g2": (-1, -1, 2, 6, 9),
    "o": (-1, 2, 5, 8, 10),
    "1a": (-1, 3, 7, 12, 15),
    "1b": (1, 5, 10, 15, 17),
    "2a": (3, 8, 13, 18, 20),
    "2b": (6, 11, 16, 21, 99),
}


def build_bias(vectors, full, near, far):
    lane = iota((16, 384), 1)
    own_head = jnp.where(lane % HEADS == iota((16, 384), 0), vectors[12:13, :384], 0.0).astype(bf16)
    rel = iota((384, 1024), 1) - 512
    onehot = (bucket_index(rel) == iota((384, 1024), 0) // HEADS).astype(bf16)
    by_rel = jnp.dot(own_head, onehot, preferred_element_type=f32)
    for h in range(HEADS):
        far[h, 0:8] = jnp.broadcast_to(by_rel[h : h + 1, 0:1], (8, 128))
        far[h, 8:16] = jnp.broadcast_to(by_rel[h : h + 1, 1023:1024], (8, 128))
        for d in range(-3, 4):
            if abs(d) >= 2:
                at = 512 + 128 * d
                block = jnp.broadcast_to(by_rel[h : h + 1, at : at + 1], (128, 128)).astype(bf16)
            else:
                base = 512 + 128 * d - 128
                row = jnp.broadcast_to(by_rel[h : h + 1, base : base + 256], (128, 256))
                tile = pltpu.roll(row, 0, 1, stride=1, stride_axis=0)[:, 128:]
                near[h, d + 1] = tile
                block = tile.astype(bf16)
            for bi in range(4):
                bj = bi + d
                if 0 <= bj < 4:
                    full[h, bi * 128 : (bi + 1) * 128, bj * 128 : (bj + 1) * 128] = block


def build_marks(s, perm_row, row_mark, key_mark, slot_hot):
    rank = ranking_column(perm_row)
    rank_row = jnp.transpose(jnp.broadcast_to(rank, (LEN, 128)))[:1]
    slot = iota((LEN, 128), 1).astype(f32) + float(LEN - PRED)
    limit = jnp.maximum(rank, float(LEN - PRED - 1))
    row_mark[s, :LEN] = jnp.where(limit < slot, 1.0, 0.0).astype(bf16)
    row_mark[s, LEN:] = jnp.where(iota((QP, 128), 0) <= iota((QP, 128), 1), 1.0, 0.0).astype(bf16)
    key_mark[s] = jnp.where(rank == slot, -1e9, 0.0).astype(bf16)
    wanted = (iota((QP, LEN), 0) + (LEN - PRED)).astype(f32)
    slot_hot[s] = (rank_row == wanted).astype(bf16)


def project_group(x, weights, vectors, g, qkv_ref):
    cols = pl.ds(pl.multiple_of(g * GROUP, 128), GROUP)
    bias_q = vectors[0:1, cols]
    bias_v = vectors[1:2, cols]
    eighth = jnp.asarray(0.125, bf16)
    rows = jnp.dot(x[:LEN], weights, preferred_element_type=f32)
    qkv_ref[0, 0, :LEN, :GROUP] = (rows[:, :GROUP] + bias_q).astype(bf16) * eighth
    qkv_ref[0, 0, :LEN, GROUP : 2 * GROUP] = rows[:, GROUP : 2 * GROUP].astype(bf16)
    qkv_ref[0, 0, :LEN, 2 * GROUP :] = (rows[:, 2 * GROUP :] + bias_v).astype(bf16)
    rows = jnp.dot(x[LEN:], weights[:, :GROUP], preferred_element_type=f32)
    qkv_ref[0, 0, LEN:, :GROUP] = (rows + bias_q).astype(bf16) * eighth


def attend_pair(s, hp, j, qkv_ref, o_ref, ol_ref, r_ref, p_ref, full, near, far, scores, row_mark, key_mark, slot_hot):
    q2 = qkv_ref[0, 0, :, pl.ds(pl.multiple_of(j * 128, 128), 128)]
    k2 = qkv_ref[0, 0, :LEN, pl.ds(pl.multiple_of(GROUP + j * 128, 128), 128)]
    v2 = qkv_ref[0, 0, :LEN, pl.ds(pl.multiple_of(2 * GROUP + j * 128, 128), 128)]
    half = iota((LEN, 128), 1) // 64
    left = jnp.concatenate([q2, row_mark[s]], axis=1)
    for h in range(2):
        right = jnp.concatenate([jnp.where(half == h, k2, jnp.zeros_like(k2)), key_mark[s]], axis=1)
        scores[h, :LEN] = lax.dot_general(left[:LEN], right, NT, preferred_element_type=f32)
        scores[h, LEN:] = lax.dot_general(left[LEN:], right, NT, preferred_element_type=f32) + jnp.dot(
            slot_hot[s], full[2 * hp + h], preferred_element_type=f32
        )
    for h in range(2):
        head = 2 * hp + h
        for bi in range(4):
            rows = slice(bi * 128, bi * 128 + 128)
            tiles = []
            for bj in range(4):
                d = bj - bi
                bias = near[head, d + 1] if abs(d) < 2 else far[head, 8:9] if d > 0 else far[head, 0:1]
                tiles.append(scores[h, rows, bj * 128 : (bj + 1) * 128] + bias)
            biased = jnp.concatenate(tiles, axis=1)
            peak = jnp.max(biased, axis=1, keepdims=True)
            p_ref[0, h, rows] = jnp.exp(biased - peak).astype(bf16)
        biased = scores[h, LEN:]
        peak = jnp.max(biased, axis=1, keepdims=True)
        p_ref[0, h, LEN:] = jnp.exp(biased - peak).astype(bf16)
    mixed = []
    for h in range(2):
        vm = jnp.where(half == h, v2, jnp.ones_like(v2))
        mixed.append(jnp.dot(p_ref[0, h], vm, preferred_element_type=f32))
    low = iota((R, 128), 1) < 64
    inverse = 1.0 / pltpu.roll(jnp.where(low, mixed[1], mixed[0]), 64, 1)
    out = jnp.where(low, mixed[0], mixed[1]) * inverse
    out_low = out.astype(bf16)
    o_ref[0] = out_low
    ol_ref[0] = (out - out_low.astype(f32)).astype(bf16)
    r_ref[0] = inverse


def forward_kernel(remote, n, *refs):
    if remote:
        (
            perm_ref, content_ref, query_ref, raw_ref, wq, wk, wv, wo, w1, w2,
            qkv_ref, o_ref, ol_ref, r_ref, p_ref, g_ref, slope_ref, unit_ref, inv_ref, a_ref,
            vec_ref, wqkv_out, wo_out, w1_out, w2_out,
            full, near, far, scores, row_mark, key_mark, slot_hot, x_all, o_all, low_all, x_sem,
            wo_all, w1_all, wqkv, own_qkv, vec_send, vec_recv, local_sem, send, recv, vec_send_sem, vec_recv_sem,
        ) = refs
    else:
        (
            perm_ref, content_ref, query_ref, vec_in, wqkv, wo_all, w1_all,
            qkv_ref, o_ref, ol_ref, r_ref, p_ref, g_ref, slope_ref, unit_ref, inv_ref, a_ref,
            full, near, far, scores, row_mark, key_mark, slot_hot, x_all, o_all, low_all, x_sem,
        ) = refs
    step = pl.program_id(0)
    g, s, j = attention_step(step, n)
    attention_steps = 6 * n
    last = attention_steps + 2 * n - 1

    x_load = pltpu.make_async_copy(content_ref, x_all.at[:, :LEN], x_sem)

    @pl.when(step == 0)
    def _():
        x_load.start()
        place_queries(n, query_ref, x_all)

    if remote:
        z, x_at, c, y = place()
        shard = D // 16
        items = {}
        for i in range(3):
            items[f"g{i}"] = Gather(wqkv.at[i], (0, shard), (0, D), send, recv, i)
        items["o"] = Gather(wo_all, (0, shard), (0, D), send, recv, 3)
        items["1a"] = Gather(w1_all, (0, shard), (0, FF // 2), send, recv, 4)
        items["1b"] = Gather(w1_all, (0, shard), (FF // 2, FF // 2), send, recv, 5)
        items["2a"] = Gather(w2_out, (0, 96), (0, D), send, recv, 6)
        items["2b"] = Gather(w2_out, (96, 96), (0, D), send, recv, 7)
        own = []
        for part, whole, cols in (
            (wo, wo_all, (0, D)), (w1, w1_all, (0, FF // 2)), (w1, w1_all, (FF // 2, FF // 2)), (w2, w2_out, (0, D)),
        ):
            half = half_of(y, cols)
            own.append(
                pltpu.make_async_copy(part.at[:, half], whole.at[z, x_at, c, :, half], local_sem.at[len(own)])
            )

        def vec_copy(k):
            other = (
                device(z, x_at, 1 - c, y), device(z, 1 - x_at, c, y), device(z, 1 - x_at, 1 - c, y),
                *(device((z + t) % 4, x_at, c, y) for t in (1, 2, 3)),
            )[k]
            return pltpu.make_async_remote_copy(
                src_ref=vec_send.at[k // 3], dst_ref=vec_recv.at[k],
                send_sem=vec_send_sem.at[k], recv_sem=vec_recv_sem.at[k], device_id=other, device_id_type=MESH,
            )

        @pl.when(step == 0)
        def _():
            greet()
            half = half_of(y, (0, D))
            for i in range(3):
                for m, part in enumerate((wq, wk, wv)):
                    own_qkv[i, :, m * GROUP : (m + 1) * GROUP] = part[:, i * GROUP : (i + 1) * GROUP]
                wqkv[i, z, x_at, c, :, half] = own_qkv[i, :, half]
            items["g0"].step(0)
            for copy in own:
                copy.start()
            vec_send[0] = spread_vectors(raw_ref[...], z * 4 + x_at * 2 + c)
            for k in (0, 1, 2):
                vec_copy(k).start()
            build_marks(0, perm_ref[0:1], row_mark, key_mark, slot_hot)
            items["g0"].step(1)
            items["g1"].step(0)
            items["g2"].step(0)
            for k in (0, 1, 2):
                vec_copy(k).wait_recv()
            vec_send[1] = vec_send[0] + vec_recv[0] + vec_recv[1] + vec_recv[2]
            for k in (3, 4, 5):
                vec_copy(k).start()
            items["g0"].step(2)
            for i in range(1, n):
                build_marks(i, perm_ref[i : i + 1], row_mark, key_mark, slot_hot)
            items["g1"].step(1)
            for copy in own:
                copy.wait()
            items["o"].step(0)
            for k in (3, 4, 5):
                vec_copy(k).wait_recv()
            vec_ref[...] = vec_send[1] + vec_recv[3] + vec_recv[4] + vec_recv[5]
            items["g0"].step(3)
            build_bias(vec_ref[...], full, near, far)
            items["g2"].step(1)
            items["1a"].step(0)
            items["g1"].step(2)
            items["g0"].step(4)

        back = [
            pltpu.make_async_copy(here, there, local_sem.at[i])
            for i, (here, there) in enumerate(((wqkv, wqkv_out), (wo_all, wo_out), (w1_all, w1_out)))
        ]

        @pl.when(step == attention_steps)
        def _():
            for copy in back:
                copy.start()

        for at in sorted({a for steps in GATHER_STEPS.values() for a in steps if 0 <= a <= last}):

            @pl.when(step == at)
            def _(at=at):
                for stage in range(5):
                    for name, steps in GATHER_STEPS.items():
                        if steps[stage] == at:
                            items[name].step(stage)
        vectors = vec_ref
    else:
        vectors = vec_in

        @pl.when(step == 0)
        def _():
            for i in range(n):
                build_marks(i, perm_ref[i : i + 1], row_mark, key_mark, slot_hot)
            build_bias(vec_in[...], full, near, far)

    @pl.when(step == 0)
    def _():
        x_load.wait()

    @pl.when((step < attention_steps) & (j == 0))
    def _():
        weights = wqkv[g].reshape(D, D) if remote else wqkv[g]
        project_group(x_all[s], weights, vectors, g, qkv_ref)

    @pl.when(step < attention_steps)
    def _():
        attend_pair(
            s, 2 * g + j, j, qkv_ref, o_ref, ol_ref, r_ref, p_ref,
            full, near, far, scores, row_mark, key_mark, slot_hot,
        )
        o_all[s, :, pl.ds(pl.multiple_of((2 * g + j) * 128, 128), 128)] = o_ref[0]

    def before_ffn(s):
        y1 = x_all[s].astype(f32) + vectors[2:3] + jnp.dot(
            o_all[s], wo_all[...].reshape(D, D), preferred_element_type=f32
        )
        unit, inv = norm_parts(y1)
        unit_ref[0] = unit
        inv_ref[0] = jnp.broadcast_to(inv, (R, 128))
        low = (unit * vectors[3:4] + vectors[4:5]).astype(bf16)
        a_ref[0] = low
        low_all[s % 2] = low

    def first_ffn(s, part):
        for i in range(2):
            cols = slice(i * D, (i + 1) * D)
            at = (2 * part + i) * D
            weights = w1_all[:, :, :, :, at : at + D].reshape(D, D) if remote else w1_all[:, at : at + D]
            hidden = jnp.dot(low_all[s % 2], weights, preferred_element_type=f32)
            hidden = hidden + vectors[8 + 2 * part + i : 9 + 2 * part + i]
            g_ref[0, :, cols], slope_ref[0, :, cols] = gelu_parts(hidden)

    @pl.when(step == attention_steps - 1)
    def _():
        before_ffn(0)

    for after in range(n):

        @pl.when(step == attention_steps + 2 * after)
        def _(after=after):
            first_ffn(after, 0)

        @pl.when(step == attention_steps + 2 * after + 1)
        def _(after=after):
            first_ffn(after, 1)
            if after < n - 1:
                before_ffn(after + 1)

    if remote:

        @pl.when(step == last)
        def _():
            for stage in range(5):
                for name, steps in GATHER_STEPS.items():
                    if steps[stage] > last:
                        items[name].step(stage)
            for k in range(6):
                vec_copy(k).wait_send()
            for item in items.values():
                item.drain()
            for copy in back:
                copy.wait()


def place_queries(n, query_ref, x_all):
    x_all[:, R - 16 :] = jnp.zeros((n, 16, D), bf16)
    for i in range(n):
        x_all[i, LEN : LEN + PRED] = query_ref[i]


def attention_step(step, n):
    t = jnp.minimum(step, 6 * n - 1)
    return t // (2 * n), (t // 2) % n, t % 2


def after_step(step, n):
    t = jnp.maximum(step - 6 * n, 0)
    return t // 2, t % 2


def norm_parts(values):
    centered = values - jnp.mean(values, axis=-1, keepdims=True)
    inv = lax.rsqrt(jnp.mean(centered * centered, axis=-1, keepdims=True) + eps_norm)
    return centered * inv, inv


def gelu_parts(hidden):
    phi = 0.5 + 0.5 * lax.erf(hidden * inverse_root)
    bell = jnp.exp(-0.5 * hidden * hidden) * density_scale
    return (hidden * phi).astype(bf16), (phi + hidden * bell).astype(bf16)


def forward_call(n, remote, *operands):
    sds = jax.ShapeDtypeStruct

    def pair(step):
        g, s, j = attention_step(step, n)
        return (s, 0, 2 * g + j)

    def group(step):
        g, s, j = attention_step(step, n)
        return (g, s, 0, 0)

    def pair_scores(step):
        g, s, j = attention_step(step, n)
        return (s, 2 * g + j, 0, 0)

    def after(step):
        s, part = after_step(step, n)
        return (s, 0, part)

    def after_whole(step):
        return (jnp.clip((step - 6 * n + 1) // 2, 0, n - 1), 0, 0)

    out_specs = [
        pl.BlockSpec((1, 1, R, D), group), *[pl.BlockSpec((1, R, 128), pair)] * 3,
        pl.BlockSpec((1, 2, R, LEN), pair_scores),
        *[pl.BlockSpec((1, R, FF // 2), after)] * 2,
        pl.BlockSpec((1, R, D), after_whole), pl.BlockSpec((1, R, 128), after_whole), pl.BlockSpec((1, R, D), after_whole),
    ]
    out_shape = [
        sds((3, n, R, D), bf16), sds((n, R, D), bf16), sds((n, R, D), bf16), sds((n, R, D), f32),
        sds((n, HEADS, R, LEN), bf16), sds((n, R, FF), bf16), sds((n, R, FF), bf16), sds((n, R, D), f32),
        sds((n, R, 128), f32), sds((n, R, D), bf16),
    ]
    scratch = [
        pltpu.VMEM((HEADS, LEN, LEN), bf16),
        pltpu.VMEM((HEADS, 3, 128, 128), f32),
        pltpu.VMEM((HEADS, 16, 128), f32),
        pltpu.VMEM((2, R, LEN), f32),
        pltpu.VMEM((n, R, 128), bf16),
        pltpu.VMEM((n, LEN, 128), bf16),
        pltpu.VMEM((n, QP, LEN), bf16),
        pltpu.VMEM((n, R, D), bf16),
        pltpu.VMEM((n, R, D), bf16),
        pltpu.VMEM((2, R, D), bf16),
        pltpu.SemaphoreType.DMA,
    ]
    if remote:
        in_specs = [VMEM_WHOLE, ANYWHERE] + [VMEM_WHOLE] * 8
        out_specs += [pl.BlockSpec((16, D), lambda step: (0, 0))] + [ANYWHERE] * 4
        block = (4, 2, 2, D // 16)
        out_shape += [
            sds((16, D), f32), sds((3, *block, D), bf16), sds((*block, D), bf16), sds((*block, FF), bf16),
            sds((4, 2, 2, FF // 16, D), bf16),
        ]
        scratch += [
            pltpu.VMEM((*block, D), bf16),
            pltpu.VMEM((*block, FF), bf16),
            pltpu.VMEM((3, *block, D), bf16),
            pltpu.VMEM((3, D // 16, D), bf16),
            pltpu.VMEM((2, 16, D), f32),
            pltpu.VMEM((6, 16, D), f32),
            pltpu.SemaphoreType.DMA((4,)),
            pltpu.SemaphoreType.DMA((8, 8)),
            pltpu.SemaphoreType.DMA((8, 8)),
            pltpu.SemaphoreType.DMA((6,)),
            pltpu.SemaphoreType.DMA((6,)),
        ]
        params = pltpu.CompilerParams(vmem_limit_bytes=VMEM_LIMIT, collective_id=1, has_side_effects=True)
    else:
        in_specs = [VMEM_WHOLE, ANYWHERE] + [VMEM_WHOLE] * 5
        params = pltpu.CompilerParams(vmem_limit_bytes=VMEM_LIMIT)
    return pl.pallas_call(
        functools.partial(forward_kernel, remote, n),
        grid=(8 * n,),
        in_specs=in_specs,
        out_specs=out_specs,
        out_shape=out_shape,
        scratch_shapes=scratch,
        compiler_params=params,
        name="attention_forward",
    )(*operands)


def norm_back(grad, unit, inv, gain):
    scaled = grad * gain
    return inv * (
        scaled - jnp.mean(scaled, axis=-1, keepdims=True) - unit * jnp.mean(scaled * unit, axis=-1, keepdims=True)
    )


def column_sum(values):
    return jnp.sum(values.astype(f32), axis=0, keepdims=True)


def middle_kernel(
    n, unit_ref, inv_ref, g_ref, slope_ref, content_cot, query_cot, vec, wo_hbm, w1_hbm, w2_hbm,
    content_out, query_out, d2_ref, dh_ref, d1_ref, do_ref, dy_ref, sums,
    wo, w1, w2, padded, sem,
):
    s = pl.program_id(0)
    loads = [
        pltpu.make_async_copy(there, here, sem.at[i])
        for i, (there, here) in enumerate(((w2_hbm, w2), (w1_hbm, w1), (wo_hbm, wo)))
    ]

    @pl.when(s == 0)
    def _():
        for copy in loads:
            copy.start()
        sums[...] = jnp.zeros_like(sums)
        padded[PRED - PRED % 8 :] = jnp.zeros((QP - PRED + PRED % 8, D), f32)
        loads[0].wait()

    padded[:PRED] = query_cot[0].astype(f32)
    unit1 = unit_ref[0]
    normed = unit1 * vec[3:4] + vec[4:5]
    y2 = normed + vec[5:6] + jnp.dot(g_ref[0], w2[...], preferred_element_type=f32)
    unit2, inv2 = norm_parts(y2)
    out = (unit2 * vec[6:7] + vec[7:8]).astype(bf16)
    content_out[0] = out[:LEN]
    query_out[0] = out[LEN : LEN + PRED]
    cot = jnp.concatenate([content_cot[0].astype(f32), padded[...]], axis=0)
    sums[7:8] += column_sum(cot)
    sums[6:7] += column_sum(cot * unit2)
    back2 = norm_back(cot, unit2, inv2, vec[6:7])
    d2 = back2.astype(bf16)
    d2_ref[0] = d2
    sums[5:6] += column_sum(d2)

    @pl.when(s == 0)
    def _():
        loads[1].wait()
        loads[2].wait()

    da = back2
    for i in range(FF // D):
        cols = slice(i * D, (i + 1) * D)
        dg = lax.dot_general(d2, w2[cols], NT, preferred_element_type=f32)
        dh = (dg * slope_ref[0, :, cols].astype(f32)).astype(bf16)
        dh_ref[0, :, cols] = dh
        sums[8 + i : 9 + i] += column_sum(dh)
        da = da + lax.dot_general(dh, w1[:, cols], NT, preferred_element_type=f32)
    sums[4:5] += column_sum(da)
    sums[3:4] += column_sum(da * unit1)
    back1 = norm_back(da, unit1, inv_ref[0, :, :1], vec[3:4])
    dy_ref[0] = back1
    d1 = back1.astype(bf16)
    d1_ref[0] = d1
    sums[2:3] += column_sum(d1)
    do_ref[0] = lax.dot_general(d1, wo[...], NT, preferred_element_type=f32).astype(bf16)


def middle_call(n, unit1, inv1, act, slope, content_cot, query_cot, vec, wo, w1, w2):
    sds = jax.ShapeDtypeStruct

    def rows(count, width):
        return pl.BlockSpec((1, count, width), lambda s: (s, 0, 0))

    small = pl.BlockSpec((16, D), lambda s: (0, 0))
    return pl.pallas_call(
        functools.partial(middle_kernel, n),
        grid=(n,),
        in_specs=[rows(R, D), rows(R, 128), rows(R, FF), rows(R, FF), rows(LEN, D), rows(PRED, D), small]
        + [ANYWHERE] * 3,
        out_specs=[rows(LEN, D), rows(PRED, D), rows(R, D), rows(R, FF), rows(R, D), rows(R, D), rows(R, D), small],
        out_shape=[
            sds((n, LEN, D), bf16), sds((n, PRED, D), bf16), sds((n, R, D), bf16), sds((n, R, FF), bf16),
            sds((n, R, D), bf16), sds((n, R, D), bf16), sds((n, R, D), f32), sds((16, D), f32),
        ],
        scratch_shapes=[
            pltpu.VMEM((D, D), bf16), pltpu.VMEM((D, FF), bf16), pltpu.VMEM((FF, D), bf16),
            pltpu.VMEM((QP, D), f32), pltpu.SemaphoreType.DMA((3,)),
        ],
        compiler_params=pltpu.CompilerParams(vmem_limit_bytes=VMEM_LIMIT),
        name="middle",
    )(unit1, inv1, act, slope, content_cot, query_cot, vec, wo, w1, w2)


def weight_kernel(n, act, dh, d2, low1, o, d1, w1_grad, w2_grad, wo_grad):
    step = pl.program_id(0)
    chunks = FF // D

    def outer(left, right):
        return lax.dot_general(
            left[...].reshape(n * R, D), right[...].reshape(n * R, D), TN, preferred_element_type=f32
        ).astype(bf16)

    @pl.when(step < chunks)
    def _():
        w2_grad[...] = outer(act, d2)

    @pl.when((step >= chunks) & (step < 2 * chunks))
    def _():
        w1_grad[...] = outer(low1, dh)

    @pl.when(step == 2 * chunks)
    def _():
        wo_grad[...] = outer(o, d1)


def weight_call(n, act, dh, d2, low1, o, d1):
    sds = jax.ShapeDtypeStruct
    chunks = FF // D

    def first(step):
        return jnp.minimum(step, chunks - 1)

    def second(step):
        return jnp.clip(step - chunks, 0, chunks - 1)

    whole = pl.BlockSpec((n, R, D), lambda step: (0, 0, 0))
    return pl.pallas_call(
        functools.partial(weight_kernel, n),
        grid=(2 * chunks + 1,),
        in_specs=[
            pl.BlockSpec((n, R, D), lambda step: (0, 0, first(step))),
            pl.BlockSpec((n, R, D), lambda step: (0, 0, second(step))),
            whole, whole, whole, whole,
        ],
        out_specs=[
            pl.BlockSpec((D, D), lambda step: (0, second(step))),
            pl.BlockSpec((D, D), lambda step: (first(step), 0)),
            pl.BlockSpec((D, D), lambda step: (0, 0)),
        ],
        out_shape=[sds((D, FF), bf16), sds((FF, D), bf16), sds((D, D), bf16)],
        compiler_params=pltpu.CompilerParams(vmem_limit_bytes=VMEM_LIMIT),
        name="weight_gradients",
    )(act, dh, d2, low1, o, d1)

REDUCE_STEPS = {
    "2a": (0, 1, 5, 8, 12, 15),
    "2b": (0, 3, 7, 10, 14, 17),
    "1a": (2, 6, 10, 13, 17, 18),
    "1b": (4, 9, 13, 16, 18, 18),
    "o": (7, 11, 15, 17, 18, 18),
    "g0": (8, 13, 16, 18, 18, 18),
    "g1": (13, 15, 17, 18, 18, 18),
    "g2": (18, 18, 18, 18, 18, 18),
}


def add(a, b):
    return (a.astype(f32) + b.astype(f32)).astype(bf16)


class Reduce:
    @staticmethod
    def scratch(rows, cols, loads):
        half = cols // 2
        shapes = [
            (4, 2, rows, cols), (2, 2, rows, half), (2, rows, cols), (2, rows, half), (2, rows, half),
            (4, rows, half), (3, rows, half),
        ]
        if loads:
            shapes.append((4, 2, rows, cols))
        return [pltpu.VMEM(shape, bf16) for shape in shapes]

    def __init__(self, source, at, rows, cols, bufs, out, send, recv, load, item):
        self.source, self.at, self.rows, self.cols = source, at, rows, cols
        self.rc, self.ry, self.rx, self.sx, self.sy, self.a3, self.rz = bufs[:7]
        self.own = bufs[7] if len(bufs) > 7 else None
        self.out, self.send, self.recv, self.load, self.item = out, send, recv, load, item

    def part(self, core):
        rows = pl.ds(self.at[0], self.rows)
        cols = pl.ds(self.at[1], self.cols)
        return self.source.at[:, :, core, rows, cols]

    def load_copy(self):
        z, x, c, y = place()
        return pltpu.make_async_copy(self.part(c), self.own, self.load)

    def copies(self, stage):
        z, x, c, y = place()
        half = self.cols // 2
        other_half = pl.ds(pl.multiple_of((1 - y) * half, 128), half)

        def copy(index, src, dst, other):
            return pltpu.make_async_remote_copy(
                src_ref=src, dst_ref=dst,
                send_sem=self.send.at[self.item, index], recv_sem=self.recv.at[self.item, index],
                device_id=other, device_id_type=MESH,
            )

        if stage == 0:
            return [copy(0, self.part(1 - c), self.rc, device(z, x, 1 - c, y))]
        if stage == 1:
            return [
                copy(1, self.rc.at[0:2, :, :, other_half], self.ry, device(z, x, c, 1 - y)),
                copy(2, self.rc.at[2:4, 1 - x], self.rx, device(z, 1 - x, c, y)),
            ]
        if stage == 2:
            return [
                copy(3, self.ry.at[:, 1 - x], self.sx, device(z, 1 - x, c, y)),
                copy(4, self.rx.at[:, :, other_half], self.sy, device(z, x, c, 1 - y)),
            ]
        if stage == 3:
            return [
                copy(4 + k, self.a3.at[(z + k) % 4], self.rz.at[k - 1], device((z + k) % 4, x, c, y))
                for k in (1, 2, 3)
            ]
        return [copy(8, self.out.at[y], self.out.at[y], device(z, x, c, 1 - y))]

    def combine(self, stage):
        z, x, c, y = place()
        half = self.cols // 2
        own_half = pl.ds(pl.multiple_of(y * half, 128), half)
        if stage == 0:
            if self.own is not None:
                self.load_copy().wait()
            for i in range(4):
                for k in range(2):
                    mine = self.own[i, k] if self.own is not None else self.source[i, k, c]
                    self.rc[i, k] = add(self.rc[i, k], mine)
        elif stage == 1:
            for i in range(2):
                for k in range(2):
                    self.ry[i, k] = add(self.ry[i, k], self.rc[i, k, :, own_half])
                self.rx[i] = add(self.rx[i], self.rc[2 + i, x])
        elif stage == 2:
            for i in range(2):
                self.a3[i] = add(self.sx[i], self.ry[i, x])
                self.a3[2 + i] = add(self.sy[i], self.rx[i, :, own_half])
        elif stage == 3:
            total = self.a3[z].astype(f32)
            for k in range(3):
                total = total + self.rz[k].astype(f32)
            self.out[y] = total.astype(bf16)

    def step(self, stage):
        if stage == 0 and self.own is not None:
            self.load_copy().start()
        if stage > 0:
            for copy in self.copies(stage - 1):
                copy.wait_recv()
            if stage < 5:
                self.combine(stage - 1)
        if stage < 5:
            for copy in self.copies(stage):
                copy.start()

    def drain(self):
        for stage in range(5):
            for copy in self.copies(stage):
                copy.wait_send()


def reduce_table(group, n, slot_cols, kept, near_sum, far_sum):
    c = iota((896, 128), 0)
    rel = jnp.where(c < 768, 128 * (c // 256 - 1) + c % 256 - 128, jnp.where(c % 128 < 64, -200, 200))
    onehot = (bucket_index(rel) == iota((896, 128), 1)).astype(f32)
    slots = jnp.concatenate([slot_cols[i] for i in range(n)], axis=1)
    sub = iota((8, 256), 0)
    lane8 = iota((8, 128), 1)
    lane1 = iota((1, 128), 1)
    rows = []
    for head in range(4):
        moved = jnp.dot(slots, kept[head], preferred_element_type=f32)
        near = [near_sum[head, d] for d in range(3)]
        far = [far_sum[head, 0:8], far_sum[head, 8:16]]
        for bi in range(4):
            for bj in range(4):
                d = bj - bi
                tile = moved[bi * 128 : (bi + 1) * 128, bj * 128 : (bj + 1) * 128]
                if abs(d) < 2:
                    near[d + 1] = near[d + 1] + tile
                else:
                    far[int(d > 0)] = far[int(d > 0)] + tile.reshape(16, 8, 128).sum(0)
        parts = []
        for d in range(3):
            high = low = None
            for a in range(16):
                x = near[d][8 * a : 8 * a + 8]
                if a:
                    x = pltpu.roll(x, 128 - 8 * a, 1)
                keep = lane8 < 128 - 8 * a
                u = jnp.where(keep, x, 0.0)
                w = jnp.where(keep, 0.0, x)
                high = u if high is None else high + u
                low = w if low is None else low + w
            y = jnp.concatenate([low, high], axis=1)
            for k in (1, 2, 4):
                y = jnp.where((sub & k) != 0, pltpu.roll(y, 256 - k, 1), y)
            parts.append(jnp.sum(y, axis=0, keepdims=True))
        parts.append(jnp.where(lane1 == 0, jnp.sum(far[0]), jnp.where(lane1 == 64, jnp.sum(far[1]), 0.0)))
        rows.append(jnp.concatenate(parts, axis=1))
    rows.append(jnp.zeros((4, 896), f32))
    return jnp.dot(
        jnp.concatenate(rows, axis=0), onehot, preferred_element_type=f32, precision=lax.Precision.HIGHEST
    )


def table_row(by_head):
    spread = (iota((128, D), 0) == iota((128, D), 1) // HEADS).astype(f32)
    wide = jnp.dot(by_head, spread, preferred_element_type=f32, precision=lax.Precision.HIGHEST)
    lane = iota((16, D), 1)
    mine = (lane % HEADS == iota((16, D), 0)) & (lane < BUCKETS * HEADS)
    return jnp.sum(jnp.where(mine, wide, 0.0), axis=0, keepdims=True)


def attend_pair_back(
    s, hp, j, qkv_ref, o_ref, ol_ref, r_ref, p_ref, do_ref, dqkv, dp, ds, kept, near_sum, far_sum
):
    q2 = qkv_ref[0, 0, :, pl.ds(pl.multiple_of(j * 128, 128), 128)]
    k2 = qkv_ref[0, 0, :LEN, pl.ds(pl.multiple_of(GROUP + j * 128, 128), 128)]
    v2 = qkv_ref[0, 0, :LEN, pl.ds(pl.multiple_of(2 * GROUP + j * 128, 128), 128)]
    delta = (do_ref[0].astype(f32) * r_ref[0]).astype(bf16)
    prod = delta.astype(f32) * (o_ref[0].astype(f32) + ol_ref[0].astype(f32))
    high = prod.astype(bf16)
    rest = pltpu.roll(prod - high.astype(f32), 64, 1).astype(bf16)
    low = iota((R, 128), 1) < 64
    half = iota((LEN, 128), 1) // 64
    extra = [jnp.where(low, high, rest), jnp.where(low, rest, high)]
    minus = jnp.full((LEN, 128), -1.0, bf16)
    for h in range(2):
        vm = jnp.where(half == h, v2, jnp.zeros_like(v2))
        dp[h] = lax.dot_general(
            jnp.concatenate([delta, extra[h]], axis=1),
            jnp.concatenate([vm, minus], axis=1),
            NT,
            preferred_element_type=f32,
        )
    for h in range(2):
        head = 2 * j + h
        far = [None, None]
        for bi in range(4):
            rows = slice(bi * 128, bi * 128 + 128)
            d_rows = p_ref[0, h, rows].astype(f32) * dp[h, rows]
            ds[h, rows] = d_rows.astype(bf16)
            for bj in range(4):
                d = bj - bi
                tile = d_rows[:, bj * 128 : (bj + 1) * 128]
                if abs(d) < 2:
                    near_sum[head, d + 1] += tile
                else:
                    part = tile.reshape(16, 8, 128).sum(0)
                    far[int(d > 0)] = part if far[int(d > 0)] is None else far[int(d > 0)] + part
        far_sum[head, 0:8] += far[0]
        far_sum[head, 8:16] += far[1]
        d_slots = (p_ref[0, h, LEN:].astype(f32) * dp[h, LEN:]).astype(bf16)
        ds[h, LEN:] = d_slots
        kept[head, pl.ds(pl.multiple_of(s * QP, 16), QP)] = d_slots
    dq = None
    for h in range(2):
        km = jnp.where(half == h, k2, jnp.zeros_like(k2))
        part = jnp.dot(ds[h], km, preferred_element_type=f32)
        dq = part if dq is None else dq + part
    dqkv[s, :, pl.ds(pl.multiple_of(j * 128, 128), 128)] = (dq * 0.125).astype(bf16)
    q_t = jnp.transpose(q2)
    delta_t = jnp.transpose(delta)
    dk_t = [jnp.dot(q_t[h * 64 : (h + 1) * 64], ds[h], preferred_element_type=f32) for h in range(2)]
    dv_t = [jnp.dot(delta_t[h * 64 : (h + 1) * 64], p_ref[0, h], preferred_element_type=f32) for h in range(2)]
    dqkv[s, :LEN, pl.ds(pl.multiple_of(GROUP + j * 128, 128), 128)] = jnp.transpose(
        jnp.concatenate(dk_t, axis=0).astype(bf16)
    )
    dqkv[s, :LEN, pl.ds(pl.multiple_of(2 * GROUP + j * 128, 128), 128)] = jnp.transpose(
        jnp.concatenate(dv_t, axis=0).astype(bf16)
    )


def backward_kernel(remote, n, *refs):
    (
        perm_ref, content_ref, query_ref, wqkv, vec_in, qkv_ref, o_ref, ol_ref, r_ref, p_ref, do_ref, dy_ref,
        *refs,
    ) = refs
    if remote:
        (
            wo_grad, w1_grad, w2_grad,
            dx_ref, vec_ref, g_out, o_out, w1_out, w2_out,
            dx, dqkv, dp, ds, kept, slot_cols, near_sum, far_sum, tab, x_all, dy_sem, x_sem,
            wqkv_grad, g_sum, o_sum, w1_sum, w2_sum, vec_send, vec_recv, load_sem, send, recv, vec_send_sem, vec_recv_sem,
            *bufs,
        ) = refs
    else:
        (
            dx_ref, vec_ref, wqkv_grad,
            dx, dqkv, dp, ds, kept, slot_cols, near_sum, far_sum, tab, x_all, dy_sem, x_sem,
        ) = refs
    g = pl.program_id(0)
    s = pl.program_id(1)
    j = pl.program_id(2)
    step = (g * n + s) * 2 + j
    last = 3 * n * 2 - 1
    loads = [
        pltpu.make_async_copy(dy_ref, dx, dy_sem),
        pltpu.make_async_copy(content_ref, x_all.at[:, :LEN], x_sem),
    ]

    if remote:
        z, x_at, c, y = place()
        shard = D // 16
        wide = 2 * FF // 4

        def item(name, index, source, at, rows, cols, out):
            first = index * 8 if index < 5 else 40 + (index - 5) * 7
            take = 8 if index < 5 else 7
            return Reduce(
                source, at, rows, cols, bufs[first : first + take], out, send, recv,
                load_sem.at[index] if index < 5 else None, index,
            )

        items = {
            "2a": item("2a", 0, w2_grad, (0, 0), 96, D, w2_sum.at[0]),
            "2b": item("2b", 1, w2_grad, (96, 0), 96, D, w2_sum.at[1]),
            "1a": item("1a", 2, w1_grad, (0, 0), shard, wide, w1_sum.at[0]),
            "1b": item("1b", 3, w1_grad, (0, wide), shard, wide, w1_sum.at[1]),
            "o": item("o", 4, wo_grad, (0, 0), shard, D, o_sum),
        }
        for i in range(3):
            items[f"g{i}"] = item(f"g{i}", 5 + i, wqkv_grad.at[i], (0, 0), shard, D, g_sum.at[i])

        def vec_copy(k):
            other = (
                device(z, x_at, 1 - c, y),
                device(z, x_at, c, 1 - y), device(z, 1 - x_at, c, y), device(z, 1 - x_at, c, 1 - y),
                *(device((z + t) % 4, x_at, c, y) for t in (1, 2, 3)),
            )[k]
            return pltpu.make_async_remote_copy(
                src_ref=vec_send.at[0 if k == 0 else 1 if k < 4 else 2], dst_ref=vec_recv.at[k],
                send_sem=vec_send_sem.at[k], recv_sem=vec_recv_sem.at[k], device_id=other, device_id_type=MESH,
            )

    @pl.when(step == 0)
    def _():
        for copy in loads:
            copy.start()
        if remote:
            greet()
        place_queries(n, query_ref, x_all)
        vec_ref[...] = vec_in[...]
        for i in range(n):
            rank = ranking_column(perm_ref[i : i + 1])
            slot_cols[i] = (rank == (iota((LEN, QP), 1) + (LEN - PRED)).astype(f32)).astype(bf16)
        dqkv[:, LEN:, GROUP:] = jnp.zeros((n, QP, 2 * GROUP), bf16)

    if remote:
        for at in sorted({a for steps in REDUCE_STEPS.values() for a in steps if a <= last}):

            @pl.when(step == at)
            def _(at=at):
                for stage in range(6):
                    for name, steps in REDUCE_STEPS.items():
                        if steps[stage] == at:
                            items[name].step(stage)

    @pl.when((s == 0) & (j == 0))
    def _():
        near_sum[...] = jnp.zeros_like(near_sum)
        far_sum[...] = jnp.zeros_like(far_sum)

    attend_pair_back(
        s, 2 * g + j, j, qkv_ref, o_ref, ol_ref, r_ref, p_ref, do_ref, dqkv, dp, ds, kept, near_sum, far_sum
    )

    @pl.when(step == 1)
    def _():
        for copy in loads:
            copy.wait()

    @pl.when((s == n - 1) & (j == 1))
    def _():
        total = lax.dot_general(
            x_all[...].reshape(n * R, D), dqkv[...].reshape(n * R, D), TN, preferred_element_type=f32
        ).astype(bf16)
        wqkv_grad[g] = total.reshape(4, 2, 2, D // 16, D) if remote else total

    if remote:

        @pl.when(step == last)
        def _():
            items["g2"].step(0)

    @pl.when(j == 1)
    def _():
        weights = wqkv[g]
        dx[s] += lax.dot_general(dqkv[s], weights, NT, preferred_element_type=f32)

    @pl.when((s == n - 1) & (j == 1))
    def _():
        tab[g] = reduce_table(g, n, slot_cols, kept, near_sum, far_sum)
        sums = jnp.sum(dqkv[0].astype(f32), axis=0, keepdims=True)
        for i in range(1, n):
            sums = sums + jnp.sum(dqkv[i].astype(f32), axis=0, keepdims=True)
        cols = pl.ds(pl.multiple_of(g * GROUP, 128), GROUP)
        vec_ref[0:1, cols] = sums[:, :GROUP]
        vec_ref[1:2, cols] = sums[:, 2 * GROUP :]

    @pl.when(step == last)
    def _():
        by_head = jnp.concatenate([tab[0, :4], tab[1, :4], tab[2, :4], jnp.zeros((4, 128), f32)], axis=0)
        vec_ref[12:13] = table_row(by_head)
        out_copy = pltpu.make_async_copy(dx, dx_ref, dy_sem)
        out_copy.start()
        if remote:
            vec_send[0] = vec_ref[...]
            vec_copy(0).start()
            tail = [(stage, name) for stage in range(6) for name in REDUCE_STEPS if REDUCE_STEPS[name][stage] > last]
            tail.remove((0, "g2"))
            order = sorted(tail, key=lambda t: t[0] - LATE[t[1]])
            for stage, name in order:
                items[name].step(stage)
                if name == "g2" and stage == 1:
                    vec_copy(0).wait_recv()
                    vec_send[1] = vec_send[0] + vec_recv[0]
                    for k in (1, 2, 3):
                        vec_copy(k).start()
                if name == "g2" and stage == 2:
                    for k in (1, 2, 3):
                        vec_copy(k).wait_recv()
                    vec_send[2] = vec_send[1] + vec_recv[1] + vec_recv[2] + vec_recv[3]
                    for k in (4, 5, 6):
                        vec_copy(k).start()
            for k in (4, 5, 6):
                vec_copy(k).wait_recv()
            vec_ref[...] = vec_send[2] + vec_recv[4] + vec_recv[5] + vec_recv[6]
            for k in range(7):
                vec_copy(k).wait_send()
            for entry in items.values():
                entry.drain()
            g_out[...] = g_sum[...]
            o_out[...] = o_sum[...]
            w1_out[...] = w1_sum[...]
            w2_out[...] = w2_sum[...]
        out_copy.wait()


LATE = {"2a": 0, "2b": 0, "1a": 3.8, "1b": 2.5, "o": 2.4, "g0": 1.6, "g1": 1.5, "g2": 0}


def backward_call(n, remote, *operands):
    sds = jax.ShapeDtypeStruct
    pair = pl.BlockSpec((1, R, 128), lambda g, s, j: (s, 0, 2 * g + j))
    block = (4, 2, 2, D // 16)
    in_specs = [VMEM_WHOLE, ANYWHERE, VMEM_WHOLE, VMEM_WHOLE, VMEM_WHOLE] + [
        pl.BlockSpec((1, 1, R, D), lambda g, s, j: (g, s, 0, 0)), pair, pair, pair,
        pl.BlockSpec((1, 2, R, LEN), lambda g, s, j: (s, 2 * g + j, 0, 0)),
        pair, ANYWHERE,
    ]
    small = pl.BlockSpec((16, D), lambda g, s, j: (0, 0))
    out_specs = [ANYWHERE, small]
    out_shape = [sds((n, R, D), f32), sds((16, D), f32)]
    scratch = [
        pltpu.VMEM((n, R, D), f32),
        pltpu.VMEM((n, R, D), bf16),
        pltpu.VMEM((2, R, LEN), f32),
        pltpu.VMEM((2, R, LEN), bf16),
        pltpu.VMEM((4, n * QP, LEN), bf16),
        pltpu.VMEM((n, LEN, QP), bf16),
        pltpu.VMEM((4, 3, 128, 128), f32),
        pltpu.VMEM((4, 16, 128), f32),
        pltpu.VMEM((3, 8, 128), f32),
        pltpu.VMEM((n, R, D), bf16),
        pltpu.SemaphoreType.DMA,
        pltpu.SemaphoreType.DMA,
    ]
    if remote:
        in_specs += [ANYWHERE] * 3
        out_specs += [VMEM_WHOLE] * 4
        shard = D // 16
        out_shape += [
            sds((3, 2, shard, D // 2), bf16), sds((2, shard, D // 2), bf16), sds((2, 2, shard, FF // 4), bf16),
            sds((2, 2, 96, D // 2), bf16),
        ]
        scratch += [
            pltpu.VMEM((3, *block, D), bf16),
            *(pltpu.VMEM(a.shape, bf16) for a in out_shape[2:]),
            pltpu.VMEM((3, 16, D), f32),
            pltpu.VMEM((7, 16, D), f32),
            pltpu.SemaphoreType.DMA((5,)),
            pltpu.SemaphoreType.DMA((8, 9)),
            pltpu.SemaphoreType.DMA((8, 9)),
            pltpu.SemaphoreType.DMA((7,)),
            pltpu.SemaphoreType.DMA((7,)),
        ]
        for rows, cols in ((96, D), (96, D), (shard, FF // 2), (shard, FF // 2), (shard, D)):
            scratch += Reduce.scratch(rows, cols, True)
        for _ in range(3):
            scratch += Reduce.scratch(shard, D, False)
        params = pltpu.CompilerParams(vmem_limit_bytes=VMEM_LIMIT, collective_id=2, has_side_effects=True)
    else:
        out_specs += [pl.BlockSpec(memory_space=pltpu.VMEM)]
        out_shape += [sds((3, D, D), bf16)]
        params = pltpu.CompilerParams(vmem_limit_bytes=VMEM_LIMIT)
    return pl.pallas_call(
        functools.partial(backward_kernel, remote, n),
        grid=(3, n, 2),
        in_specs=in_specs,
        out_specs=out_specs,
        out_shape=out_shape,
        scratch_shapes=scratch,
        compiler_params=params,
        name="attention_backward",
    )(*operands)


def output_kernel(dx_ref, vec, g_sum, o_sum, w1_sum, w2_sum, content, query, wq, wk, wv, wo, w1, w2, *vectors):
    content[0] = dx_ref[0, :LEN]
    query[0] = dx_ref[0, LEN : LEN + PRED]

    @pl.when(pl.program_id(0) == 0)
    def _():
        for m, out in enumerate((wq, wk, wv)):
            for g in range(3):
                for k in range(2):
                    at = m * 2 + k
                    out[:, g * GROUP + k * 128 : g * GROUP + (k + 1) * 128] = g_sum[
                        g, at // 3, :, (at % 3) * 128 : (at % 3 + 1) * 128
                    ].astype(f32)
        for k in range(2):
            wo[:, k * D // 2 : (k + 1) * D // 2] = o_sum[k].astype(f32)
            for i in range(2):
                at = i * (FF // 2) + k * (FF // 4)
                w1[:, at : at + FF // 4] = w1_sum[i, k].astype(f32)
                w2[i * 96 : (i + 1) * 96, k * D // 2 : (k + 1) * D // 2] = w2_sum[i, k].astype(f32)
        f = lax.axis_index("fsdp")
        lane = iota((D, 256), 0)
        i = iota((D, 256), 1)

        def take(rows, size, at):
            hot = jnp.where((i < size) & (lane == i + at), 1.0, 0.0)
            return jnp.dot(rows, hot, preferred_element_type=f32, precision=lax.Precision.HIGHEST)

        plain = take(vec[0:8], D // 16, f * (D // 16))
        wide = jnp.sum(jnp.where(iota((16, D), 0) == 8 + f // 4, vec[...], 0.0), axis=0, keepdims=True)
        wide = take(jnp.broadcast_to(wide, (8, D)), 192, (f % 4) * 192)
        table = take(jnp.broadcast_to(vec[12:13], (8, D)), 24, f * 24)
        rows = [plain[r : r + 1] for r in range(8)] + [wide[:1], table[:1]]
        for out, row in zip(vectors, rows):
            out[...] = row[0, : out.shape[0]]


def output_call(n, dx, vec, g_sum, o_sum, w1_sum, w2_sum, sizes):
    sds = jax.ShapeDtypeStruct

    def rows(count):
        return pl.BlockSpec((1, count, D), lambda s: (s, 0, 0))

    shard = D // 16
    return pl.pallas_call(
        output_kernel,
        grid=(n,),
        in_specs=[rows(R)] + [VMEM_WHOLE] * 5,
        out_specs=[rows(LEN), rows(PRED)] + [VMEM_WHOLE] * (6 + len(sizes)),
        out_shape=[sds((n, LEN, D), f32), sds((n, PRED, D), f32)]
        + [sds((shard, D), f32)] * 4
        + [sds((shard, FF), f32), sds((FF // 16, D), f32)]
        + [sds((size,), f32) for size in sizes],
        compiler_params=pltpu.CompilerParams(vmem_limit_bytes=VMEM_LIMIT),
        name="outputs",
    )(dx, vec, g_sum, o_sum, w1_sum, w2_sum)
def pieces(own_vectors, places):
    return sum(jnp.pad(v[None], ((at, 15 - at), (0, 256 - v.shape[0]))) for at, v in zip(places, own_vectors))


ROWS = (0, 1, 2, 3, 4, 5, 6, 7, 8, 12)


def per_device(
    content_in, query_in, permutation,
    query_weight, key_weight, value_weight, output_weight, inner_weight, outer_weight,
    query_bias, value_bias, output_bias, first_gain, first_shift, inner_bias, outer_bias,
    second_gain, second_shift, bias_table,
    content_cotangent, query_cotangent,
):
    n = content_in.shape[0]
    n_f = lax.axis_size("fsdp")
    remote = n_f == 16 and lax.axis_size("dp") == 2 and n == 3
    vectors = (
        query_bias, value_bias, output_bias, first_gain, first_shift, outer_bias, second_gain, second_shift,
        inner_bias, bias_table,
    )
    sizes = [a.shape[0] for a in vectors]
    if remote:
        qkv, o, ol, r, p, act, slope, unit1, inv1, low1, vec, wqkv, wo, w1, w2 = forward_call(
            n, True, permutation, content_in, query_in, pieces(vectors, ROWS),
            query_weight, key_weight, value_weight, output_weight, inner_weight, outer_weight,
        )
        wqkv = wqkv.reshape(3, D, D)
        wo, w1, w2 = wo.reshape(D, D), w1.reshape(D, FF), w2.reshape(FF, D)
    else:
        packed = lax.all_gather(jnp.concatenate(vectors), "fsdp", axis=0)
        rows = []
        at = 0
        for size in sizes:
            whole = packed[:, at : at + size].reshape(-1).astype(f32)
            rows.append(jnp.pad(whole, (0, -whole.shape[0] % D)).reshape(-1, D))
            at += size
        vec = jnp.concatenate(rows + [jnp.zeros((3, D), f32)], axis=0)
        whole = lax.all_gather(
            jnp.concatenate([query_weight, key_weight, value_weight, output_weight, inner_weight], axis=1),
            "fsdp", axis=0, tiled=True,
        )
        wqkv = jnp.stack(
            [
                jnp.concatenate([whole[:, m * D + g * GROUP : m * D + (g + 1) * GROUP] for m in range(3)], axis=1)
                for g in range(3)
            ]
        )
        wo, w1 = whole[:, 3 * D : 4 * D], whole[:, 4 * D :]
        w2 = lax.all_gather(outer_weight, "fsdp", axis=0, tiled=True)
        qkv, o, ol, r, p, act, slope, unit1, inv1, low1 = forward_call(
            n, False, permutation, content_in, query_in, vec, wqkv, wo, w1
        )

    content_out, query_out, d2, dh, d1, do, dy, sums = middle_call(
        n, unit1, inv1, act, slope, content_cotangent, query_cotangent, vec, wo, w1, w2
    )
    w1_grad, w2_grad, wo_grad = weight_call(n, act, dh, d2, low1, o, d1)

    if remote:
        block = (4, 2, 2)
        dx, sums, g_sum, o_sum, w1_sum, w2_sum = backward_call(
            n, True, permutation, content_in, query_in, wqkv, sums, qkv, o, ol, r, p, do, dy,
            wo_grad.reshape(*block, D // 16, D), w1_grad.reshape(*block, D // 16, FF),
            w2_grad.reshape(*block, FF // 16, D),
        )
        content_grad, query_grad, wq_s, wk_s, wv_s, wo_s, w1_s, w2_s, *shares = output_call(
            n, dx, sums, g_sum, o_sum, w1_sum, w2_sum, sizes
        )
    else:
        dx, sums, wqkv_grad = backward_call(
            n, False, permutation, content_in, query_in, wqkv, sums, qkv, o, ol, r, p, do, dy
        )
        content_grad, query_grad = dx[:, :LEN], dx[:, LEN : LEN + PRED]

        def scatter(a):
            return lax.psum_scatter(a, "fsdp", scatter_dimension=0, tiled=True)

        flat = jnp.concatenate(
            [wqkv_grad[g, :, m * GROUP : (m + 1) * GROUP] for m in range(3) for g in range(3)] + [wo_grad, w1_grad],
            axis=1,
        )
        whole_rows = [sums[i] for i in range(8)] + [sums[8:12].reshape(-1), sums[12, : BUCKETS * HEADS]]
        packed = jnp.concatenate([v.reshape(n_f, -1) for v in whole_rows], axis=1)
        totals = lax.psum((scatter(flat), scatter(w2_grad), scatter(packed).astype(bf16)), "dp")
        flat, w2_s, packed = (a.astype(f32) for a in totals)
        wq_s, wk_s, wv_s, wo_s = (flat[:, m * D : (m + 1) * D] for m in range(4))
        w1_s = flat[:, 4 * D :]
        shares = []
        at = 0
        for size in sizes:
            shares.append(packed[0, at : at + size])
            at += size
    bq_s, bv_s, bo_s, g1_s, s1_s, b2_s, g2_s, s2_s, b1_s, tab_s = shares
    return (
        content_out, query_out, content_grad, query_grad,
        wq_s, wk_s, wv_s, wo_s, w1_s, w2_s,
        bq_s, bv_s, bo_s, g1_s, s1_s, b1_s, b2_s, g2_s, s2_s, tab_s,
    )


def solution(mesh):
    rows3 = P(("dp", "fsdp"), None, None)
    matrix = P("fsdp", None)
    vector = P("fsdp")
    return jax.shard_map(
        per_device,
        mesh=mesh,
        in_specs=(rows3, rows3, P(("dp", "fsdp"), None)) + (matrix,) * 6 + (vector,) * 10 + (rows3, rows3),
        out_specs=(rows3,) * 4 + (matrix,) * 6 + (vector,) * 10,
        check_vma=False,
    )
```

```python
import functools

import jax
import jax.numpy as jnp
from jax import lax
from jax.experimental import pallas as pl
from jax.experimental.pallas import tpu as pltpu
from jax.sharding import PartitionSpec as P

D = 768
HEADS = 12
HEAD = 64
FF = 3072
GROUP = 256
BUCKETS = 32
LEN = 512
PRED = 77
QP = 80
R = LEN + QP
f32 = jnp.float32
bf16 = jnp.bfloat16
MESH = pl.DeviceIdType.MESH
NT = (((1,), (1,)), ((), ()))
TN = (((0,), (0,)), ((), ()))

eps_norm = 1e-05
inverse_root = 0.7071067811865476
density_scale = 0.3989422804014327
bucket_edges = (12, 16, 23, 32, 46, 64, 91)
VMEM_LIMIT = 60 * 1024 * 1024
VMEM_WHOLE = pl.BlockSpec(memory_space=pltpu.VMEM)
ANYWHERE = pl.BlockSpec(memory_space=pl.ANY)


def bucket_index(relative):
    distance = jnp.abs(relative)
    coarse = 8 + sum(((distance >= boundary).astype(jnp.int32) for boundary in bucket_edges))
    within = jnp.where(distance < 8, distance, coarse)
    return within + 16 * (relative > 0).astype(jnp.int32)


def iota(shape, dim):
    return lax.broadcasted_iota(jnp.int32, shape, dim)


def ranking_column(perm_row):
    hit = perm_row == iota((LEN, LEN), 0)
    return jnp.sum(jnp.where(hit, iota((LEN, LEN), 1), 0).astype(f32), axis=1, keepdims=True)


def place():
    f = lax.axis_index("fsdp")
    return f // 4, (f // 2) % 2, f % 2, lax.axis_index("dp")


def device(z, x, c, y):
    return (y, z * 4 + x * 2 + c)


def partners():
    z, x, c, y = place()
    return [device((z + k) % 4, x, c, y) for k in (1, 2, 3)] + [
        device(z, 1 - x, c, y), device(z, x, c, 1 - y), device(z, x, 1 - c, y),
        device(z, 1 - x, c, 1 - y), device(z, 1 - x, 1 - c, y),
    ]


def greet():
    barrier = pltpu.get_barrier_semaphore()
    for other in partners():
        pl.semaphore_signal(barrier, inc=1, device_id=other, device_id_type=MESH)
    pl.semaphore_wait(barrier, 8)


def half_of(y, cols):
    at, size = cols
    return pl.ds(pl.multiple_of(at + y * (size // 2), 128), size // 2)


class Gather:
    def __init__(self, ref, rows, cols, send, recv, item):
        self.ref, self.rows, self.cols = ref, rows, cols
        self.send, self.recv, self.item = send, recv, item

    def copies(self, stage):
        z, x, c, y = place()
        rows = pl.ds(*self.rows)
        every = pl.ds(*self.cols)
        half = half_of(y, self.cols)

        def copy(index, part, other):
            return pltpu.make_async_remote_copy(
                src_ref=part, dst_ref=part,
                send_sem=self.send.at[self.item, index], recv_sem=self.recv.at[self.item, index],
                device_id=other, device_id_type=MESH,
            )

        ref = self.ref
        if stage == 0:
            part = ref.at[z, x, c, rows, half]
            return [copy(k - 1, part, device((z + k) % 4, x, c, y)) for k in (1, 2, 3)]
        if stage == 1:
            return [
                copy(3, ref.at[0:2, x, c, rows, half], device(z, 1 - x, c, y)),
                copy(4, ref.at[2:4, x, c, rows, half], device(z, x, c, 1 - y)),
            ]
        if stage == 2:
            return [
                copy(5, ref.at[0:2, :, c, rows, half], device(z, x, c, 1 - y)),
                copy(6, ref.at[2:4, x, c, rows, every], device(z, 1 - x, c, y)),
            ]
        return [copy(7, ref.at[:, :, c, rows, every], device(z, x, 1 - c, y))]

    def start(self, stage):
        for copy in self.copies(stage):
            copy.start()

    def arrive(self, stage):
        for copy in self.copies(stage):
            copy.wait_recv()

    def step(self, stage):
        if stage > 0:
            self.arrive(stage - 1)
        if stage < 4:
            self.start(stage)

    def drain(self):
        for stage in range(4):
            for copy in self.copies(stage):
                copy.wait_send()


def spread_vectors(raw, f):
    i = iota((256, D), 0)
    lane = iota((256, D), 1)

    def put(size, at):
        hot = jnp.where((i < size) & (lane == i + at), 1.0, 0.0).astype(bf16)
        return jnp.dot(raw, hot, preferred_element_type=f32)

    row = iota((16, D), 0)
    plain = put(D // 16, f * (D // 16))
    wide = put(192, (f % 4) * 192)
    table = put(24, f * 24)
    wide_row = jnp.sum(jnp.where(row == 8, wide, 0.0), axis=0, keepdims=True)
    return jnp.where(
        row < 8, plain, jnp.where(row == 12, table, jnp.where(row == 8 + f // 4, jnp.broadcast_to(wide_row, (16, D)), 0.0))
    )
GATHER_STEPS = {
    "g0": (-1, -1, -1, -1, -1),
    "g1": (-1, -1, -1, 3, 6),
    "g2": (-1, -1, 2, 6, 9),
    "o": (-1, 2, 5, 8, 10),
    "1a": (-1, 3, 7, 12, 15),
    "1b": (1, 5, 10, 15, 17),
    "2a": (3, 8, 13, 18, 20),
    "2b": (6, 11, 16, 21, 99),
}


def build_bias(vectors, full, near, far):
    lane = iota((16, 384), 1)
    own_head = jnp.where(lane % HEADS == iota((16, 384), 0), vectors[12:13, :384], 0.0).astype(bf16)
    rel = iota((384, 1024), 1) - 512
    onehot = (bucket_index(rel) == iota((384, 1024), 0) // HEADS).astype(bf16)
    by_rel = jnp.dot(own_head, onehot, preferred_element_type=f32)
    for h in range(HEADS):
        far[h, 0:8] = jnp.broadcast_to(by_rel[h : h + 1, 0:1], (8, 128))
        far[h, 8:16] = jnp.broadcast_to(by_rel[h : h + 1, 1023:1024], (8, 128))
        for d in range(-3, 4):
            if abs(d) >= 2:
                at = 512 + 128 * d
                block = jnp.broadcast_to(by_rel[h : h + 1, at : at + 1], (128, 128)).astype(bf16)
            else:
                base = 512 + 128 * d - 128
                row = jnp.broadcast_to(by_rel[h : h + 1, base : base + 256], (128, 256))
                tile = pltpu.roll(row, 0, 1, stride=1, stride_axis=0)[:, 128:]
                near[h, d + 1] = tile
                block = tile.astype(bf16)
            for bi in range(4):
                bj = bi + d
                if 0 <= bj < 4:
                    full[h, bi * 128 : (bi + 1) * 128, bj * 128 : (bj + 1) * 128] = block


def build_marks(s, perm_row, row_mark, key_mark, slot_hot):
    rank = ranking_column(perm_row)
    rank_row = jnp.transpose(jnp.broadcast_to(rank, (LEN, 128)))[:1]
    slot = iota((LEN, 128), 1).astype(f32) + float(LEN - PRED)
    limit = jnp.maximum(rank, float(LEN - PRED - 1))
    row_mark[s, :LEN] = jnp.where(limit < slot, 1.0, 0.0).astype(bf16)
    row_mark[s, LEN:] = jnp.where(iota((QP, 128), 0) <= iota((QP, 128), 1), 1.0, 0.0).astype(bf16)
    key_mark[s] = jnp.where(rank == slot, -1e9, 0.0).astype(bf16)
    wanted = (iota((QP, LEN), 0) + (LEN - PRED)).astype(f32)
    slot_hot[s] = (rank_row == wanted).astype(bf16)


def project_group(x, weights, vectors, g, qkv_ref):
    cols = pl.ds(pl.multiple_of(g * GROUP, 128), GROUP)
    bias_q = vectors[0:1, cols]
    bias_v = vectors[1:2, cols]
    eighth = jnp.asarray(0.125, bf16)
    rows = jnp.dot(x[:LEN], weights, preferred_element_type=f32)
    qkv_ref[0, 0, :LEN, :GROUP] = (rows[:, :GROUP] + bias_q).astype(bf16) * eighth
    qkv_ref[0, 0, :LEN, GROUP : 2 * GROUP] = rows[:, GROUP : 2 * GROUP].astype(bf16)
    qkv_ref[0, 0, :LEN, 2 * GROUP :] = (rows[:, 2 * GROUP :] + bias_v).astype(bf16)
    rows = jnp.dot(x[LEN:], weights[:, :GROUP], preferred_element_type=f32)
    qkv_ref[0, 0, LEN:, :GROUP] = (rows + bias_q).astype(bf16) * eighth


def attend_pair(s, hp, j, qkv_ref, o_ref, ol_ref, r_ref, p_ref, full, near, far, scores, row_mark, key_mark, slot_hot):
    q2 = qkv_ref[0, 0, :, pl.ds(pl.multiple_of(j * 128, 128), 128)]
    k2 = qkv_ref[0, 0, :LEN, pl.ds(pl.multiple_of(GROUP + j * 128, 128), 128)]
    v2 = qkv_ref[0, 0, :LEN, pl.ds(pl.multiple_of(2 * GROUP + j * 128, 128), 128)]
    half = iota((LEN, 128), 1) // 64
    left = jnp.concatenate([q2, row_mark[s]], axis=1)
    for h in range(2):
        right = jnp.concatenate([jnp.where(half == h, k2, jnp.zeros_like(k2)), key_mark[s]], axis=1)
        scores[h, :LEN] = lax.dot_general(left[:LEN], right, NT, preferred_element_type=f32)
        scores[h, LEN:] = lax.dot_general(left[LEN:], right, NT, preferred_element_type=f32) + jnp.dot(
            slot_hot[s], full[2 * hp + h], preferred_element_type=f32
        )
    for h in range(2):
        head = 2 * hp + h
        for bi in range(4):
            rows = slice(bi * 128, bi * 128 + 128)
            tiles = []
            for bj in range(4):
                d = bj - bi
                bias = near[head, d + 1] if abs(d) < 2 else far[head, 8:9] if d > 0 else far[head, 0:1]
                tiles.append(scores[h, rows, bj * 128 : (bj + 1) * 128] + bias)
            biased = jnp.concatenate(tiles, axis=1)
            peak = jnp.max(biased, axis=1, keepdims=True)
            p_ref[0, h, rows] = jnp.exp(biased - peak).astype(bf16)
        biased = scores[h, LEN:]
        peak = jnp.max(biased, axis=1, keepdims=True)
        p_ref[0, h, LEN:] = jnp.exp(biased - peak).astype(bf16)
    mixed = []
    for h in range(2):
        vm = jnp.where(half == h, v2, jnp.ones_like(v2))
        mixed.append(jnp.dot(p_ref[0, h], vm, preferred_element_type=f32))
    low = iota((R, 128), 1) < 64
    inverse = 1.0 / pltpu.roll(jnp.where(low, mixed[1], mixed[0]), 64, 1)
    out = jnp.where(low, mixed[0], mixed[1]) * inverse
    out_low = out.astype(bf16)
    o_ref[0] = out_low
    ol_ref[0] = (out - out_low.astype(f32)).astype(bf16)
    r_ref[0] = inverse


def forward_kernel(remote, n, *refs):
    if remote:
        (
            perm_ref, content_ref, query_ref, raw_ref, wq, wk, wv, wo, w1, w2,
            qkv_ref, o_ref, ol_ref, r_ref, p_ref, g_ref, slope_ref, unit_ref, inv_ref, a_ref,
            vec_ref, wqkv_out, wo_out, w1_out, w2_out,
            full, near, far, scores, row_mark, key_mark, slot_hot, x_all, o_all, low_all, x_sem,
            wo_all, w1_all, wqkv, own_qkv, vec_send, vec_recv, local_sem, send, recv, vec_send_sem, vec_recv_sem,
        ) = refs
    else:
        (
            perm_ref, content_ref, query_ref, vec_in, wqkv, wo_all, w1_all,
            qkv_ref, o_ref, ol_ref, r_ref, p_ref, g_ref, slope_ref, unit_ref, inv_ref, a_ref,
            full, near, far, scores, row_mark, key_mark, slot_hot, x_all, o_all, low_all, x_sem,
        ) = refs
    step = pl.program_id(0)
    g, s, j = attention_step(step, n)
    attention_steps = 6 * n
    last = attention_steps + 2 * n - 1

    x_load = pltpu.make_async_copy(content_ref, x_all.at[:, :LEN], x_sem)

    @pl.when(step == 0)
    def _():
        x_load.start()
        place_queries(n, query_ref, x_all)

    if remote:
        z, x_at, c, y = place()
        shard = D // 16
        items = {}
        for i in range(3):
            items[f"g{i}"] = Gather(wqkv.at[i], (0, shard), (0, D), send, recv, i)
        items["o"] = Gather(wo_all, (0, shard), (0, D), send, recv, 3)
        items["1a"] = Gather(w1_all, (0, shard), (0, FF // 2), send, recv, 4)
        items["1b"] = Gather(w1_all, (0, shard), (FF // 2, FF // 2), send, recv, 5)
        items["2a"] = Gather(w2_out, (0, 96), (0, D), send, recv, 6)
        items["2b"] = Gather(w2_out, (96, 96), (0, D), send, recv, 7)
        own = []
        for part, whole, cols in (
            (wo, wo_all, (0, D)), (w1, w1_all, (0, FF // 2)), (w1, w1_all, (FF // 2, FF // 2)), (w2, w2_out, (0, D)),
        ):
            half = half_of(y, cols)
            own.append(
                pltpu.make_async_copy(part.at[:, half], whole.at[z, x_at, c, :, half], local_sem.at[len(own)])
            )

        def vec_copy(k):
            other = (
                device(z, x_at, 1 - c, y), device(z, 1 - x_at, c, y), device(z, 1 - x_at, 1 - c, y),
                *(device((z + t) % 4, x_at, c, y) for t in (1, 2, 3)),
            )[k]
            return pltpu.make_async_remote_copy(
                src_ref=vec_send.at[k // 3], dst_ref=vec_recv.at[k],
                send_sem=vec_send_sem.at[k], recv_sem=vec_recv_sem.at[k], device_id=other, device_id_type=MESH,
            )

        @pl.when(step == 0)
        def _():
            greet()
            half = half_of(y, (0, D))
            for i in range(3):
                for m, part in enumerate((wq, wk, wv)):
                    own_qkv[i, :, m * GROUP : (m + 1) * GROUP] = part[:, i * GROUP : (i + 1) * GROUP]
                wqkv[i, z, x_at, c, :, half] = own_qkv[i, :, half]
            items["g0"].step(0)
            for copy in own:
                copy.start()
            vec_send[0] = spread_vectors(raw_ref[...], z * 4 + x_at * 2 + c)
            for k in (0, 1, 2):
                vec_copy(k).start()
            build_marks(0, perm_ref[0:1], row_mark, key_mark, slot_hot)
            items["g0"].step(1)
            items["g1"].step(0)
            items["g2"].step(0)
            for k in (0, 1, 2):
                vec_copy(k).wait_recv()
            vec_send[1] = vec_send[0] + vec_recv[0] + vec_recv[1] + vec_recv[2]
            for k in (3, 4, 5):
                vec_copy(k).start()
            items["g0"].step(2)
            for i in range(1, n):
                build_marks(i, perm_ref[i : i + 1], row_mark, key_mark, slot_hot)
            items["g1"].step(1)
            for copy in own:
                copy.wait()
            items["o"].step(0)
            for k in (3, 4, 5):
                vec_copy(k).wait_recv()
            vec_ref[...] = vec_send[1] + vec_recv[3] + vec_recv[4] + vec_recv[5]
            items["g0"].step(3)
            build_bias(vec_ref[...], full, near, far)
            items["g2"].step(1)
            items["1a"].step(0)
            items["g1"].step(2)
            items["g0"].step(4)

        back = [
            pltpu.make_async_copy(here, there, local_sem.at[i])
            for i, (here, there) in enumerate(((wqkv, wqkv_out), (wo_all, wo_out), (w1_all, w1_out)))
        ]

        @pl.when(step == attention_steps)
        def _():
            for copy in back:
                copy.start()

        for at in sorted({a for steps in GATHER_STEPS.values() for a in steps if 0 <= a <= last}):

            @pl.when(step == at)
            def _(at=at):
                for stage in range(5):
                    for name, steps in GATHER_STEPS.items():
                        if steps[stage] == at:
                            items[name].step(stage)
        vectors = vec_ref
    else:
        vectors = vec_in

        @pl.when(step == 0)
        def _():
            for i in range(n):
                build_marks(i, perm_ref[i : i + 1], row_mark, key_mark, slot_hot)
            build_bias(vec_in[...], full, near, far)

    @pl.when(step == 0)
    def _():
        x_load.wait()

    @pl.when((step < attention_steps) & (j == 0))
    def _():
        weights = wqkv[g].reshape(D, D) if remote else wqkv[g]
        project_group(x_all[s], weights, vectors, g, qkv_ref)

    @pl.when(step < attention_steps)
    def _():
        attend_pair(
            s, 2 * g + j, j, qkv_ref, o_ref, ol_ref, r_ref, p_ref,
            full, near, far, scores, row_mark, key_mark, slot_hot,
        )
        o_all[s, :, pl.ds(pl.multiple_of((2 * g + j) * 128, 128), 128)] = o_ref[0]

    def before_ffn(s):
        y1 = x_all[s].astype(f32) + vectors[2:3] + jnp.dot(
            o_all[s], wo_all[...].reshape(D, D), preferred_element_type=f32
        )
        unit, inv = norm_parts(y1)
        unit_ref[0] = unit
        inv_ref[0] = jnp.broadcast_to(inv, (R, 128))
        low = (unit * vectors[3:4] + vectors[4:5]).astype(bf16)
        a_ref[0] = low
        low_all[s % 2] = low

    def first_ffn(s, part):
        for i in range(2):
            cols = slice(i * D, (i + 1) * D)
            at = (2 * part + i) * D
            weights = w1_all[:, :, :, :, at : at + D].reshape(D, D) if remote else w1_all[:, at : at + D]
            hidden = jnp.dot(low_all[s % 2], weights, preferred_element_type=f32)
            hidden = hidden + vectors[8 + 2 * part + i : 9 + 2 * part + i]
            g_ref[0, :, cols], slope_ref[0, :, cols] = gelu_parts(hidden)

    @pl.when(step == attention_steps - 1)
    def _():
        before_ffn(0)

    for after in range(n):

        @pl.when(step == attention_steps + 2 * after)
        def _(after=after):
            first_ffn(after, 0)

        @pl.when(step == attention_steps + 2 * after + 1)
        def _(after=after):
            first_ffn(after, 1)
            if after < n - 1:
                before_ffn(after + 1)

    if remote:

        @pl.when(step == last)
        def _():
            for stage in range(5):
                for name, steps in GATHER_STEPS.items():
                    if steps[stage] > last:
                        items[name].step(stage)
            for k in range(6):
                vec_copy(k).wait_send()
            for item in items.values():
                item.drain()
            for copy in back:
                copy.wait()


def place_queries(n, query_ref, x_all):
    x_all[:, R - 16 :] = jnp.zeros((n, 16, D), bf16)
    for i in range(n):
        x_all[i, LEN : LEN + PRED] = query_ref[i]


def attention_step(step, n):
    t = jnp.minimum(step, 6 * n - 1)
    return t // (2 * n), (t // 2) % n, t % 2


def after_step(step, n):
    t = jnp.maximum(step - 6 * n, 0)
    return t // 2, t % 2


def norm_parts(values):
    centered = values - jnp.mean(values, axis=-1, keepdims=True)
    inv = lax.rsqrt(jnp.mean(centered * centered, axis=-1, keepdims=True) + eps_norm)
    return centered * inv, inv


def gelu_parts(hidden):
    phi = 0.5 + 0.5 * lax.erf(hidden * inverse_root)
    bell = jnp.exp(-0.5 * hidden * hidden) * density_scale
    return (hidden * phi).astype(bf16), (phi + hidden * bell).astype(bf16)


def forward_call(n, remote, *operands):
    sds = jax.ShapeDtypeStruct

    def pair(step):
        g, s, j = attention_step(step, n)
        return (s, 0, 2 * g + j)

    def group(step):
        g, s, j = attention_step(step, n)
        return (g, s, 0, 0)

    def pair_scores(step):
        g, s, j = attention_step(step, n)
        return (s, 2 * g + j, 0, 0)

    def after(step):
        s, part = after_step(step, n)
        return (s, 0, part)

    def after_whole(step):
        return (jnp.clip((step - 6 * n + 1) // 2, 0, n - 1), 0, 0)

    out_specs = [
        pl.BlockSpec((1, 1, R, D), group), *[pl.BlockSpec((1, R, 128), pair)] * 3,
        pl.BlockSpec((1, 2, R, LEN), pair_scores),
        *[pl.BlockSpec((1, R, FF // 2), after)] * 2,
        pl.BlockSpec((1, R, D), after_whole), pl.BlockSpec((1, R, 128), after_whole), pl.BlockSpec((1, R, D), after_whole),
    ]
    out_shape = [
        sds((3, n, R, D), bf16), sds((n, R, D), bf16), sds((n, R, D), bf16), sds((n, R, D), f32),
        sds((n, HEADS, R, LEN), bf16), sds((n, R, FF), bf16), sds((n, R, FF), bf16), sds((n, R, D), f32),
        sds((n, R, 128), f32), sds((n, R, D), bf16),
    ]
    scratch = [
        pltpu.VMEM((HEADS, LEN, LEN), bf16),
        pltpu.VMEM((HEADS, 3, 128, 128), f32),
        pltpu.VMEM((HEADS, 16, 128), f32),
        pltpu.VMEM((2, R, LEN), f32),
        pltpu.VMEM((n, R, 128), bf16),
        pltpu.VMEM((n, LEN, 128), bf16),
        pltpu.VMEM((n, QP, LEN), bf16),
        pltpu.VMEM((n, R, D), bf16),
        pltpu.VMEM((n, R, D), bf16),
        pltpu.VMEM((2, R, D), bf16),
        pltpu.SemaphoreType.DMA,
    ]
    if remote:
        in_specs = [VMEM_WHOLE, ANYWHERE] + [VMEM_WHOLE] * 8
        out_specs += [pl.BlockSpec((16, D), lambda step: (0, 0))] + [ANYWHERE] * 4
        block = (4, 2, 2, D // 16)
        out_shape += [
            sds((16, D), f32), sds((3, *block, D), bf16), sds((*block, D), bf16), sds((*block, FF), bf16),
            sds((4, 2, 2, FF // 16, D), bf16),
        ]
        scratch += [
            pltpu.VMEM((*block, D), bf16),
            pltpu.VMEM((*block, FF), bf16),
            pltpu.VMEM((3, *block, D), bf16),
            pltpu.VMEM((3, D // 16, D), bf16),
            pltpu.VMEM((2, 16, D), f32),
            pltpu.VMEM((6, 16, D), f32),
            pltpu.SemaphoreType.DMA((4,)),
            pltpu.SemaphoreType.DMA((8, 8)),
            pltpu.SemaphoreType.DMA((8, 8)),
            pltpu.SemaphoreType.DMA((6,)),
            pltpu.SemaphoreType.DMA((6,)),
        ]
        params = pltpu.CompilerParams(vmem_limit_bytes=VMEM_LIMIT, collective_id=1, has_side_effects=True)
    else:
        in_specs = [VMEM_WHOLE, ANYWHERE] + [VMEM_WHOLE] * 5
        params = pltpu.CompilerParams(vmem_limit_bytes=VMEM_LIMIT)
    return pl.pallas_call(
        functools.partial(forward_kernel, remote, n),
        grid=(8 * n,),
        in_specs=in_specs,
        out_specs=out_specs,
        out_shape=out_shape,
        scratch_shapes=scratch,
        compiler_params=params,
        name="attention_forward",
    )(*operands)


def norm_back(grad, unit, inv, gain):
    scaled = grad * gain
    return inv * (
        scaled - jnp.mean(scaled, axis=-1, keepdims=True) - unit * jnp.mean(scaled * unit, axis=-1, keepdims=True)
    )


def column_sum(values):
    return jnp.sum(values.astype(f32), axis=0, keepdims=True)


def middle_kernel(
    n, unit_ref, inv_ref, g_ref, slope_ref, content_cot, query_cot, vec, wo_hbm, w1_hbm, w2_hbm,
    content_out, query_out, d2_ref, dh_ref, d1_ref, do_ref, dy_ref, sums,
    wo, w1, w2, padded, sem,
):
    s = pl.program_id(0)
    loads = [
        pltpu.make_async_copy(there, here, sem.at[i])
        for i, (there, here) in enumerate(((w2_hbm, w2), (w1_hbm, w1), (wo_hbm, wo)))
    ]

    @pl.when(s == 0)
    def _():
        for copy in loads:
            copy.start()
        sums[...] = jnp.zeros_like(sums)
        padded[PRED - PRED % 8 :] = jnp.zeros((QP - PRED + PRED % 8, D), f32)
        loads[0].wait()

    padded[:PRED] = query_cot[0].astype(f32)
    unit1 = unit_ref[0]
    normed = unit1 * vec[3:4] + vec[4:5]
    y2 = normed + vec[5:6] + jnp.dot(g_ref[0], w2[...], preferred_element_type=f32)
    unit2, inv2 = norm_parts(y2)
    out = (unit2 * vec[6:7] + vec[7:8]).astype(bf16)
    content_out[0] = out[:LEN]
    query_out[0] = out[LEN : LEN + PRED]
    cot = jnp.concatenate([content_cot[0].astype(f32), padded[...]], axis=0)
    sums[7:8] += column_sum(cot)
    sums[6:7] += column_sum(cot * unit2)
    back2 = norm_back(cot, unit2, inv2, vec[6:7])
    d2 = back2.astype(bf16)
    d2_ref[0] = d2
    sums[5:6] += column_sum(d2)

    @pl.when(s == 0)
    def _():
        loads[1].wait()
        loads[2].wait()

    da = back2
    for i in range(FF // D):
        cols = slice(i * D, (i + 1) * D)
        dg = lax.dot_general(d2, w2[cols], NT, preferred_element_type=f32)
        dh = (dg * slope_ref[0, :, cols].astype(f32)).astype(bf16)
        dh_ref[0, :, cols] = dh
        sums[8 + i : 9 + i] += column_sum(dh)
        da = da + lax.dot_general(dh, w1[:, cols], NT, preferred_element_type=f32)
    sums[4:5] += column_sum(da)
    sums[3:4] += column_sum(da * unit1)
    back1 = norm_back(da, unit1, inv_ref[0, :, :1], vec[3:4])
    dy_ref[0] = back1
    d1 = back1.astype(bf16)
    d1_ref[0] = d1
    sums[2:3] += column_sum(d1)
    do_ref[0] = lax.dot_general(d1, wo[...], NT, preferred_element_type=f32).astype(bf16)


def middle_call(n, unit1, inv1, act, slope, content_cot, query_cot, vec, wo, w1, w2):
    sds = jax.ShapeDtypeStruct

    def rows(count, width):
        return pl.BlockSpec((1, count, width), lambda s: (s, 0, 0))

    small = pl.BlockSpec((16, D), lambda s: (0, 0))
    return pl.pallas_call(
        functools.partial(middle_kernel, n),
        grid=(n,),
        in_specs=[rows(R, D), rows(R, 128), rows(R, FF), rows(R, FF), rows(LEN, D), rows(PRED, D), small]
        + [ANYWHERE] * 3,
        out_specs=[rows(LEN, D), rows(PRED, D), rows(R, D), rows(R, FF), rows(R, D), rows(R, D), rows(R, D), small],
        out_shape=[
            sds((n, LEN, D), bf16), sds((n, PRED, D), bf16), sds((n, R, D), bf16), sds((n, R, FF), bf16),
            sds((n, R, D), bf16), sds((n, R, D), bf16), sds((n, R, D), f32), sds((16, D), f32),
        ],
        scratch_shapes=[
            pltpu.VMEM((D, D), bf16), pltpu.VMEM((D, FF), bf16), pltpu.VMEM((FF, D), bf16),
            pltpu.VMEM((QP, D), f32), pltpu.SemaphoreType.DMA((3,)),
        ],
        compiler_params=pltpu.CompilerParams(vmem_limit_bytes=VMEM_LIMIT),
        name="middle",
    )(unit1, inv1, act, slope, content_cot, query_cot, vec, wo, w1, w2)


def weight_kernel(n, act, dh, d2, low1, o, d1, w1_grad, w2_grad, wo_grad, left, right, low, sem):
    step = pl.program_id(0)
    chunks = FF // D
    low_load = pltpu.make_async_copy(low1, low, sem.at[0])
    left_load = pltpu.make_async_copy(o, left, sem.at[1])
    right_load = pltpu.make_async_copy(d1, right, sem.at[2])
    d2_load = pltpu.make_async_copy(d2, right, sem.at[3])

    def outer(a, b):
        return lax.dot_general(
            a[...].reshape(n * R, D), b[...].reshape(n * R, D), TN, preferred_element_type=f32
        ).astype(bf16)

    @pl.when(step == 0)
    def _():
        d2_load.start()
        d2_load.wait()
        low_load.start()

    @pl.when(step < chunks)
    def _():
        w2_grad[...] = outer(act, right)

    @pl.when(step == chunks)
    def _():
        low_load.wait()
        left_load.start()
        right_load.start()

    @pl.when((step >= chunks) & (step < 2 * chunks))
    def _():
        w1_grad[...] = outer(low, dh)

    @pl.when(step == 2 * chunks)
    def _():
        left_load.wait()
        right_load.wait()
        wo_grad[...] = outer(left, right)


def weight_call(n, act, dh, d2, low1, o, d1):
    sds = jax.ShapeDtypeStruct
    chunks = FF // D

    def first(step):
        return jnp.minimum(step, chunks - 1)

    def second(step):
        return jnp.clip(step - chunks, 0, chunks - 1)

    return pl.pallas_call(
        functools.partial(weight_kernel, n),
        grid=(2 * chunks + 1,),
        in_specs=[
            pl.BlockSpec((n, R, D), lambda step: (0, 0, first(step))),
            pl.BlockSpec((n, R, D), lambda step: (0, 0, second(step))),
            ANYWHERE, ANYWHERE, ANYWHERE, ANYWHERE,
        ],
        out_specs=[
            pl.BlockSpec((D, D), lambda step: (0, second(step))),
            pl.BlockSpec((D, D), lambda step: (first(step), 0)),
            pl.BlockSpec((D, D), lambda step: (0, 0)),
        ],
        out_shape=[sds((D, FF), bf16), sds((FF, D), bf16), sds((D, D), bf16)],
        scratch_shapes=[pltpu.VMEM((n, R, D), bf16)] * 3 + [pltpu.SemaphoreType.DMA((4,))],
        compiler_params=pltpu.CompilerParams(vmem_limit_bytes=VMEM_LIMIT),
        name="weight_gradients",
    )(act, dh, d2, low1, o, d1)

REDUCE_STEPS = {
    "2a": (0, 1, 5, 8, 12, 15),
    "2b": (0, 3, 7, 10, 14, 17),
    "1a": (2, 6, 10, 13, 17, 18),
    "1b": (4, 9, 13, 16, 18, 18),
    "o": (7, 11, 15, 17, 18, 18),
    "g0": (8, 13, 16, 18, 18, 18),
    "g1": (13, 15, 17, 18, 18, 18),
    "g2": (18, 18, 18, 18, 18, 18),
}


def add(a, b):
    return (a.astype(f32) + b.astype(f32)).astype(bf16)


class Reduce:
    @staticmethod
    def scratch(rows, cols, loads):
        half = cols // 2
        shapes = [
            (4, 2, rows, cols), (2, 2, rows, half), (2, rows, cols), (2, rows, half), (2, rows, half),
            (4, rows, half), (3, rows, half),
        ]
        if loads:
            shapes.append((4, 2, rows, cols))
        return [pltpu.VMEM(shape, bf16) for shape in shapes]

    def __init__(self, source, at, rows, cols, bufs, out, send, recv, load, item):
        self.source, self.at, self.rows, self.cols = source, at, rows, cols
        self.rc, self.ry, self.rx, self.sx, self.sy, self.a3, self.rz = bufs[:7]
        self.own = bufs[7] if len(bufs) > 7 else None
        self.out, self.send, self.recv, self.load, self.item = out, send, recv, load, item

    def part(self, core):
        rows = pl.ds(self.at[0], self.rows)
        cols = pl.ds(self.at[1], self.cols)
        return self.source.at[:, :, core, rows, cols]

    def load_copy(self):
        z, x, c, y = place()
        return pltpu.make_async_copy(self.part(c), self.own, self.load)

    def copies(self, stage):
        z, x, c, y = place()
        half = self.cols // 2
        other_half = pl.ds(pl.multiple_of((1 - y) * half, 128), half)

        def copy(index, src, dst, other):
            return pltpu.make_async_remote_copy(
                src_ref=src, dst_ref=dst,
                send_sem=self.send.at[self.item, index], recv_sem=self.recv.at[self.item, index],
                device_id=other, device_id_type=MESH,
            )

        if stage == 0:
            return [copy(0, self.part(1 - c), self.rc, device(z, x, 1 - c, y))]
        if stage == 1:
            return [
                copy(1, self.rc.at[0:2, :, :, other_half], self.ry, device(z, x, c, 1 - y)),
                copy(2, self.rc.at[2:4, 1 - x], self.rx, device(z, 1 - x, c, y)),
            ]
        if stage == 2:
            return [
                copy(3, self.ry.at[:, 1 - x], self.sx, device(z, 1 - x, c, y)),
                copy(4, self.rx.at[:, :, other_half], self.sy, device(z, x, c, 1 - y)),
            ]
        if stage == 3:
            return [
                copy(4 + k, self.a3.at[(z + k) % 4], self.rz.at[k - 1], device((z + k) % 4, x, c, y))
                for k in (1, 2, 3)
            ]
        return [copy(8, self.out.at[y], self.out.at[y], device(z, x, c, 1 - y))]

    def combine(self, stage):
        z, x, c, y = place()
        half = self.cols // 2
        own_half = pl.ds(pl.multiple_of(y * half, 128), half)
        if stage == 0:
            if self.own is not None:
                self.load_copy().wait()
            for i in range(4):
                for k in range(2):
                    mine = self.own[i, k] if self.own is not None else self.source[i, k, c]
                    self.rc[i, k] = add(self.rc[i, k], mine)
        elif stage == 1:
            for i in range(2):
                for k in range(2):
                    self.ry[i, k] = add(self.ry[i, k], self.rc[i, k, :, own_half])
                self.rx[i] = add(self.rx[i], self.rc[2 + i, x])
        elif stage == 2:
            for i in range(2):
                self.a3[i] = add(self.sx[i], self.ry[i, x])
                self.a3[2 + i] = add(self.sy[i], self.rx[i, :, own_half])
        elif stage == 3:
            total = self.a3[z].astype(f32)
            for k in range(3):
                total = total + self.rz[k].astype(f32)
            self.out[y] = total.astype(bf16)

    def step(self, stage):
        if stage == 0 and self.own is not None:
            self.load_copy().start()
        if stage > 0:
            for copy in self.copies(stage - 1):
                copy.wait_recv()
            if stage < 5:
                self.combine(stage - 1)
        if stage < 5:
            for copy in self.copies(stage):
                copy.start()

    def drain(self):
        for stage in range(5):
            for copy in self.copies(stage):
                copy.wait_send()


def reduce_table(group, n, slot_cols, kept, near_sum, far_sum):
    c = iota((896, 128), 0)
    rel = jnp.where(c < 768, 128 * (c // 256 - 1) + c % 256 - 128, jnp.where(c % 128 < 64, -200, 200))
    onehot = (bucket_index(rel) == iota((896, 128), 1)).astype(f32)
    slots = jnp.concatenate([slot_cols[i] for i in range(n)], axis=1)
    sub = iota((8, 256), 0)
    lane8 = iota((8, 128), 1)
    lane1 = iota((1, 128), 1)
    rows = []
    for head in range(4):
        moved = jnp.dot(slots, kept[head], preferred_element_type=f32)
        near = [near_sum[head, d] for d in range(3)]
        far = [far_sum[head, 0:8], far_sum[head, 8:16]]
        for bi in range(4):
            for bj in range(4):
                d = bj - bi
                tile = moved[bi * 128 : (bi + 1) * 128, bj * 128 : (bj + 1) * 128]
                if abs(d) < 2:
                    near[d + 1] = near[d + 1] + tile
                else:
                    far[int(d > 0)] = far[int(d > 0)] + tile.reshape(16, 8, 128).sum(0)
        parts = []
        for d in range(3):
            high = low = None
            for a in range(16):
                x = near[d][8 * a : 8 * a + 8]
                if a:
                    x = pltpu.roll(x, 128 - 8 * a, 1)
                keep = lane8 < 128 - 8 * a
                u = jnp.where(keep, x, 0.0)
                w = jnp.where(keep, 0.0, x)
                high = u if high is None else high + u
                low = w if low is None else low + w
            y = jnp.concatenate([low, high], axis=1)
            for k in (1, 2, 4):
                y = jnp.where((sub & k) != 0, pltpu.roll(y, 256 - k, 1), y)
            parts.append(jnp.sum(y, axis=0, keepdims=True))
        parts.append(jnp.where(lane1 == 0, jnp.sum(far[0]), jnp.where(lane1 == 64, jnp.sum(far[1]), 0.0)))
        rows.append(jnp.concatenate(parts, axis=1))
    rows.append(jnp.zeros((4, 896), f32))
    return jnp.dot(
        jnp.concatenate(rows, axis=0), onehot, preferred_element_type=f32, precision=lax.Precision.HIGHEST
    )


def table_row(by_head):
    spread = (iota((128, D), 0) == iota((128, D), 1) // HEADS).astype(f32)
    wide = jnp.dot(by_head, spread, preferred_element_type=f32, precision=lax.Precision.HIGHEST)
    lane = iota((16, D), 1)
    mine = (lane % HEADS == iota((16, D), 0)) & (lane < BUCKETS * HEADS)
    return jnp.sum(jnp.where(mine, wide, 0.0), axis=0, keepdims=True)


def attend_pair_back(
    s, hp, j, qkv_ref, o_ref, ol_ref, r_ref, p_ref, do_ref, dqkv, dp, ds, kept, near_sum, far_sum
):
    q2 = qkv_ref[0, 0, :, pl.ds(pl.multiple_of(j * 128, 128), 128)]
    k2 = qkv_ref[0, 0, :LEN, pl.ds(pl.multiple_of(GROUP + j * 128, 128), 128)]
    v2 = qkv_ref[0, 0, :LEN, pl.ds(pl.multiple_of(2 * GROUP + j * 128, 128), 128)]
    delta = (do_ref[0].astype(f32) * r_ref[0]).astype(bf16)
    prod = delta.astype(f32) * (o_ref[0].astype(f32) + ol_ref[0].astype(f32))
    high = prod.astype(bf16)
    rest = pltpu.roll(prod - high.astype(f32), 64, 1).astype(bf16)
    low = iota((R, 128), 1) < 64
    half = iota((LEN, 128), 1) // 64
    extra = [jnp.where(low, high, rest), jnp.where(low, rest, high)]
    minus = jnp.full((LEN, 128), -1.0, bf16)
    for h in range(2):
        vm = jnp.where(half == h, v2, jnp.zeros_like(v2))
        dp[h] = lax.dot_general(
            jnp.concatenate([delta, extra[h]], axis=1),
            jnp.concatenate([vm, minus], axis=1),
            NT,
            preferred_element_type=f32,
        )
    for h in range(2):
        head = 2 * j + h
        far = [None, None]
        for bi in range(4):
            rows = slice(bi * 128, bi * 128 + 128)
            d_rows = p_ref[0, h, rows].astype(f32) * dp[h, rows]
            ds[h, rows] = d_rows.astype(bf16)
            for bj in range(4):
                d = bj - bi
                tile = d_rows[:, bj * 128 : (bj + 1) * 128]
                if abs(d) < 2:
                    near_sum[head, d + 1] += tile
                else:
                    part = tile.reshape(16, 8, 128).sum(0)
                    far[int(d > 0)] = part if far[int(d > 0)] is None else far[int(d > 0)] + part
        far_sum[head, 0:8] += far[0]
        far_sum[head, 8:16] += far[1]
        d_slots = (p_ref[0, h, LEN:].astype(f32) * dp[h, LEN:]).astype(bf16)
        ds[h, LEN:] = d_slots
        kept[head, pl.ds(pl.multiple_of(s * QP, 16), QP)] = d_slots
    dq = None
    for h in range(2):
        km = jnp.where(half == h, k2, jnp.zeros_like(k2))
        part = jnp.dot(ds[h], km, preferred_element_type=f32)
        dq = part if dq is None else dq + part
    dqkv[s, :, pl.ds(pl.multiple_of(j * 128, 128), 128)] = (dq * 0.125).astype(bf16)
    q_t = jnp.transpose(q2)
    delta_t = jnp.transpose(delta)
    dk_t = [jnp.dot(q_t[h * 64 : (h + 1) * 64], ds[h], preferred_element_type=f32) for h in range(2)]
    dv_t = [jnp.dot(delta_t[h * 64 : (h + 1) * 64], p_ref[0, h], preferred_element_type=f32) for h in range(2)]
    dqkv[s, :LEN, pl.ds(pl.multiple_of(GROUP + j * 128, 128), 128)] = jnp.transpose(
        jnp.concatenate(dk_t, axis=0).astype(bf16)
    )
    dqkv[s, :LEN, pl.ds(pl.multiple_of(2 * GROUP + j * 128, 128), 128)] = jnp.transpose(
        jnp.concatenate(dv_t, axis=0).astype(bf16)
    )


def backward_kernel(remote, n, *refs):
    (
        perm_ref, content_ref, query_ref, wqkv, vec_in, qkv_ref, o_ref, ol_ref, r_ref, p_ref, do_ref, dy_ref,
        *refs,
    ) = refs
    if remote:
        (
            wo_grad, w1_grad, w2_grad,
            dx_ref, vec_ref, g_out, o_out, w1_out, w2_out,
            dx, dqkv, dp, ds, kept, slot_cols, near_sum, far_sum, tab, x_all, dy_sem, x_sem,
            wqkv_grad, g_sum, o_sum, w1_sum, w2_sum, vec_send, vec_recv, load_sem, send, recv, vec_send_sem, vec_recv_sem,
            *bufs,
        ) = refs
    else:
        (
            dx_ref, vec_ref, wqkv_grad,
            dx, dqkv, dp, ds, kept, slot_cols, near_sum, far_sum, tab, x_all, dy_sem, x_sem,
        ) = refs
    g = pl.program_id(0)
    s = pl.program_id(1)
    j = pl.program_id(2)
    step = (g * n + s) * 2 + j
    last = 3 * n * 2 - 1
    loads = [
        pltpu.make_async_copy(dy_ref, dx, dy_sem),
        pltpu.make_async_copy(content_ref, x_all.at[:, :LEN], x_sem),
    ]

    if remote:
        z, x_at, c, y = place()
        shard = D // 16
        wide = 2 * FF // 4

        def item(name, index, source, at, rows, cols, out):
            first = index * 8 if index < 5 else 40 + (index - 5) * 7
            take = 8 if index < 5 else 7
            return Reduce(
                source, at, rows, cols, bufs[first : first + take], out, send, recv,
                load_sem.at[index] if index < 5 else None, index,
            )

        items = {
            "2a": item("2a", 0, w2_grad, (0, 0), 96, D, w2_sum.at[0]),
            "2b": item("2b", 1, w2_grad, (96, 0), 96, D, w2_sum.at[1]),
            "1a": item("1a", 2, w1_grad, (0, 0), shard, wide, w1_sum.at[0]),
            "1b": item("1b", 3, w1_grad, (0, wide), shard, wide, w1_sum.at[1]),
            "o": item("o", 4, wo_grad, (0, 0), shard, D, o_sum),
        }
        for i in range(3):
            items[f"g{i}"] = item(f"g{i}", 5 + i, wqkv_grad.at[i], (0, 0), shard, D, g_sum.at[i])

        def vec_copy(k):
            other = (
                device(z, x_at, 1 - c, y),
                device(z, x_at, c, 1 - y), device(z, 1 - x_at, c, y), device(z, 1 - x_at, c, 1 - y),
                *(device((z + t) % 4, x_at, c, y) for t in (1, 2, 3)),
            )[k]
            return pltpu.make_async_remote_copy(
                src_ref=vec_send.at[0 if k == 0 else 1 if k < 4 else 2], dst_ref=vec_recv.at[k],
                send_sem=vec_send_sem.at[k], recv_sem=vec_recv_sem.at[k], device_id=other, device_id_type=MESH,
            )

    @pl.when(step == 0)
    def _():
        for copy in loads:
            copy.start()
        if remote:
            greet()
        place_queries(n, query_ref, x_all)
        vec_ref[...] = vec_in[...]
        for i in range(n):
            rank = ranking_column(perm_ref[i : i + 1])
            slot_cols[i] = (rank == (iota((LEN, QP), 1) + (LEN - PRED)).astype(f32)).astype(bf16)
        dqkv[:, LEN:, GROUP:] = jnp.zeros((n, QP, 2 * GROUP), bf16)

    if remote:
        for at in sorted({a for steps in REDUCE_STEPS.values() for a in steps if a <= last}):

            @pl.when(step == at)
            def _(at=at):
                for stage in range(6):
                    for name, steps in REDUCE_STEPS.items():
                        if steps[stage] == at:
                            items[name].step(stage)

    @pl.when((s == 0) & (j == 0))
    def _():
        near_sum[...] = jnp.zeros_like(near_sum)
        far_sum[...] = jnp.zeros_like(far_sum)

    attend_pair_back(
        s, 2 * g + j, j, qkv_ref, o_ref, ol_ref, r_ref, p_ref, do_ref, dqkv, dp, ds, kept, near_sum, far_sum
    )

    @pl.when(step == 1)
    def _():
        for copy in loads:
            copy.wait()

    @pl.when((s == n - 1) & (j == 1))
    def _():
        total = lax.dot_general(
            x_all[...].reshape(n * R, D), dqkv[...].reshape(n * R, D), TN, preferred_element_type=f32
        ).astype(bf16)
        wqkv_grad[g] = total.reshape(4, 2, 2, D // 16, D) if remote else total

    if remote:

        @pl.when(step == last)
        def _():
            items["g2"].step(0)

    @pl.when(j == 1)
    def _():
        weights = wqkv[g]
        dx[s] += lax.dot_general(dqkv[s], weights, NT, preferred_element_type=f32)

    @pl.when((s == n - 1) & (j == 1))
    def _():
        tab[g] = reduce_table(g, n, slot_cols, kept, near_sum, far_sum)
        sums = jnp.sum(dqkv[0].astype(f32), axis=0, keepdims=True)
        for i in range(1, n):
            sums = sums + jnp.sum(dqkv[i].astype(f32), axis=0, keepdims=True)
        cols = pl.ds(pl.multiple_of(g * GROUP, 128), GROUP)
        vec_ref[0:1, cols] = sums[:, :GROUP]
        vec_ref[1:2, cols] = sums[:, 2 * GROUP :]

    @pl.when(step == last)
    def _():
        by_head = jnp.concatenate([tab[0, :4], tab[1, :4], tab[2, :4], jnp.zeros((4, 128), f32)], axis=0)
        vec_ref[12:13] = table_row(by_head)
        out_copy = pltpu.make_async_copy(dx, dx_ref, dy_sem)
        out_copy.start()
        if remote:
            vec_send[0] = vec_ref[...]
            vec_copy(0).start()
            tail = [(stage, name) for stage in range(6) for name in REDUCE_STEPS if REDUCE_STEPS[name][stage] > last]
            tail.remove((0, "g2"))
            order = sorted(tail, key=lambda t: t[0] - LATE[t[1]])
            for stage, name in order:
                items[name].step(stage)
                if name == "g2" and stage == 1:
                    vec_copy(0).wait_recv()
                    vec_send[1] = vec_send[0] + vec_recv[0]
                    for k in (1, 2, 3):
                        vec_copy(k).start()
                if name == "g2" and stage == 2:
                    for k in (1, 2, 3):
                        vec_copy(k).wait_recv()
                    vec_send[2] = vec_send[1] + vec_recv[1] + vec_recv[2] + vec_recv[3]
                    for k in (4, 5, 6):
                        vec_copy(k).start()
            for k in (4, 5, 6):
                vec_copy(k).wait_recv()
            vec_ref[...] = vec_send[2] + vec_recv[4] + vec_recv[5] + vec_recv[6]
            for k in range(7):
                vec_copy(k).wait_send()
            for entry in items.values():
                entry.drain()
            g_out[...] = g_sum[...]
            o_out[...] = o_sum[...]
            w1_out[...] = w1_sum[...]
            w2_out[...] = w2_sum[...]
        out_copy.wait()


LATE = {"2a": 0, "2b": 0, "1a": 3.8, "1b": 2.5, "o": 2.4, "g0": 1.6, "g1": 1.5, "g2": 0}


def backward_call(n, remote, *operands):
    sds = jax.ShapeDtypeStruct
    pair = pl.BlockSpec((1, R, 128), lambda g, s, j: (s, 0, 2 * g + j))
    block = (4, 2, 2, D // 16)
    in_specs = [VMEM_WHOLE, ANYWHERE, VMEM_WHOLE, VMEM_WHOLE, VMEM_WHOLE] + [
        pl.BlockSpec((1, 1, R, D), lambda g, s, j: (g, s, 0, 0)), pair, pair, pair,
        pl.BlockSpec((1, 2, R, LEN), lambda g, s, j: (s, 2 * g + j, 0, 0)),
        pair, ANYWHERE,
    ]
    small = pl.BlockSpec((16, D), lambda g, s, j: (0, 0))
    out_specs = [ANYWHERE, small]
    out_shape = [sds((n, R, D), f32), sds((16, D), f32)]
    scratch = [
        pltpu.VMEM((n, R, D), f32),
        pltpu.VMEM((n, R, D), bf16),
        pltpu.VMEM((2, R, LEN), f32),
        pltpu.VMEM((2, R, LEN), bf16),
        pltpu.VMEM((4, n * QP, LEN), bf16),
        pltpu.VMEM((n, LEN, QP), bf16),
        pltpu.VMEM((4, 3, 128, 128), f32),
        pltpu.VMEM((4, 16, 128), f32),
        pltpu.VMEM((3, 8, 128), f32),
        pltpu.VMEM((n, R, D), bf16),
        pltpu.SemaphoreType.DMA,
        pltpu.SemaphoreType.DMA,
    ]
    if remote:
        in_specs += [ANYWHERE] * 3
        out_specs += [VMEM_WHOLE] * 4
        shard = D // 16
        out_shape += [
            sds((3, 2, shard, D // 2), bf16), sds((2, shard, D // 2), bf16), sds((2, 2, shard, FF // 4), bf16),
            sds((2, 2, 96, D // 2), bf16),
        ]
        scratch += [
            pltpu.VMEM((3, *block, D), bf16),
            *(pltpu.VMEM(a.shape, bf16) for a in out_shape[2:]),
            pltpu.VMEM((3, 16, D), f32),
            pltpu.VMEM((7, 16, D), f32),
            pltpu.SemaphoreType.DMA((5,)),
            pltpu.SemaphoreType.DMA((8, 9)),
            pltpu.SemaphoreType.DMA((8, 9)),
            pltpu.SemaphoreType.DMA((7,)),
            pltpu.SemaphoreType.DMA((7,)),
        ]
        for rows, cols in ((96, D), (96, D), (shard, FF // 2), (shard, FF // 2), (shard, D)):
            scratch += Reduce.scratch(rows, cols, True)
        for _ in range(3):
            scratch += Reduce.scratch(shard, D, False)
        params = pltpu.CompilerParams(vmem_limit_bytes=VMEM_LIMIT, collective_id=2, has_side_effects=True)
    else:
        out_specs += [pl.BlockSpec(memory_space=pltpu.VMEM)]
        out_shape += [sds((3, D, D), bf16)]
        params = pltpu.CompilerParams(vmem_limit_bytes=VMEM_LIMIT)
    return pl.pallas_call(
        functools.partial(backward_kernel, remote, n),
        grid=(3, n, 2),
        in_specs=in_specs,
        out_specs=out_specs,
        out_shape=out_shape,
        scratch_shapes=scratch,
        compiler_params=params,
        name="attention_backward",
    )(*operands)


def output_kernel(dx_ref, vec, g_sum, o_sum, w1_sum, w2_sum, content, query, wq, wk, wv, wo, w1, w2, *vectors):
    content[0] = dx_ref[0, :LEN]
    query[0] = dx_ref[0, LEN : LEN + PRED]

    @pl.when(pl.program_id(0) == 0)
    def _():
        for m, out in enumerate((wq, wk, wv)):
            for g in range(3):
                for k in range(2):
                    at = m * 2 + k
                    out[:, g * GROUP + k * 128 : g * GROUP + (k + 1) * 128] = g_sum[
                        g, at // 3, :, (at % 3) * 128 : (at % 3 + 1) * 128
                    ].astype(f32)
        for k in range(2):
            wo[:, k * D // 2 : (k + 1) * D // 2] = o_sum[k].astype(f32)
            for i in range(2):
                at = i * (FF // 2) + k * (FF // 4)
                w1[:, at : at + FF // 4] = w1_sum[i, k].astype(f32)
                w2[i * 96 : (i + 1) * 96, k * D // 2 : (k + 1) * D // 2] = w2_sum[i, k].astype(f32)
        f = lax.axis_index("fsdp")
        lane = iota((D, 256), 0)
        i = iota((D, 256), 1)

        def take(rows, size, at):
            hot = jnp.where((i < size) & (lane == i + at), 1.0, 0.0)
            return jnp.dot(rows, hot, preferred_element_type=f32, precision=lax.Precision.HIGHEST)

        plain = take(vec[0:8], D // 16, f * (D // 16))
        wide = jnp.sum(jnp.where(iota((16, D), 0) == 8 + f // 4, vec[...], 0.0), axis=0, keepdims=True)
        wide = take(jnp.broadcast_to(wide, (8, D)), 192, (f % 4) * 192)
        table = take(jnp.broadcast_to(vec[12:13], (8, D)), 24, f * 24)
        rows = [plain[r : r + 1] for r in range(8)] + [wide[:1], table[:1]]
        for out, row in zip(vectors, rows):
            out[...] = row[0, : out.shape[0]]


def output_call(n, dx, vec, g_sum, o_sum, w1_sum, w2_sum, sizes):
    sds = jax.ShapeDtypeStruct

    def rows(count):
        return pl.BlockSpec((1, count, D), lambda s: (s, 0, 0))

    shard = D // 16
    return pl.pallas_call(
        output_kernel,
        grid=(n,),
        in_specs=[rows(R)] + [VMEM_WHOLE] * 5,
        out_specs=[rows(LEN), rows(PRED)] + [VMEM_WHOLE] * (6 + len(sizes)),
        out_shape=[sds((n, LEN, D), f32), sds((n, PRED, D), f32)]
        + [sds((shard, D), f32)] * 4
        + [sds((shard, FF), f32), sds((FF // 16, D), f32)]
        + [sds((size,), f32) for size in sizes],
        compiler_params=pltpu.CompilerParams(vmem_limit_bytes=VMEM_LIMIT),
        name="outputs",
    )(dx, vec, g_sum, o_sum, w1_sum, w2_sum)
def pieces(own_vectors, places):
    return sum(jnp.pad(v[None], ((at, 15 - at), (0, 256 - v.shape[0]))) for at, v in zip(places, own_vectors))


ROWS = (0, 1, 2, 3, 4, 5, 6, 7, 8, 12)


def per_device(
    content_in, query_in, permutation,
    query_weight, key_weight, value_weight, output_weight, inner_weight, outer_weight,
    query_bias, value_bias, output_bias, first_gain, first_shift, inner_bias, outer_bias,
    second_gain, second_shift, bias_table,
    content_cotangent, query_cotangent,
):
    n = content_in.shape[0]
    n_f = lax.axis_size("fsdp")
    remote = n_f == 16 and lax.axis_size("dp") == 2 and n == 3
    vectors = (
        query_bias, value_bias, output_bias, first_gain, first_shift, outer_bias, second_gain, second_shift,
        inner_bias, bias_table,
    )
    sizes = [a.shape[0] for a in vectors]
    if remote:
        qkv, o, ol, r, p, act, slope, unit1, inv1, low1, vec, wqkv, wo, w1, w2 = forward_call(
            n, True, permutation, content_in, query_in, pieces(vectors, ROWS),
            query_weight, key_weight, value_weight, output_weight, inner_weight, outer_weight,
        )
        wqkv = wqkv.reshape(3, D, D)
        wo, w1, w2 = wo.reshape(D, D), w1.reshape(D, FF), w2.reshape(FF, D)
    else:
        packed = lax.all_gather(jnp.concatenate(vectors), "fsdp", axis=0)
        rows = []
        at = 0
        for size in sizes:
            whole = packed[:, at : at + size].reshape(-1).astype(f32)
            rows.append(jnp.pad(whole, (0, -whole.shape[0] % D)).reshape(-1, D))
            at += size
        vec = jnp.concatenate(rows + [jnp.zeros((3, D), f32)], axis=0)
        whole = lax.all_gather(
            jnp.concatenate([query_weight, key_weight, value_weight, output_weight, inner_weight], axis=1),
            "fsdp", axis=0, tiled=True,
        )
        wqkv = jnp.stack(
            [
                jnp.concatenate([whole[:, m * D + g * GROUP : m * D + (g + 1) * GROUP] for m in range(3)], axis=1)
                for g in range(3)
            ]
        )
        wo, w1 = whole[:, 3 * D : 4 * D], whole[:, 4 * D :]
        w2 = lax.all_gather(outer_weight, "fsdp", axis=0, tiled=True)
        qkv, o, ol, r, p, act, slope, unit1, inv1, low1 = forward_call(
            n, False, permutation, content_in, query_in, vec, wqkv, wo, w1
        )

    content_out, query_out, d2, dh, d1, do, dy, sums = middle_call(
        n, unit1, inv1, act, slope, content_cotangent, query_cotangent, vec, wo, w1, w2
    )
    w1_grad, w2_grad, wo_grad = weight_call(n, act, dh, d2, low1, o, d1)

    if remote:
        block = (4, 2, 2)
        dx, sums, g_sum, o_sum, w1_sum, w2_sum = backward_call(
            n, True, permutation, content_in, query_in, wqkv, sums, qkv, o, ol, r, p, do, dy,
            wo_grad.reshape(*block, D // 16, D), w1_grad.reshape(*block, D // 16, FF),
            w2_grad.reshape(*block, FF // 16, D),
        )
        content_grad, query_grad, wq_s, wk_s, wv_s, wo_s, w1_s, w2_s, *shares = output_call(
            n, dx, sums, g_sum, o_sum, w1_sum, w2_sum, sizes
        )
    else:
        dx, sums, wqkv_grad = backward_call(
            n, False, permutation, content_in, query_in, wqkv, sums, qkv, o, ol, r, p, do, dy
        )
        content_grad, query_grad = dx[:, :LEN], dx[:, LEN : LEN + PRED]

        def scatter(a):
            return lax.psum_scatter(a, "fsdp", scatter_dimension=0, tiled=True)

        flat = jnp.concatenate(
            [wqkv_grad[g, :, m * GROUP : (m + 1) * GROUP] for m in range(3) for g in range(3)] + [wo_grad, w1_grad],
            axis=1,
        )
        whole_rows = [sums[i] for i in range(8)] + [sums[8:12].reshape(-1), sums[12, : BUCKETS * HEADS]]
        packed = jnp.concatenate([v.reshape(n_f, -1) for v in whole_rows], axis=1)
        totals = lax.psum((scatter(flat), scatter(w2_grad), scatter(packed).astype(bf16)), "dp")
        flat, w2_s, packed = (a.astype(f32) for a in totals)
        wq_s, wk_s, wv_s, wo_s = (flat[:, m * D : (m + 1) * D] for m in range(4))
        w1_s = flat[:, 4 * D :]
        shares = []
        at = 0
        for size in sizes:
            shares.append(packed[0, at : at + size])
            at += size
    bq_s, bv_s, bo_s, g1_s, s1_s, b2_s, g2_s, s2_s, b1_s, tab_s = shares
    return (
        content_out, query_out, content_grad, query_grad,
        wq_s, wk_s, wv_s, wo_s, w1_s, w2_s,
        bq_s, bv_s, bo_s, g1_s, s1_s, b1_s, b2_s, g2_s, s2_s, tab_s,
    )


def solution(mesh):
    rows3 = P(("dp", "fsdp"), None, None)
    matrix = P("fsdp", None)
    vector = P("fsdp")
    return jax.shard_map(
        per_device,
        mesh=mesh,
        in_specs=(rows3, rows3, P(("dp", "fsdp"), None)) + (matrix,) * 6 + (vector,) * 10 + (rows3, rows3),
        out_specs=(rows3,) * 4 + (matrix,) * 6 + (vector,) * 10,
        check_vma=False,
    )
```

```python
import functools

import jax
import jax.numpy as jnp
from jax import lax
from jax.experimental import pallas as pl
from jax.experimental.pallas import tpu as pltpu
from jax.sharding import PartitionSpec as P

D = 768
HEADS = 12
HEAD = 64
FF = 3072
GROUP = 256
BUCKETS = 32
LEN = 512
PRED = 77
QP = 80
R = LEN + QP
f32 = jnp.float32
bf16 = jnp.bfloat16
MESH = pl.DeviceIdType.MESH
NT = (((1,), (1,)), ((), ()))
TN = (((0,), (0,)), ((), ()))

eps_norm = 1e-05
inverse_root = 0.7071067811865476
density_scale = 0.3989422804014327
bucket_edges = (12, 16, 23, 32, 46, 64, 91)
VMEM_LIMIT = 60 * 1024 * 1024
VMEM_WHOLE = pl.BlockSpec(memory_space=pltpu.VMEM)
ANYWHERE = pl.BlockSpec(memory_space=pl.ANY)


def bucket_index(relative):
    distance = jnp.abs(relative)
    coarse = 8 + sum(((distance >= boundary).astype(jnp.int32) for boundary in bucket_edges))
    within = jnp.where(distance < 8, distance, coarse)
    return within + 16 * (relative > 0).astype(jnp.int32)


def iota(shape, dim):
    return lax.broadcasted_iota(jnp.int32, shape, dim)


def ranking_column(perm_row):
    hit = perm_row == iota((LEN, LEN), 0)
    return jnp.sum(jnp.where(hit, iota((LEN, LEN), 1), 0).astype(f32), axis=1, keepdims=True)


def place():
    f = lax.axis_index("fsdp")
    return f // 4, (f // 2) % 2, f % 2, lax.axis_index("dp")


def device(z, x, c, y):
    return (y, z * 4 + x * 2 + c)


def partners():
    z, x, c, y = place()
    return [device((z + k) % 4, x, c, y) for k in (1, 2, 3)] + [
        device(z, 1 - x, c, y), device(z, x, c, 1 - y), device(z, x, 1 - c, y),
        device(z, 1 - x, c, 1 - y), device(z, 1 - x, 1 - c, y),
    ]


def greet():
    barrier = pltpu.get_barrier_semaphore()
    for other in partners():
        pl.semaphore_signal(barrier, inc=1, device_id=other, device_id_type=MESH)
    pl.semaphore_wait(barrier, 8)


def half_of(y, cols):
    at, size = cols
    return pl.ds(pl.multiple_of(at + y * (size // 2), 128), size // 2)


class Gather:
    def __init__(self, ref, rows, cols, send, recv, item):
        self.ref, self.rows, self.cols = ref, rows, cols
        self.send, self.recv, self.item = send, recv, item

    def copies(self, stage):
        z, x, c, y = place()
        rows = pl.ds(*self.rows)
        every = pl.ds(*self.cols)
        half = half_of(y, self.cols)

        def copy(index, part, other):
            return pltpu.make_async_remote_copy(
                src_ref=part, dst_ref=part,
                send_sem=self.send.at[self.item, index], recv_sem=self.recv.at[self.item, index],
                device_id=other, device_id_type=MESH,
            )

        ref = self.ref
        if stage == 0:
            part = ref.at[z, x, c, rows, half]
            return [copy(k - 1, part, device((z + k) % 4, x, c, y)) for k in (1, 2, 3)]
        if stage == 1:
            return [
                copy(3, ref.at[0:2, x, c, rows, half], device(z, 1 - x, c, y)),
                copy(4, ref.at[2:4, x, c, rows, half], device(z, x, c, 1 - y)),
            ]
        if stage == 2:
            return [
                copy(5, ref.at[0:2, :, c, rows, half], device(z, x, c, 1 - y)),
                copy(6, ref.at[2:4, x, c, rows, every], device(z, 1 - x, c, y)),
            ]
        return [copy(7, ref.at[:, :, c, rows, every], device(z, x, 1 - c, y))]

    def start(self, stage):
        for copy in self.copies(stage):
            copy.start()

    def arrive(self, stage):
        for copy in self.copies(stage):
            copy.wait_recv()

    def step(self, stage):
        if stage > 0:
            self.arrive(stage - 1)
        if stage < 4:
            self.start(stage)

    def drain(self):
        for stage in range(4):
            for copy in self.copies(stage):
                copy.wait_send()


def spread_vectors(raw, f):
    i = iota((256, D), 0)
    lane = iota((256, D), 1)

    def put(size, at):
        hot = jnp.where((i < size) & (lane == i + at), 1.0, 0.0).astype(bf16)
        return jnp.dot(raw, hot, preferred_element_type=f32)

    row = iota((16, D), 0)
    plain = put(D // 16, f * (D // 16))
    wide = put(192, (f % 4) * 192)
    table = put(24, f * 24)
    wide_row = jnp.sum(jnp.where(row == 8, wide, 0.0), axis=0, keepdims=True)
    return jnp.where(
        row < 8, plain, jnp.where(row == 12, table, jnp.where(row == 8 + f // 4, jnp.broadcast_to(wide_row, (16, D)), 0.0))
    )
GATHER_STEPS = {
    "g0": (-1, -1, -1, -1, -1),
    "g1": (-1, -1, -1, 3, 6),
    "g2": (-1, -1, 2, 6, 9),
    "o": (-1, 2, 5, 8, 10),
    "1a": (-1, 3, 7, 12, 15),
    "1b": (1, 5, 10, 15, 17),
    "2a": (3, 8, 13, 18, 20),
    "2b": (6, 11, 16, 21, 99),
}


def build_bias(vectors, full, near, far):
    lane = iota((16, 384), 1)
    own_head = jnp.where(lane % HEADS == iota((16, 384), 0), vectors[12:13, :384], 0.0).astype(bf16)
    rel = iota((384, 1024), 1) - 512
    onehot = (bucket_index(rel) == iota((384, 1024), 0) // HEADS).astype(bf16)
    by_rel = jnp.dot(own_head, onehot, preferred_element_type=f32)
    for h in range(HEADS):
        far[h, 0:8] = jnp.broadcast_to(by_rel[h : h + 1, 0:1], (8, 128))
        far[h, 8:16] = jnp.broadcast_to(by_rel[h : h + 1, 1023:1024], (8, 128))
        for d in range(-3, 4):
            if abs(d) >= 2:
                at = 512 + 128 * d
                block = jnp.broadcast_to(by_rel[h : h + 1, at : at + 1], (128, 128)).astype(bf16)
            else:
                base = 512 + 128 * d - 128
                row = jnp.broadcast_to(by_rel[h : h + 1, base : base + 256], (128, 256))
                tile = pltpu.roll(row, 0, 1, stride=1, stride_axis=0)[:, 128:]
                near[h, d + 1] = tile
                block = tile.astype(bf16)
            for bi in range(4):
                bj = bi + d
                if 0 <= bj < 4:
                    full[h, bi * 128 : (bi + 1) * 128, bj * 128 : (bj + 1) * 128] = block


def build_marks(s, perm_row, row_mark, key_mark, slot_hot):
    rank = ranking_column(perm_row)
    rank_row = jnp.transpose(jnp.broadcast_to(rank, (LEN, 128)))[:1]
    slot = iota((LEN, 128), 1).astype(f32) + float(LEN - PRED)
    limit = jnp.maximum(rank, float(LEN - PRED - 1))
    row_mark[s, :LEN] = jnp.where(limit < slot, 1.0, 0.0).astype(bf16)
    row_mark[s, LEN:] = jnp.where(iota((QP, 128), 0) <= iota((QP, 128), 1), 1.0, 0.0).astype(bf16)
    key_mark[s] = jnp.where(rank == slot, -1e9, 0.0).astype(bf16)
    wanted = (iota((QP, LEN), 0) + (LEN - PRED)).astype(f32)
    slot_hot[s] = (rank_row == wanted).astype(bf16)


def project_group(x, weights, vectors, g, qkv_ref):
    cols = pl.ds(pl.multiple_of(g * GROUP, 128), GROUP)
    bias_q = vectors[0:1, cols]
    bias_v = vectors[1:2, cols]
    eighth = jnp.asarray(0.125, bf16)
    rows = jnp.dot(x[:LEN], weights, preferred_element_type=f32)
    qkv_ref[0, 0, :LEN, :GROUP] = (rows[:, :GROUP] + bias_q).astype(bf16) * eighth
    qkv_ref[0, 0, :LEN, GROUP : 2 * GROUP] = rows[:, GROUP : 2 * GROUP].astype(bf16)
    qkv_ref[0, 0, :LEN, 2 * GROUP :] = (rows[:, 2 * GROUP :] + bias_v).astype(bf16)
    rows = jnp.dot(x[LEN:], weights[:, :GROUP], preferred_element_type=f32)
    qkv_ref[0, 0, LEN:, :GROUP] = (rows + bias_q).astype(bf16) * eighth


def attend_pair(s, hp, j, qkv_ref, o_ref, ol_ref, r_ref, p_ref, full, near, far, scores, row_mark, key_mark, slot_hot):
    q2 = qkv_ref[0, 0, :, pl.ds(pl.multiple_of(j * 128, 128), 128)]
    k2 = qkv_ref[0, 0, :LEN, pl.ds(pl.multiple_of(GROUP + j * 128, 128), 128)]
    v2 = qkv_ref[0, 0, :LEN, pl.ds(pl.multiple_of(2 * GROUP + j * 128, 128), 128)]
    half = iota((LEN, 128), 1) // 64
    left = jnp.concatenate([q2, row_mark[s]], axis=1)
    for h in range(2):
        right = jnp.concatenate([jnp.where(half == h, k2, jnp.zeros_like(k2)), key_mark[s]], axis=1)
        scores[h, :LEN] = lax.dot_general(left[:LEN], right, NT, preferred_element_type=f32)
        scores[h, LEN:] = lax.dot_general(left[LEN:], right, NT, preferred_element_type=f32) + jnp.dot(
            slot_hot[s], full[2 * hp + h], preferred_element_type=f32
        )
    for h in range(2):
        head = 2 * hp + h
        for bi in range(4):
            rows = slice(bi * 128, bi * 128 + 128)
            tiles = []
            for bj in range(4):
                d = bj - bi
                bias = near[head, d + 1] if abs(d) < 2 else far[head, 8:9] if d > 0 else far[head, 0:1]
                tiles.append(scores[h, rows, bj * 128 : (bj + 1) * 128] + bias)
            biased = jnp.concatenate(tiles, axis=1)
            peak = jnp.max(biased, axis=1, keepdims=True)
            p_ref[0, h, rows] = jnp.exp(biased - peak).astype(bf16)
        biased = scores[h, LEN:]
        peak = jnp.max(biased, axis=1, keepdims=True)
        p_ref[0, h, LEN:] = jnp.exp(biased - peak).astype(bf16)
    mixed = []
    for h in range(2):
        vm = jnp.where(half == h, v2, jnp.ones_like(v2))
        mixed.append(jnp.dot(p_ref[0, h], vm, preferred_element_type=f32))
    low = iota((R, 128), 1) < 64
    inverse = 1.0 / pltpu.roll(jnp.where(low, mixed[1], mixed[0]), 64, 1)
    out = jnp.where(low, mixed[0], mixed[1]) * inverse
    out_low = out.astype(bf16)
    o_ref[0] = out_low
    ol_ref[0] = (out - out_low.astype(f32)).astype(bf16)
    r_ref[0] = inverse


def forward_kernel(remote, n, *refs):
    if remote:
        (
            perm_ref, content_ref, query_ref, raw_ref, wq, wk, wv, wo, w1, w2,
            qkv_ref, o_ref, ol_ref, r_ref, p_ref, g_ref, slope_ref, unit_ref, inv_ref, a_ref,
            vec_ref, wqkv_out, wo_out, w1_out, w2_out,
            full, near, far, scores, row_mark, key_mark, slot_hot, x_all, o_all, low_all, x_sem,
            wo_all, w1_all, wqkv, own_qkv, vec_send, vec_recv, local_sem, send, recv, vec_send_sem, vec_recv_sem,
        ) = refs
    else:
        (
            perm_ref, content_ref, query_ref, vec_in, wqkv, wo_all, w1_all,
            qkv_ref, o_ref, ol_ref, r_ref, p_ref, g_ref, slope_ref, unit_ref, inv_ref, a_ref,
            full, near, far, scores, row_mark, key_mark, slot_hot, x_all, o_all, low_all, x_sem,
        ) = refs
    step = pl.program_id(0)
    g, s, j = attention_step(step, n)
    attention_steps = 6 * n
    last = attention_steps + 2 * n - 1

    x_load = pltpu.make_async_copy(content_ref, x_all.at[:, :LEN], x_sem)

    @pl.when(step == 0)
    def _():
        x_load.start()
        place_queries(n, query_ref, x_all)

    if remote:
        z, x_at, c, y = place()
        shard = D // 16
        items = {}
        for i in range(3):
            items[f"g{i}"] = Gather(wqkv.at[i], (0, shard), (0, D), send, recv, i)
        items["o"] = Gather(wo_all, (0, shard), (0, D), send, recv, 3)
        items["1a"] = Gather(w1_all, (0, shard), (0, FF // 2), send, recv, 4)
        items["1b"] = Gather(w1_all, (0, shard), (FF // 2, FF // 2), send, recv, 5)
        items["2a"] = Gather(w2_out, (0, 96), (0, D), send, recv, 6)
        items["2b"] = Gather(w2_out, (96, 96), (0, D), send, recv, 7)
        own = []
        for part, whole, cols in (
            (wo, wo_all, (0, D)), (w1, w1_all, (0, FF // 2)), (w1, w1_all, (FF // 2, FF // 2)), (w2, w2_out, (0, D)),
        ):
            half = half_of(y, cols)
            own.append(
                pltpu.make_async_copy(part.at[:, half], whole.at[z, x_at, c, :, half], local_sem.at[len(own)])
            )

        def vec_copy(k):
            other = (
                device(z, x_at, 1 - c, y), device(z, 1 - x_at, c, y), device(z, 1 - x_at, 1 - c, y),
                *(device((z + t) % 4, x_at, c, y) for t in (1, 2, 3)),
            )[k]
            return pltpu.make_async_remote_copy(
                src_ref=vec_send.at[k // 3], dst_ref=vec_recv.at[k],
                send_sem=vec_send_sem.at[k], recv_sem=vec_recv_sem.at[k], device_id=other, device_id_type=MESH,
            )

        @pl.when(step == 0)
        def _():
            greet()
            half = half_of(y, (0, D))
            for i in range(3):
                for m, part in enumerate((wq, wk, wv)):
                    own_qkv[i, :, m * GROUP : (m + 1) * GROUP] = part[:, i * GROUP : (i + 1) * GROUP]
                wqkv[i, z, x_at, c, :, half] = own_qkv[i, :, half]
            items["g0"].step(0)
            for copy in own:
                copy.start()
            vec_send[0] = spread_vectors(raw_ref[...], z * 4 + x_at * 2 + c)
            for k in (0, 1, 2):
                vec_copy(k).start()
            build_marks(0, perm_ref[0:1], row_mark, key_mark, slot_hot)
            items["g0"].step(1)
            items["g1"].step(0)
            items["g2"].step(0)
            for k in (0, 1, 2):
                vec_copy(k).wait_recv()
            vec_send[1] = vec_send[0] + vec_recv[0] + vec_recv[1] + vec_recv[2]
            for k in (3, 4, 5):
                vec_copy(k).start()
            items["g0"].step(2)
            for i in range(1, n):
                build_marks(i, perm_ref[i : i + 1], row_mark, key_mark, slot_hot)
            items["g1"].step(1)
            for copy in own:
                copy.wait()
            items["o"].step(0)
            for k in (3, 4, 5):
                vec_copy(k).wait_recv()
            vec_ref[...] = vec_send[1] + vec_recv[3] + vec_recv[4] + vec_recv[5]
            items["g0"].step(3)
            build_bias(vec_ref[...], full, near, far)
            items["g2"].step(1)
            items["1a"].step(0)
            items["g1"].step(2)
            items["g0"].step(4)

        back = [
            pltpu.make_async_copy(here, there, local_sem.at[i])
            for i, (here, there) in enumerate(((wqkv, wqkv_out), (wo_all, wo_out), (w1_all, w1_out)))
        ]

        @pl.when(step == attention_steps)
        def _():
            for copy in back:
                copy.start()

        for at in sorted({a for steps in GATHER_STEPS.values() for a in steps if 0 <= a <= last}):

            @pl.when(step == at)
            def _(at=at):
                for stage in range(5):
                    for name, steps in GATHER_STEPS.items():
                        if steps[stage] == at:
                            items[name].step(stage)
        vectors = vec_ref
    else:
        vectors = vec_in

        @pl.when(step == 0)
        def _():
            for i in range(n):
                build_marks(i, perm_ref[i : i + 1], row_mark, key_mark, slot_hot)
            build_bias(vec_in[...], full, near, far)

    @pl.when(step == 0)
    def _():
        x_load.wait()

    @pl.when((step < attention_steps) & (j == 0))
    def _():
        weights = wqkv[g].reshape(D, D) if remote else wqkv[g]
        project_group(x_all[s], weights, vectors, g, qkv_ref)

    @pl.when(step < attention_steps)
    def _():
        attend_pair(
            s, 2 * g + j, j, qkv_ref, o_ref, ol_ref, r_ref, p_ref,
            full, near, far, scores, row_mark, key_mark, slot_hot,
        )
        o_all[s, :, pl.ds(pl.multiple_of((2 * g + j) * 128, 128), 128)] = o_ref[0]

    def before_ffn(s):
        y1 = x_all[s].astype(f32) + vectors[2:3] + jnp.dot(
            o_all[s], wo_all[...].reshape(D, D), preferred_element_type=f32
        )
        unit, inv = norm_parts(y1)
        unit_ref[0] = unit
        inv_ref[0] = jnp.broadcast_to(inv, (R, 128))
        low = (unit * vectors[3:4] + vectors[4:5]).astype(bf16)
        a_ref[0] = low
        low_all[s % 2] = low

    def first_ffn(s, part):
        for i in range(2):
            cols = slice(i * D, (i + 1) * D)
            at = (2 * part + i) * D
            weights = w1_all[:, :, :, :, at : at + D].reshape(D, D) if remote else w1_all[:, at : at + D]
            hidden = jnp.dot(low_all[s % 2], weights, preferred_element_type=f32)
            hidden = hidden + vectors[8 + 2 * part + i : 9 + 2 * part + i]
            g_ref[0, :, cols], slope_ref[0, :, cols] = gelu_parts(hidden)

    @pl.when(step == attention_steps - 1)
    def _():
        before_ffn(0)

    for after in range(n):

        @pl.when(step == attention_steps + 2 * after)
        def _(after=after):
            first_ffn(after, 0)

        @pl.when(step == attention_steps + 2 * after + 1)
        def _(after=after):
            first_ffn(after, 1)
            if after < n - 1:
                before_ffn(after + 1)

    if remote:

        @pl.when(step == last)
        def _():
            for stage in range(5):
                for name, steps in GATHER_STEPS.items():
                    if steps[stage] > last:
                        items[name].step(stage)
            for k in range(6):
                vec_copy(k).wait_send()
            for item in items.values():
                item.drain()
            for copy in back:
                copy.wait()


def place_queries(n, query_ref, x_all):
    x_all[:, R - 16 :] = jnp.zeros((n, 16, D), bf16)
    for i in range(n):
        x_all[i, LEN : LEN + PRED] = query_ref[i]


def attention_step(step, n):
    t = jnp.minimum(step, 6 * n - 1)
    return t // (2 * n), (t // 2) % n, t % 2


def after_step(step, n):
    t = jnp.maximum(step - 6 * n, 0)
    return t // 2, t % 2


def norm_parts(values):
    centered = values - jnp.mean(values, axis=-1, keepdims=True)
    inv = lax.rsqrt(jnp.mean(centered * centered, axis=-1, keepdims=True) + eps_norm)
    return centered * inv, inv


def gelu_parts(hidden):
    phi = 0.5 + 0.5 * lax.erf(hidden * inverse_root)
    bell = jnp.exp(-0.5 * hidden * hidden) * density_scale
    return (hidden * phi).astype(bf16), (phi + hidden * bell).astype(bf16)


def forward_call(n, remote, *operands):
    sds = jax.ShapeDtypeStruct

    def pair(step):
        g, s, j = attention_step(step, n)
        return (s, 0, 2 * g + j)

    def group(step):
        g, s, j = attention_step(step, n)
        return (g, s, 0, 0)

    def pair_scores(step):
        g, s, j = attention_step(step, n)
        return (s, 2 * g + j, 0, 0)

    def after(step):
        s, part = after_step(step, n)
        return (s, 0, part)

    def after_whole(step):
        return (jnp.clip((step - 6 * n + 1) // 2, 0, n - 1), 0, 0)

    out_specs = [
        pl.BlockSpec((1, 1, R, D), group), *[pl.BlockSpec((1, R, 128), pair)] * 3,
        pl.BlockSpec((1, 2, R, LEN), pair_scores),
        *[pl.BlockSpec((1, R, FF // 2), after)] * 2,
        pl.BlockSpec((1, R, D), after_whole), pl.BlockSpec((1, R, 128), after_whole), pl.BlockSpec((1, R, D), after_whole),
    ]
    out_shape = [
        sds((3, n, R, D), bf16), sds((n, R, D), bf16), sds((n, R, D), bf16), sds((n, R, D), f32),
        sds((n, HEADS, R, LEN), bf16), sds((n, R, FF), bf16), sds((n, R, FF), bf16), sds((n, R, D), f32),
        sds((n, R, 128), f32), sds((n, R, D), bf16),
    ]
    scratch = [
        pltpu.VMEM((HEADS, LEN, LEN), bf16),
        pltpu.VMEM((HEADS, 3, 128, 128), f32),
        pltpu.VMEM((HEADS, 16, 128), f32),
        pltpu.VMEM((2, R, LEN), f32),
        pltpu.VMEM((n, R, 128), bf16),
        pltpu.VMEM((n, LEN, 128), bf16),
        pltpu.VMEM((n, QP, LEN), bf16),
        pltpu.VMEM((n, R, D), bf16),
        pltpu.VMEM((n, R, D), bf16),
        pltpu.VMEM((2, R, D), bf16),
        pltpu.SemaphoreType.DMA,
    ]
    if remote:
        in_specs = [VMEM_WHOLE, ANYWHERE] + [VMEM_WHOLE] * 8
        out_specs += [pl.BlockSpec((16, D), lambda step: (0, 0))] + [ANYWHERE] * 4
        block = (4, 2, 2, D // 16)
        out_shape += [
            sds((16, D), f32), sds((3, *block, D), bf16), sds((*block, D), bf16), sds((*block, FF), bf16),
            sds((4, 2, 2, FF // 16, D), bf16),
        ]
        scratch += [
            pltpu.VMEM((*block, D), bf16),
            pltpu.VMEM((*block, FF), bf16),
            pltpu.VMEM((3, *block, D), bf16),
            pltpu.VMEM((3, D // 16, D), bf16),
            pltpu.VMEM((2, 16, D), f32),
            pltpu.VMEM((6, 16, D), f32),
            pltpu.SemaphoreType.DMA((4,)),
            pltpu.SemaphoreType.DMA((8, 8)),
            pltpu.SemaphoreType.DMA((8, 8)),
            pltpu.SemaphoreType.DMA((6,)),
            pltpu.SemaphoreType.DMA((6,)),
        ]
        params = pltpu.CompilerParams(vmem_limit_bytes=VMEM_LIMIT, collective_id=1, has_side_effects=True)
    else:
        in_specs = [VMEM_WHOLE, ANYWHERE] + [VMEM_WHOLE] * 5
        params = pltpu.CompilerParams(vmem_limit_bytes=VMEM_LIMIT)
    return pl.pallas_call(
        functools.partial(forward_kernel, remote, n),
        grid=(8 * n,),
        in_specs=in_specs,
        out_specs=out_specs,
        out_shape=out_shape,
        scratch_shapes=scratch,
        compiler_params=params,
        name="attention_forward",
    )(*operands)


def norm_back(grad, unit, inv, gain):
    scaled = grad * gain
    return inv * (
        scaled - jnp.mean(scaled, axis=-1, keepdims=True) - unit * jnp.mean(scaled * unit, axis=-1, keepdims=True)
    )


def column_sum(values):
    return jnp.sum(values.astype(f32), axis=0, keepdims=True)


def middle_kernel(
    n, unit_ref, inv_ref, g_ref, slope_ref, content_cot, query_cot, vec, wo_hbm, w1_hbm, w2_hbm,
    content_out, query_out, d2_ref, dh_ref, d1_ref, do_ref, dy_ref, sums,
    wo, w1, w2, padded, sem,
):
    s = pl.program_id(0)
    loads = [
        pltpu.make_async_copy(there, here, sem.at[i])
        for i, (there, here) in enumerate(((w2_hbm, w2), (w1_hbm, w1), (wo_hbm, wo)))
    ]

    @pl.when(s == 0)
    def _():
        for copy in loads:
            copy.start()
        sums[...] = jnp.zeros_like(sums)
        padded[PRED - PRED % 8 :] = jnp.zeros((QP - PRED + PRED % 8, D), f32)
        loads[0].wait()

    padded[:PRED] = query_cot[0].astype(f32)
    unit1 = unit_ref[0]
    normed = unit1 * vec[3:4] + vec[4:5]
    y2 = normed + vec[5:6] + jnp.dot(g_ref[0], w2[...], preferred_element_type=f32)
    unit2, inv2 = norm_parts(y2)
    out = (unit2 * vec[6:7] + vec[7:8]).astype(bf16)
    content_out[0] = out[:LEN]
    query_out[0] = out[LEN : LEN + PRED]
    cot = jnp.concatenate([content_cot[0].astype(f32), padded[...]], axis=0)
    sums[7:8] += column_sum(cot)
    sums[6:7] += column_sum(cot * unit2)
    back2 = norm_back(cot, unit2, inv2, vec[6:7])
    d2 = back2.astype(bf16)
    d2_ref[0] = d2
    sums[5:6] += column_sum(d2)

    @pl.when(s == 0)
    def _():
        loads[1].wait()
        loads[2].wait()

    da = back2
    for i in range(FF // D):
        cols = slice(i * D, (i + 1) * D)
        dg = lax.dot_general(d2, w2[cols], NT, preferred_element_type=f32)
        dh = (dg * slope_ref[0, :, cols].astype(f32)).astype(bf16)
        dh_ref[0, :, cols] = dh
        sums[8 + i : 9 + i] += column_sum(dh)
        da = da + lax.dot_general(dh, w1[:, cols], NT, preferred_element_type=f32)
    sums[4:5] += column_sum(da)
    sums[3:4] += column_sum(da * unit1)
    back1 = norm_back(da, unit1, inv_ref[0, :, :1], vec[3:4])
    dy_ref[0] = back1
    d1 = back1.astype(bf16)
    d1_ref[0] = d1
    sums[2:3] += column_sum(d1)
    do_ref[0] = lax.dot_general(d1, wo[...], NT, preferred_element_type=f32).astype(bf16)


def middle_call(n, unit1, inv1, act, slope, content_cot, query_cot, vec, wo, w1, w2):
    sds = jax.ShapeDtypeStruct

    def rows(count, width):
        return pl.BlockSpec((1, count, width), lambda s: (s, 0, 0))

    small = pl.BlockSpec((16, D), lambda s: (0, 0))
    return pl.pallas_call(
        functools.partial(middle_kernel, n),
        grid=(n,),
        in_specs=[rows(R, D), rows(R, 128), rows(R, FF), rows(R, FF), rows(LEN, D), rows(PRED, D), small]
        + [ANYWHERE] * 3,
        out_specs=[rows(LEN, D), rows(PRED, D), rows(R, D), rows(R, FF), rows(R, D), rows(R, D), rows(R, D), small],
        out_shape=[
            sds((n, LEN, D), bf16), sds((n, PRED, D), bf16), sds((n, R, D), bf16), sds((n, R, FF), bf16),
            sds((n, R, D), bf16), sds((n, R, D), bf16), sds((n, R, D), f32), sds((16, D), f32),
        ],
        scratch_shapes=[
            pltpu.VMEM((D, D), bf16), pltpu.VMEM((D, FF), bf16), pltpu.VMEM((FF, D), bf16),
            pltpu.VMEM((QP, D), f32), pltpu.SemaphoreType.DMA((3,)),
        ],
        compiler_params=pltpu.CompilerParams(vmem_limit_bytes=VMEM_LIMIT),
        name="middle",
    )(unit1, inv1, act, slope, content_cot, query_cot, vec, wo, w1, w2)


def weight_kernel(n, act, dh, d2, low1, o, d1, w1_grad, w2_grad, wo_grad, left, right, low, sem):
    step = pl.program_id(0)
    chunks = FF // D
    low_load = pltpu.make_async_copy(low1, low, sem.at[0])
    left_load = pltpu.make_async_copy(o, left, sem.at[1])
    right_load = pltpu.make_async_copy(d1, right, sem.at[2])
    d2_load = pltpu.make_async_copy(d2, right, sem.at[3])

    def outer(a, b):
        return lax.dot_general(
            a[...].reshape(n * R, D), b[...].reshape(n * R, D), TN, preferred_element_type=f32
        ).astype(bf16)

    @pl.when(step == 0)
    def _():
        d2_load.start()
        d2_load.wait()
        low_load.start()

    @pl.when(step < chunks)
    def _():
        w2_grad[...] = outer(act, right)

    @pl.when(step == chunks)
    def _():
        low_load.wait()
        left_load.start()
        right_load.start()

    @pl.when((step >= chunks) & (step < 2 * chunks))
    def _():
        w1_grad[...] = outer(low, dh)

    @pl.when(step == 2 * chunks)
    def _():
        left_load.wait()
        right_load.wait()
        wo_grad[...] = outer(left, right)


def weight_call(n, act, dh, d2, low1, o, d1):
    sds = jax.ShapeDtypeStruct
    chunks = FF // D

    def first(step):
        return jnp.minimum(step, chunks - 1)

    def second(step):
        return jnp.clip(step - chunks, 0, chunks - 1)

    return pl.pallas_call(
        functools.partial(weight_kernel, n),
        grid=(2 * chunks + 1,),
        in_specs=[
            pl.BlockSpec((n, R, D), lambda step: (0, 0, first(step))),
            pl.BlockSpec((n, R, D), lambda step: (0, 0, second(step))),
            ANYWHERE, ANYWHERE, ANYWHERE, ANYWHERE,
        ],
        out_specs=[
            pl.BlockSpec((D, D), lambda step: (0, second(step))),
            pl.BlockSpec((D, D), lambda step: (first(step), 0)),
            pl.BlockSpec((D, D), lambda step: (0, 0)),
        ],
        out_shape=[sds((D, FF), bf16), sds((FF, D), bf16), sds((D, D), bf16)],
        scratch_shapes=[pltpu.VMEM((n, R, D), bf16)] * 3 + [pltpu.SemaphoreType.DMA((4,))],
        compiler_params=pltpu.CompilerParams(vmem_limit_bytes=VMEM_LIMIT),
        name="weight_gradients",
    )(act, dh, d2, low1, o, d1)

REDUCE_STEPS = {
    "2a": (0, 1, 5, 8, 12, 15),
    "2b": (0, 3, 7, 10, 14, 17),
    "1a": (2, 6, 10, 13, 17, 18),
    "1b": (4, 9, 13, 16, 18, 18),
    "o": (7, 11, 15, 17, 18, 18),
    "g0": (8, 13, 16, 18, 18, 18),
    "g1": (13, 15, 17, 18, 18, 18),
    "g2": (18, 18, 18, 18, 18, 18),
}


def add(a, b):
    return (a.astype(f32) + b.astype(f32)).astype(bf16)


class Reduce:
    @staticmethod
    def scratch(rows, cols, loads):
        half = cols // 2
        shapes = [
            (4, 2, rows, cols), (2, 2, rows, half), (2, rows, cols), (2, rows, half), (2, rows, half),
            (4, rows, half), (3, rows, half),
        ]
        if loads:
            shapes.append((4, 2, rows, cols))
        return [pltpu.VMEM(shape, bf16) for shape in shapes]

    def __init__(self, source, at, rows, cols, bufs, out, send, recv, load, item):
        self.source, self.at, self.rows, self.cols = source, at, rows, cols
        self.rc, self.ry, self.rx, self.sx, self.sy, self.a3, self.rz = bufs[:7]
        self.own = bufs[7] if len(bufs) > 7 else None
        self.out, self.send, self.recv, self.load, self.item = out, send, recv, load, item

    def part(self, core):
        rows = pl.ds(self.at[0], self.rows)
        cols = pl.ds(self.at[1], self.cols)
        return self.source.at[:, :, core, rows, cols]

    def load_copy(self):
        z, x, c, y = place()
        return pltpu.make_async_copy(self.part(c), self.own, self.load)

    def copies(self, stage):
        z, x, c, y = place()
        half = self.cols // 2
        other_half = pl.ds(pl.multiple_of((1 - y) * half, 128), half)

        def copy(index, src, dst, other):
            return pltpu.make_async_remote_copy(
                src_ref=src, dst_ref=dst,
                send_sem=self.send.at[self.item, index], recv_sem=self.recv.at[self.item, index],
                device_id=other, device_id_type=MESH,
            )

        if stage == 0:
            return [copy(0, self.part(1 - c), self.rc, device(z, x, 1 - c, y))]
        if stage == 1:
            return [
                copy(1, self.rc.at[0:2, :, :, other_half], self.ry, device(z, x, c, 1 - y)),
                copy(2, self.rc.at[2:4, 1 - x], self.rx, device(z, 1 - x, c, y)),
            ]
        if stage == 2:
            return [
                copy(3, self.ry.at[:, 1 - x], self.sx, device(z, 1 - x, c, y)),
                copy(4, self.rx.at[:, :, other_half], self.sy, device(z, x, c, 1 - y)),
            ]
        if stage == 3:
            return [
                copy(4 + k, self.a3.at[(z + k) % 4], self.rz.at[k - 1], device((z + k) % 4, x, c, y))
                for k in (1, 2, 3)
            ]
        return [copy(8, self.out.at[y], self.out.at[y], device(z, x, c, 1 - y))]

    def combine(self, stage):
        z, x, c, y = place()
        half = self.cols // 2
        own_half = pl.ds(pl.multiple_of(y * half, 128), half)
        if stage == 0:
            if self.own is not None:
                self.load_copy().wait()
            for i in range(4):
                for k in range(2):
                    mine = self.own[i, k] if self.own is not None else self.source[i, k, c]
                    self.rc[i, k] = add(self.rc[i, k], mine)
        elif stage == 1:
            for i in range(2):
                for k in range(2):
                    self.ry[i, k] = add(self.ry[i, k], self.rc[i, k, :, own_half])
                self.rx[i] = add(self.rx[i], self.rc[2 + i, x])
        elif stage == 2:
            for i in range(2):
                self.a3[i] = add(self.sx[i], self.ry[i, x])
                self.a3[2 + i] = add(self.sy[i], self.rx[i, :, own_half])
        elif stage == 3:
            total = self.a3[z].astype(f32)
            for k in range(3):
                total = total + self.rz[k].astype(f32)
            self.out[y] = total.astype(bf16)

    def step(self, stage):
        if stage == 0 and self.own is not None:
            self.load_copy().start()
        if stage > 0:
            for copy in self.copies(stage - 1):
                copy.wait_recv()
            if stage < 5:
                self.combine(stage - 1)
        if stage < 5:
            for copy in self.copies(stage):
                copy.start()

    def drain(self):
        for stage in range(5):
            for copy in self.copies(stage):
                copy.wait_send()


def reduce_table(group, n, slot_cols, kept, near_sum, far_sum):
    c = iota((896, 128), 0)
    rel = jnp.where(c < 768, 128 * (c // 256 - 1) + c % 256 - 128, jnp.where(c % 128 < 64, -200, 200))
    onehot = (bucket_index(rel) == iota((896, 128), 1)).astype(f32)
    slots = jnp.concatenate([slot_cols[i] for i in range(n)], axis=1)
    sub = iota((8, 256), 0)
    lane8 = iota((8, 128), 1)
    lane1 = iota((1, 128), 1)
    rows = []
    for head in range(4):
        moved = jnp.dot(slots, kept[head], preferred_element_type=f32)
        near = [near_sum[head, d] for d in range(3)]
        far = [far_sum[head, 0:8], far_sum[head, 8:16]]
        for bi in range(4):
            for bj in range(4):
                d = bj - bi
                tile = moved[bi * 128 : (bi + 1) * 128, bj * 128 : (bj + 1) * 128]
                if abs(d) < 2:
                    near[d + 1] = near[d + 1] + tile
                else:
                    far[int(d > 0)] = far[int(d > 0)] + tile.reshape(16, 8, 128).sum(0)
        parts = []
        for d in range(3):
            high = low = None
            for a in range(16):
                x = near[d][8 * a : 8 * a + 8]
                if a:
                    x = pltpu.roll(x, 128 - 8 * a, 1)
                keep = lane8 < 128 - 8 * a
                u = jnp.where(keep, x, 0.0)
                w = jnp.where(keep, 0.0, x)
                high = u if high is None else high + u
                low = w if low is None else low + w
            y = jnp.concatenate([low, high], axis=1)
            for k in (1, 2, 4):
                y = jnp.where((sub & k) != 0, pltpu.roll(y, 256 - k, 1), y)
            parts.append(jnp.sum(y, axis=0, keepdims=True))
        parts.append(jnp.where(lane1 == 0, jnp.sum(far[0]), jnp.where(lane1 == 64, jnp.sum(far[1]), 0.0)))
        rows.append(jnp.concatenate(parts, axis=1))
    rows.append(jnp.zeros((4, 896), f32))
    return jnp.dot(
        jnp.concatenate(rows, axis=0), onehot, preferred_element_type=f32, precision=lax.Precision.HIGHEST
    )


def table_row(by_head):
    spread = (iota((128, D), 0) == iota((128, D), 1) // HEADS).astype(f32)
    wide = jnp.dot(by_head, spread, preferred_element_type=f32, precision=lax.Precision.HIGHEST)
    lane = iota((16, D), 1)
    mine = (lane % HEADS == iota((16, D), 0)) & (lane < BUCKETS * HEADS)
    return jnp.sum(jnp.where(mine, wide, 0.0), axis=0, keepdims=True)


def attend_pair_back(
    s, hp, j, qkv_ref, o_ref, ol_ref, r_ref, p_ref, do_ref, dqkv, dp, ds, kept, near_sum, far_sum
):
    q2 = qkv_ref[0, 0, :, pl.ds(pl.multiple_of(j * 128, 128), 128)]
    k2 = qkv_ref[0, 0, :LEN, pl.ds(pl.multiple_of(GROUP + j * 128, 128), 128)]
    v2 = qkv_ref[0, 0, :LEN, pl.ds(pl.multiple_of(2 * GROUP + j * 128, 128), 128)]
    delta = (do_ref[0].astype(f32) * r_ref[0]).astype(bf16)
    prod = delta.astype(f32) * (o_ref[0].astype(f32) + ol_ref[0].astype(f32))
    high = prod.astype(bf16)
    rest = pltpu.roll(prod - high.astype(f32), 64, 1).astype(bf16)
    low = iota((R, 128), 1) < 64
    half = iota((LEN, 128), 1) // 64
    extra = [jnp.where(low, high, rest), jnp.where(low, rest, high)]
    minus = jnp.full((LEN, 128), -1.0, bf16)
    for h in range(2):
        vm = jnp.where(half == h, v2, jnp.zeros_like(v2))
        dp[h] = lax.dot_general(
            jnp.concatenate([delta, extra[h]], axis=1),
            jnp.concatenate([vm, minus], axis=1),
            NT,
            preferred_element_type=f32,
        )
    for h in range(2):
        head = 2 * j + h
        far = [None, None]
        for bi in range(4):
            rows = slice(bi * 128, bi * 128 + 128)
            d_rows = p_ref[0, h, rows].astype(f32) * dp[h, rows]
            ds[h, rows] = d_rows.astype(bf16)
            for bj in range(4):
                d = bj - bi
                tile = d_rows[:, bj * 128 : (bj + 1) * 128]
                if abs(d) < 2:
                    near_sum[head, d + 1] += tile
                else:
                    part = tile.reshape(16, 8, 128).sum(0)
                    far[int(d > 0)] = part if far[int(d > 0)] is None else far[int(d > 0)] + part
        far_sum[head, 0:8] += far[0]
        far_sum[head, 8:16] += far[1]
        d_slots = (p_ref[0, h, LEN:].astype(f32) * dp[h, LEN:]).astype(bf16)
        ds[h, LEN:] = d_slots
        kept[head, pl.ds(pl.multiple_of(s * QP, 16), QP)] = d_slots
    dq = None
    for h in range(2):
        km = jnp.where(half == h, k2, jnp.zeros_like(k2))
        part = jnp.dot(ds[h], km, preferred_element_type=f32)
        dq = part if dq is None else dq + part
    dqkv[s, :, pl.ds(pl.multiple_of(j * 128, 128), 128)] = (dq * 0.125).astype(bf16)
    q_t = jnp.transpose(q2)
    delta_t = jnp.transpose(delta)
    dk_t = [jnp.dot(q_t[h * 64 : (h + 1) * 64], ds[h], preferred_element_type=f32) for h in range(2)]
    dv_t = [jnp.dot(delta_t[h * 64 : (h + 1) * 64], p_ref[0, h], preferred_element_type=f32) for h in range(2)]
    dqkv[s, :LEN, pl.ds(pl.multiple_of(GROUP + j * 128, 128), 128)] = jnp.transpose(
        jnp.concatenate(dk_t, axis=0).astype(bf16)
    )
    dqkv[s, :LEN, pl.ds(pl.multiple_of(2 * GROUP + j * 128, 128), 128)] = jnp.transpose(
        jnp.concatenate(dv_t, axis=0).astype(bf16)
    )


def backward_kernel(remote, n, *refs):
    (
        perm_ref, content_ref, query_ref, wqkv, vec_in, qkv_ref, o_ref, ol_ref, r_ref, p_ref, do_ref, dy_ref,
        *refs,
    ) = refs
    if remote:
        (
            wo_grad, w1_grad, w2_grad,
            dx_ref, vec_ref, g_out, o_out, w1_out, w2_out,
            dx, dqkv, dp, ds, kept, slot_cols, near_sum, far_sum, tab, x_all, dy_sem, x_sem,
            wqkv_grad, g_sum, o_sum, w1_sum, w2_sum, vec_send, vec_recv, load_sem, send, recv, vec_send_sem, vec_recv_sem,
            *bufs,
        ) = refs
    else:
        (
            dx_ref, vec_ref, wqkv_grad,
            dx, dqkv, dp, ds, kept, slot_cols, near_sum, far_sum, tab, x_all, dy_sem, x_sem,
        ) = refs
    g = pl.program_id(0)
    s = pl.program_id(1)
    j = pl.program_id(2)
    step = (g * n + s) * 2 + j
    last = 3 * n * 2 - 1
    loads = [
        pltpu.make_async_copy(dy_ref, dx, dy_sem),
        pltpu.make_async_copy(content_ref, x_all.at[:, :LEN], x_sem),
    ]

    if remote:
        z, x_at, c, y = place()
        shard = D // 16
        wide = 2 * FF // 4

        def item(name, index, source, at, rows, cols, out):
            first = index * 8 if index < 5 else 40 + (index - 5) * 7
            take = 8 if index < 5 else 7
            return Reduce(
                source, at, rows, cols, bufs[first : first + take], out, send, recv,
                load_sem.at[index] if index < 5 else None, index,
            )

        items = {
            "2a": item("2a", 0, w2_grad, (0, 0), 96, D, w2_sum.at[0]),
            "2b": item("2b", 1, w2_grad, (96, 0), 96, D, w2_sum.at[1]),
            "1a": item("1a", 2, w1_grad, (0, 0), shard, wide, w1_sum.at[0]),
            "1b": item("1b", 3, w1_grad, (0, wide), shard, wide, w1_sum.at[1]),
            "o": item("o", 4, wo_grad, (0, 0), shard, D, o_sum),
        }
        for i in range(3):
            items[f"g{i}"] = item(f"g{i}", 5 + i, wqkv_grad.at[i], (0, 0), shard, D, g_sum.at[i])

        def vec_copy(k):
            other = (
                device(z, x_at, 1 - c, y),
                device(z, x_at, c, 1 - y), device(z, 1 - x_at, c, y), device(z, 1 - x_at, c, 1 - y),
                *(device((z + t) % 4, x_at, c, y) for t in (1, 2, 3)),
            )[k]
            return pltpu.make_async_remote_copy(
                src_ref=vec_send.at[0 if k == 0 else 1 if k < 4 else 2], dst_ref=vec_recv.at[k],
                send_sem=vec_send_sem.at[k], recv_sem=vec_recv_sem.at[k], device_id=other, device_id_type=MESH,
            )

    @pl.when(step == 0)
    def _():
        for copy in loads:
            copy.start()
        if remote:
            greet()
        place_queries(n, query_ref, x_all)
        vec_ref[...] = vec_in[...]
        for i in range(n):
            rank = ranking_column(perm_ref[i : i + 1])
            slot_cols[i] = (rank == (iota((LEN, QP), 1) + (LEN - PRED)).astype(f32)).astype(bf16)
        dqkv[:, LEN:, GROUP:] = jnp.zeros((n, QP, 2 * GROUP), bf16)

    if remote:
        for at in sorted({a for steps in REDUCE_STEPS.values() for a in steps if a <= last}):

            @pl.when(step == at)
            def _(at=at):
                for stage in range(6):
                    for name, steps in REDUCE_STEPS.items():
                        if steps[stage] == at:
                            items[name].step(stage)

    @pl.when((s == 0) & (j == 0))
    def _():
        near_sum[...] = jnp.zeros_like(near_sum)
        far_sum[...] = jnp.zeros_like(far_sum)

    attend_pair_back(
        s, 2 * g + j, j, qkv_ref, o_ref, ol_ref, r_ref, p_ref, do_ref, dqkv, dp, ds, kept, near_sum, far_sum
    )

    @pl.when(step == 1)
    def _():
        for copy in loads:
            copy.wait()

    @pl.when((s == n - 1) & (j == 1))
    def _():
        total = lax.dot_general(
            x_all[...].reshape(n * R, D), dqkv[...].reshape(n * R, D), TN, preferred_element_type=f32
        ).astype(bf16)
        wqkv_grad[g] = total.reshape(4, 2, 2, D // 16, D) if remote else total

    if remote:

        @pl.when(step == last)
        def _():
            items["g2"].step(0)

    @pl.when(j == 1)
    def _():
        weights = wqkv[g]
        dx[s] += lax.dot_general(dqkv[s], weights, NT, preferred_element_type=f32)

    @pl.when((s == n - 1) & (j == 1))
    def _():
        tab[g] = reduce_table(g, n, slot_cols, kept, near_sum, far_sum)
        sums = jnp.sum(dqkv[0].astype(f32), axis=0, keepdims=True)
        for i in range(1, n):
            sums = sums + jnp.sum(dqkv[i].astype(f32), axis=0, keepdims=True)
        cols = pl.ds(pl.multiple_of(g * GROUP, 128), GROUP)
        vec_ref[0:1, cols] = sums[:, :GROUP]
        vec_ref[1:2, cols] = sums[:, 2 * GROUP :]

    @pl.when(step == last)
    def _():
        by_head = jnp.concatenate([tab[0, :4], tab[1, :4], tab[2, :4], jnp.zeros((4, 128), f32)], axis=0)
        vec_ref[12:13] = table_row(by_head)
        out_copy = pltpu.make_async_copy(dx, dx_ref, dy_sem)
        out_copy.start()
        if remote:
            vec_send[0] = vec_ref[...]
            vec_copy(0).start()
            tail = [(stage, name) for stage in range(6) for name in REDUCE_STEPS if REDUCE_STEPS[name][stage] > last]
            tail.remove((0, "g2"))
            order = sorted(tail, key=lambda t: t[0] - LATE[t[1]])
            for stage, name in order:
                items[name].step(stage)
                if name == "g2" and stage == 1:
                    vec_copy(0).wait_recv()
                    vec_send[1] = vec_send[0] + vec_recv[0]
                    for k in (1, 2, 3):
                        vec_copy(k).start()
                if name == "g2" and stage == 2:
                    for k in (1, 2, 3):
                        vec_copy(k).wait_recv()
                    vec_send[2] = vec_send[1] + vec_recv[1] + vec_recv[2] + vec_recv[3]
                    for k in (4, 5, 6):
                        vec_copy(k).start()
            for k in (4, 5, 6):
                vec_copy(k).wait_recv()
            vec_ref[...] = vec_send[2] + vec_recv[4] + vec_recv[5] + vec_recv[6]
            for k in range(7):
                vec_copy(k).wait_send()
            for entry in items.values():
                entry.drain()
            g_out[...] = g_sum[...]
            o_out[...] = o_sum[...]
            w1_out[...] = w1_sum[...]
            w2_out[...] = w2_sum[...]
        out_copy.wait()


LATE = {"2a": 0, "2b": 0, "1a": 3.8, "1b": 2.5, "o": 2.4, "g0": 1.6, "g1": 1.5, "g2": 0}


def backward_call(n, remote, *operands):
    sds = jax.ShapeDtypeStruct
    pair = pl.BlockSpec((1, R, 128), lambda g, s, j: (s, 0, 2 * g + j))
    block = (4, 2, 2, D // 16)
    in_specs = [VMEM_WHOLE, ANYWHERE, VMEM_WHOLE, VMEM_WHOLE, VMEM_WHOLE] + [
        pl.BlockSpec((1, 1, R, D), lambda g, s, j: (g, s, 0, 0)), pair, pair, pair,
        pl.BlockSpec((1, 2, R, LEN), lambda g, s, j: (s, 2 * g + j, 0, 0)),
        pair, ANYWHERE,
    ]
    small = pl.BlockSpec((16, D), lambda g, s, j: (0, 0))
    out_specs = [ANYWHERE, small]
    out_shape = [sds((n, R, D), f32), sds((16, D), f32)]
    scratch = [
        pltpu.VMEM((n, R, D), f32),
        pltpu.VMEM((n, R, D), bf16),
        pltpu.VMEM((2, R, LEN), f32),
        pltpu.VMEM((2, R, LEN), bf16),
        pltpu.VMEM((4, n * QP, LEN), bf16),
        pltpu.VMEM((n, LEN, QP), bf16),
        pltpu.VMEM((4, 3, 128, 128), f32),
        pltpu.VMEM((4, 16, 128), f32),
        pltpu.VMEM((3, 8, 128), f32),
        pltpu.VMEM((n, R, D), bf16),
        pltpu.SemaphoreType.DMA,
        pltpu.SemaphoreType.DMA,
    ]
    if remote:
        in_specs += [ANYWHERE] * 3
        out_specs += [VMEM_WHOLE] * 4
        shard = D // 16
        out_shape += [
            sds((3, 2, shard, D // 2), bf16), sds((2, shard, D // 2), bf16), sds((2, 2, shard, FF // 4), bf16),
            sds((2, 2, 96, D // 2), bf16),
        ]
        scratch += [
            pltpu.VMEM((3, *block, D), bf16),
            *(pltpu.VMEM(a.shape, bf16) for a in out_shape[2:]),
            pltpu.VMEM((3, 16, D), f32),
            pltpu.VMEM((7, 16, D), f32),
            pltpu.SemaphoreType.DMA((5,)),
            pltpu.SemaphoreType.DMA((8, 9)),
            pltpu.SemaphoreType.DMA((8, 9)),
            pltpu.SemaphoreType.DMA((7,)),
            pltpu.SemaphoreType.DMA((7,)),
        ]
        for rows, cols in ((96, D), (96, D), (shard, FF // 2), (shard, FF // 2), (shard, D)):
            scratch += Reduce.scratch(rows, cols, True)
        for _ in range(3):
            scratch += Reduce.scratch(shard, D, False)
        params = pltpu.CompilerParams(vmem_limit_bytes=VMEM_LIMIT, collective_id=2, has_side_effects=True)
    else:
        out_specs += [pl.BlockSpec(memory_space=pltpu.VMEM)]
        out_shape += [sds((3, D, D), bf16)]
        params = pltpu.CompilerParams(vmem_limit_bytes=VMEM_LIMIT)
    return pl.pallas_call(
        functools.partial(backward_kernel, remote, n),
        grid=(3, n, 2),
        in_specs=in_specs,
        out_specs=out_specs,
        out_shape=out_shape,
        scratch_shapes=scratch,
        compiler_params=params,
        name="attention_backward",
    )(*operands)


def output_kernel(dx_ref, vec, g_sum, o_sum, w1_sum, w2_sum, content, query, wq, wk, wv, wo, w1, w2, *vectors):
    content[0] = dx_ref[0, :LEN]
    query[0] = dx_ref[0, LEN : LEN + PRED]

    @pl.when(pl.program_id(0) == 1)
    def _():
        for m, out in enumerate((wq, wk, wv)):
            for g in range(3):
                for k in range(2):
                    at = m * 2 + k
                    out[:, g * GROUP + k * 128 : g * GROUP + (k + 1) * 128] = g_sum[
                        g, at // 3, :, (at % 3) * 128 : (at % 3 + 1) * 128
                    ].astype(f32)
        for k in range(2):
            wo[:, k * D // 2 : (k + 1) * D // 2] = o_sum[k].astype(f32)
            for i in range(2):
                at = i * (FF // 2) + k * (FF // 4)
                w1[:, at : at + FF // 4] = w1_sum[i, k].astype(f32)
                w2[i * 96 : (i + 1) * 96, k * D // 2 : (k + 1) * D // 2] = w2_sum[i, k].astype(f32)
        f = lax.axis_index("fsdp")
        lane = iota((D, 256), 0)
        i = iota((D, 256), 1)

        def take(rows, size, at):
            hot = jnp.where((i < size) & (lane == i + at), 1.0, 0.0)
            return jnp.dot(rows, hot, preferred_element_type=f32, precision=lax.Precision.HIGHEST)

        plain = take(vec[0:8], D // 16, f * (D // 16))
        wide = jnp.sum(jnp.where(iota((16, D), 0) == 8 + f // 4, vec[...], 0.0), axis=0, keepdims=True)
        wide = take(jnp.broadcast_to(wide, (8, D)), 192, (f % 4) * 192)
        table = take(jnp.broadcast_to(vec[12:13], (8, D)), 24, f * 24)
        rows = [plain[r : r + 1] for r in range(8)] + [wide[:1], table[:1]]
        for out, row in zip(vectors, rows):
            out[...] = row[0, : out.shape[0]]


def output_call(n, dx, vec, g_sum, o_sum, w1_sum, w2_sum, sizes):
    sds = jax.ShapeDtypeStruct

    def rows(count):
        return pl.BlockSpec((1, count, D), lambda s: (s, 0, 0))

    shard = D // 16
    return pl.pallas_call(
        output_kernel,
        grid=(n,),
        in_specs=[rows(R)] + [VMEM_WHOLE] * 5,
        out_specs=[rows(LEN), rows(PRED)] + [VMEM_WHOLE] * (6 + len(sizes)),
        out_shape=[sds((n, LEN, D), f32), sds((n, PRED, D), f32)]
        + [sds((shard, D), f32)] * 4
        + [sds((shard, FF), f32), sds((FF // 16, D), f32)]
        + [sds((size,), f32) for size in sizes],
        compiler_params=pltpu.CompilerParams(vmem_limit_bytes=VMEM_LIMIT),
        name="outputs",
    )(dx, vec, g_sum, o_sum, w1_sum, w2_sum)
def pieces(own_vectors, places):
    return sum(jnp.pad(v[None], ((at, 15 - at), (0, 256 - v.shape[0]))) for at, v in zip(places, own_vectors))


ROWS = (0, 1, 2, 3, 4, 5, 6, 7, 8, 12)


def per_device(
    content_in, query_in, permutation,
    query_weight, key_weight, value_weight, output_weight, inner_weight, outer_weight,
    query_bias, value_bias, output_bias, first_gain, first_shift, inner_bias, outer_bias,
    second_gain, second_shift, bias_table,
    content_cotangent, query_cotangent,
):
    n = content_in.shape[0]
    n_f = lax.axis_size("fsdp")
    remote = n_f == 16 and lax.axis_size("dp") == 2 and n == 3
    vectors = (
        query_bias, value_bias, output_bias, first_gain, first_shift, outer_bias, second_gain, second_shift,
        inner_bias, bias_table,
    )
    sizes = [a.shape[0] for a in vectors]
    if remote:
        qkv, o, ol, r, p, act, slope, unit1, inv1, low1, vec, wqkv, wo, w1, w2 = forward_call(
            n, True, permutation, content_in, query_in, pieces(vectors, ROWS),
            query_weight, key_weight, value_weight, output_weight, inner_weight, outer_weight,
        )
        wqkv = wqkv.reshape(3, D, D)
        wo, w1, w2 = wo.reshape(D, D), w1.reshape(D, FF), w2.reshape(FF, D)
    else:
        packed = lax.all_gather(jnp.concatenate(vectors), "fsdp", axis=0)
        rows = []
        at = 0
        for size in sizes:
            whole = packed[:, at : at + size].reshape(-1).astype(f32)
            rows.append(jnp.pad(whole, (0, -whole.shape[0] % D)).reshape(-1, D))
            at += size
        vec = jnp.concatenate(rows + [jnp.zeros((3, D), f32)], axis=0)
        whole = lax.all_gather(
            jnp.concatenate([query_weight, key_weight, value_weight, output_weight, inner_weight], axis=1),
            "fsdp", axis=0, tiled=True,
        )
        wqkv = jnp.stack(
            [
                jnp.concatenate([whole[:, m * D + g * GROUP : m * D + (g + 1) * GROUP] for m in range(3)], axis=1)
                for g in range(3)
            ]
        )
        wo, w1 = whole[:, 3 * D : 4 * D], whole[:, 4 * D :]
        w2 = lax.all_gather(outer_weight, "fsdp", axis=0, tiled=True)
        qkv, o, ol, r, p, act, slope, unit1, inv1, low1 = forward_call(
            n, False, permutation, content_in, query_in, vec, wqkv, wo, w1
        )

    content_out, query_out, d2, dh, d1, do, dy, sums = middle_call(
        n, unit1, inv1, act, slope, content_cotangent, query_cotangent, vec, wo, w1, w2
    )
    w1_grad, w2_grad, wo_grad = weight_call(n, act, dh, d2, low1, o, d1)

    if remote:
        block = (4, 2, 2)
        dx, sums, g_sum, o_sum, w1_sum, w2_sum = backward_call(
            n, True, permutation, content_in, query_in, wqkv, sums, qkv, o, ol, r, p, do, dy,
            wo_grad.reshape(*block, D // 16, D), w1_grad.reshape(*block, D // 16, FF),
            w2_grad.reshape(*block, FF // 16, D),
        )
        content_grad, query_grad, wq_s, wk_s, wv_s, wo_s, w1_s, w2_s, *shares = output_call(
            n, dx, sums, g_sum, o_sum, w1_sum, w2_sum, sizes
        )
    else:
        dx, sums, wqkv_grad = backward_call(
            n, False, permutation, content_in, query_in, wqkv, sums, qkv, o, ol, r, p, do, dy
        )
        content_grad, query_grad = dx[:, :LEN], dx[:, LEN : LEN + PRED]

        def scatter(a):
            return lax.psum_scatter(a, "fsdp", scatter_dimension=0, tiled=True)

        flat = jnp.concatenate(
            [wqkv_grad[g, :, m * GROUP : (m + 1) * GROUP] for m in range(3) for g in range(3)] + [wo_grad, w1_grad],
            axis=1,
        )
        whole_rows = [sums[i] for i in range(8)] + [sums[8:12].reshape(-1), sums[12, : BUCKETS * HEADS]]
        packed = jnp.concatenate([v.reshape(n_f, -1) for v in whole_rows], axis=1)
        totals = lax.psum((scatter(flat), scatter(w2_grad), scatter(packed).astype(bf16)), "dp")
        flat, w2_s, packed = (a.astype(f32) for a in totals)
        wq_s, wk_s, wv_s, wo_s = (flat[:, m * D : (m + 1) * D] for m in range(4))
        w1_s = flat[:, 4 * D :]
        shares = []
        at = 0
        for size in sizes:
            shares.append(packed[0, at : at + size])
            at += size
    bq_s, bv_s, bo_s, g1_s, s1_s, b2_s, g2_s, s2_s, b1_s, tab_s = shares
    return (
        content_out, query_out, content_grad, query_grad,
        wq_s, wk_s, wv_s, wo_s, w1_s, w2_s,
        bq_s, bv_s, bo_s, g1_s, s1_s, b1_s, b2_s, g2_s, s2_s, tab_s,
    )


def solution(mesh):
    rows3 = P(("dp", "fsdp"), None, None)
    matrix = P("fsdp", None)
    vector = P("fsdp")
    return jax.shard_map(
        per_device,
        mesh=mesh,
        in_specs=(rows3, rows3, P(("dp", "fsdp"), None)) + (matrix,) * 6 + (vector,) * 10 + (rows3, rows3),
        out_specs=(rows3,) * 4 + (matrix,) * 6 + (vector,) * 10,
        check_vma=False,
    )
```
